128 devices in a mesh: gx: 16 (over y, z), gy: 8 (over x, core).
Axes of the slice: x: 4, y: 4, z: 4, core: 2. Of those that a mesh axis runs over, the one named last changes fastest.
Arguments:
- fluid_vel: float32 [3, 128, 128, 256], P(None, 'gx', 'gy'), may hold values from -6 to 6
- part_pos: float32 [32768, 3, 128], P(('gx', 'gy')), may hold values from 0 to 1
- part_vel: float32 [32768, 3, 128], P(('gx', 'gy')), may hold values from -6 to 6
- brick_owner: int32 [32768, 1], P(('gx', 'gy')), may hold values from 0 to 127; in each aligned block of 256 rows (0 to 255, 256 to 511, ...) at most 4 rows name the same one
- brick_local: int32 [32768], P(('gx', 'gy')), may hold values from 0 to 255
- cell_in_brick: int32 [32768, 128], P(('gx', 'gy')), may hold values from 0 to 127
- pair_self: int32 [2, 65536], P(None, ('gx', 'gy')), may hold values from 0 to 255
- pair_other: int32 [2, 65536], P(None, ('gx', 'gy')), may hold values from 0 to 287
- halo_list: int32 [4096], P(('gx', 'gy')), may hold values from 0 to 255
Outputs:
- fluid_new: float32 [3, 128, 128, 256], P(None, 'gx', 'gy')
- pos_out: float32 [32768, 3, 128], P(('gx', 'gy'))
- vel_out: float32 [32768, 3, 128], P(('gx', 'gy'))
The draws below stay inside these ranges and needn't reach their ends.
Inputs may be any that keep to these rules, and one draw needn't show every extreme that they name: `brick_owner`: within the 256 blocks of one device (aligned blocks of rows), no tile is named more than 4 times, a bound that some block reaches.
All inputs are finite; a program needn't handle non-finite values.
Results may differ from the reference program's by a relative error of at most 0.0001.
Values sent between devices are 32-bit elements; how exact they have to be, the bound alone decides.
No kernel may reach another device: no remote copies, remote signals or barrier semaphores. Data moves between devices by JAX's collectives and lax.ppermute only.
A program may use at most 64 MiB of HBM per device.

```python
import math
import jax
import jax.numpy as jnp
import numpy as np
from jax import lax

CX = 8
CY = 16
NZ = 256
BLK_DEV = 256
PAIRS_DEV = 512
HB = 16
SUBSTEPS = 2
PER_BLOCK = 128
BRICK_X = 2
BRICK_Y = 4
BRICK_Z = 16
NX = 128
NY = 128
TILES = 128
BRICKS_DEV = 256
BLOCKS = 32768
PAIRS = 65536
HALO_ROWS = 4096
CAP = 4
N_GX = 16
N_GY = 8


def set_ends(values, key, smallest, high):
    spot = [jax.random.randint(jax.random.fold_in(key, axis), (), 0, length) for axis, length in enumerate(values.shape)]
    longest = values.shape.index(max(values.shape))
    next_to = spot[:longest] + [(spot[longest] + 1) % values.shape[longest]] + spot[longest + 1:]
    return values.at[tuple(spot)].set(smallest).at[tuple(next_to)].set(high)


def levels(stream_key, shape, shards, low, top_value):
    loudness, own = 1.0, jax.random.fold_in(stream_key, 6)
    for dim, shards_of in shards:
        draws = jnp.exp(jax.random.uniform(jax.random.fold_in(own, dim), (shards_of,), jnp.float32, low / len(shards), top_value / len(shards)))
        loudness = loudness * jnp.repeat(draws, shape[dim] // shards_of).reshape([-1 if axis == dim else 1 for axis in range(len(shape))])
    return loudness


def deal_out(rng, own, number, rows, count, top, most, skew):
    sequence = jax.random.permutation(rng, count)
    packed, common = portions_of(count, rows * top, most, skew, True), portions_of(count, rows * top, most, skew, False)
    places = jnp.arange(count)

    def named(tallies, offset_by):
        used = int((tallies > 0).sum())
        fixed = max(1, used // 4)
        passed = fixed + (places - fixed + offset_by * (used - fixed)) % max(1, count - fixed)
        return jnp.zeros((count,), jnp.int32).at[sequence[jnp.where(places < fixed, places, passed)]].set(jnp.asarray(tallies, jnp.int32))

    tallies = jnp.where(number % 4 == 0, named(packed, number // 4), named(common, number - number // 4 - 1))
    mixed = jax.random.permutation(jax.random.fold_in(own, 3), count)
    source_of, sink = mixed[0:count // 2 * 2:2], mixed[1:count // 2 * 2:2]
    room = jnp.minimum(tallies[source_of] - 1, most - tallies[sink]) // 2
    room = jnp.where((source_of == sequence[0]) | (sink == sequence[0]) | (tallies[sink] == 0), 0, jnp.maximum(room, 0))
    passed = jax.random.randint(jax.random.fold_in(own, 4), (count // 2,), 0, 1 << 20) % (room + 1)
    tallies = tallies.at[source_of].add(-passed).at[sink].add(passed)
    items = jnp.searchsorted(jnp.cumsum(tallies), jnp.arange(rows * top), side="right").astype(jnp.int32)
    table = items.reshape(top, rows).T
    table = table[jax.random.permutation(jax.random.fold_in(own, 1), rows)]
    offset_by = jax.random.randint(jax.random.fold_in(own, 2), (rows, 1), 0, top)
    return jnp.take_along_axis(table, (jnp.arange(top)[None, :] + offset_by) % top, axis=1)


def portions_of(amount, total, limit, lean, full):
    weights = [(1 << 20) // math.isqrt(standing ** lean) + 1 for standing in range(1, amount + 1)]
    largest = limit if full else min(limit, max(-(-total // amount), total * weights[0] // sum(weights)))
    least = 1 if total - largest >= amount - 1 else 0
    holding, spare = [largest] + [least] * (amount - 1), total - largest - least * (amount - 1)
    while spare > 0:
        candidates = [i for i in range(1, amount) if holding[i] < largest] or [i for i in range(1, amount) if holding[i] < limit]
        pool, remaining = sum([weights[i] for i in candidates]), spare
        for i in candidates:
            addition = min(limit - holding[i], max(1, remaining * weights[i] // pool), spare)
            holding[i] = holding[i] + addition
            spare = spare - addition
    return np.array(holding)


def gaussian(rng, shape, scale, reach, cuts=(), held_as=jnp.bfloat16):
    loudness = levels(rng, shape, cuts, -0.22, 0.18) if cuts else 1.0
    entries = jax.random.normal(rng, shape, jnp.float32) * scale * loudness
    return jnp.minimum(jnp.maximum(entries, -reach), reach).astype(held_as)


def setup_inputs(seed: int = 0) -> dict:
    keys = jax.random.split(jax.random.key(seed), 10)
    fluid_vel = gaussian(keys[0], (3, NX, NY, NZ), 1.0, 6.0, ((1, 16), (2, 8)), jnp.float32)
    part_pos = jnp.clip(1.0 * jax.random.uniform(keys[1], (BLOCKS, 3, PER_BLOCK), jnp.float32) ** levels(keys[1], (BLOCKS, 3, PER_BLOCK), ((0, 128),), -0.2, 0.2), 0.0, 1.0)
    part_vel = gaussian(keys[2], (BLOCKS, 3, PER_BLOCK), 1.0, 6.0, ((0, 128),), jnp.float32)
    brick_owner_keys = jax.random.split(jax.random.fold_in(keys[3], 1), BLOCKS // BLK_DEV)
    brick_owner_turns = jax.random.permutation(jax.random.fold_in(keys[3], 3), BLOCKS // BLK_DEV)
    brick_owner = jax.vmap(lambda own, number: deal_out(jax.random.fold_in(keys[3], 2), own, number, BLK_DEV, TILES, 1, CAP, 2))(brick_owner_keys, brick_owner_turns).reshape((BLOCKS, 1))
    brick_local = set_ends(jax.random.randint(keys[4], (BLOCKS,), 0, BRICKS_DEV), jax.random.fold_in(keys[4], 1), 0, BRICKS_DEV - 1).astype(jnp.int32)
    cell_in_brick = set_ends(jax.random.randint(keys[5], (BLOCKS, PER_BLOCK), 0, PER_BLOCK), jax.random.fold_in(keys[5], 1), 0, PER_BLOCK - 1).astype(jnp.int32)
    pair_self = set_ends(jax.random.randint(keys[6], (SUBSTEPS, PAIRS), 0, BLK_DEV), jax.random.fold_in(keys[6], 1), 0, BLK_DEV - 1).astype(jnp.int32)
    pair_other = set_ends(jax.random.randint(keys[7], (SUBSTEPS, PAIRS), 0, BLK_DEV + 2 * HB), jax.random.fold_in(keys[7], 1), 0, (BLK_DEV + 2 * HB) - 1).astype(jnp.int32)
    halo_list = set_ends(jax.random.randint(keys[8], (HALO_ROWS,), 0, BLK_DEV), jax.random.fold_in(keys[8], 1), 0, BLK_DEV - 1).astype(jnp.int32)
    return {"fluid_vel": fluid_vel, "part_pos": part_pos, "part_vel": part_vel, "brick_owner": brick_owner, "brick_local": brick_local, "cell_in_brick": cell_in_brick, "pair_self": pair_self, "pair_other": pair_other, "halo_list": halo_list}


def pair_force(xa, xb):
    dist2 = 0.0025 + (xa[:, 0, :, None] - xb[:, 0, None, :]) ** 2
    dist2 = dist2 + (xa[:, 1, :, None] - xb[:, 1, None, :]) ** 2
    dist2 = dist2 + (xa[:, 2, :, None] - xb[:, 2, None, :]) ** 2
    dist = jnp.sqrt(dist2)
    coef = 10.0 * jnp.maximum(0.25 - dist, 0.0) / dist
    total = lax.optimization_barrier(jnp.sum(coef, axis=2))
    pulled = jnp.einsum('gij,gcj->gci', coef, xb, precision=lax.Precision.HIGHEST)
    return xa * total[:, None, :] - pulled

def to_grid(bricks):
    comps = bricks.shape[2]
    parts = bricks.reshape(N_GX, N_GY, CX // BRICK_X, CY // BRICK_Y, NZ // BRICK_Z, comps, BRICK_X, BRICK_Y, BRICK_Z)
    parts = jnp.transpose(parts, (5, 0, 2, 6, 1, 3, 7, 4, 8))
    return parts.reshape(comps, NX, NY, NZ)

def to_bricks(grid):
    comps = grid.shape[0]
    parts = grid.reshape(comps, N_GX, CX // BRICK_X, BRICK_X, N_GY, CY // BRICK_Y, BRICK_Y, NZ // BRICK_Z, BRICK_Z)
    parts = jnp.transpose(parts, (1, 4, 2, 5, 7, 0, 3, 6, 8))
    return parts.reshape(N_GX * N_GY, BRICKS_DEV, comps, PER_BLOCK)

def reference(fluid_vel, part_pos, part_vel, brick_owner, brick_local, cell_in_brick, pair_self, pair_other, halo_list):
    tiles = N_GX * N_GY
    target = brick_owner[:, 0]
    flat = ((target * BRICKS_DEV + brick_local)[:, None] * PER_BLOCK + cell_in_brick).reshape(-1)
    loads = jnp.concatenate([jnp.ones((BLOCKS, 1, PER_BLOCK), jnp.float32), part_vel], axis=1)
    loads = jnp.transpose(loads, (1, 0, 2)).reshape(4, -1)
    spread = jax.vmap(lambda row: jax.ops.segment_sum(row, flat, num_segments=tiles * BRICKS_DEV * PER_BLOCK))(loads)
    spread = jnp.transpose(spread.reshape(4, tiles, BRICKS_DEV, PER_BLOCK), (1, 2, 0, 3))
    deposit = to_grid(spread)
    count = deposit[0]
    momentum = deposit[1:]
    solid = 0.5 * count
    voids = 1.0 - 0.6 * solid / (1.0 + solid)
    beta = (1.0 - voids) / (voids * voids)
    padded = jnp.pad(fluid_vel, ((0, 0), (1, 1), (1, 1), (1, 1)))
    beside = padded[:, 2:, 1:-1, 1:-1] + padded[:, :-2, 1:-1, 1:-1]
    beside = beside + padded[:, 1:-1, 2:, 1:-1] + padded[:, 1:-1, :-2, 1:-1]
    beside = beside + padded[:, 1:-1, 1:-1, 2:] + padded[:, 1:-1, 1:-1, :-2]
    lap = beside - 6.0 * fluid_vel
    fluid_new = fluid_vel + 0.1 * lap + 0.15 * beta[None] * (momentum - count[None] * fluid_vel)
    table = to_bricks(jnp.concatenate([fluid_new, beta[None]], axis=0))
    mine = table[target, brick_local]
    local_fluid = jnp.take_along_axis(mine, jnp.broadcast_to(cell_in_brick[:, None, :], mine.shape), axis=2)
    flow = local_fluid[:, :3, :]
    drift = 2.0 * local_fluid[:, 3:4, :]
    down = jnp.array([0.0, 0.0, -1.0], jnp.float32)[None, :, None]
    lists = halo_list.reshape(N_GX, N_GY, 2 * HB)
    position = part_pos
    velocity = part_vel
    for step in range(SUBSTEPS):
        grouped = position.reshape(N_GX, N_GY, BLK_DEV, 3, PER_BLOCK)
        index = jnp.broadcast_to(lists[:, :, :, None, None], (N_GX, N_GY, 2 * HB, 3, PER_BLOCK))
        sent = jnp.take_along_axis(grouped, index, axis=2)
        lower = jnp.roll(sent[:, :, HB:], 1, axis=0)
        upper = jnp.roll(sent[:, :, :HB], -1, axis=0)
        extended = jnp.concatenate([grouped, lower, upper], axis=2).reshape(tiles, BLK_DEV + 2 * HB, 3, PER_BLOCK)
        selfs = pair_self[step].reshape(tiles, PAIRS_DEV)
        others = pair_other[step].reshape(tiles, PAIRS_DEV)

        def device_push(item):
            whole, first, second = item
            force = pair_force(whole[first], whole[second])
            return jax.ops.segment_sum(force, first, num_segments=BLK_DEV)
        push = lax.map(device_push, (extended, selfs, others)).reshape(BLOCKS, 3, PER_BLOCK)
        velocity = velocity + 0.1 * (push + drift * (flow - velocity) + down)
        position = position + 0.1 * velocity
    return (fluid_new, position, velocity)
```

```python
import functools

import jax
import jax.numpy as jnp
from jax import lax
from jax.experimental import pallas as pl
from jax.experimental.pallas import tpu as pltpu
from jax.sharding import PartitionSpec as P

F32 = jnp.float32
BF16 = jnp.bfloat16
CAP = 4
EPS2 = 0.0025
VMEM = pl.BlockSpec(memory_space=pltpu.VMEM)
SMEM = pl.BlockSpec(memory_space=pltpu.SMEM)
PARAMS = dict(vmem_limit_bytes=48 * 1024 * 1024)


def split2(x):
    hi = x.astype(BF16)
    return hi, (x - hi.astype(F32)).astype(BF16)


def onehot_cells(row):
    cells = lax.broadcasted_iota(jnp.int32, (128, 128), 0)
    return (cells == jnp.broadcast_to(row, (128, 128))).astype(F32).astype(BF16)


def dot(a, b, dims=((1,), (0,))):
    return lax.dot_general(a, b, (dims, ((), ())), preferred_element_type=F32)


def pack_rows(halo, pos, out, first, half):
    for j in range(16):
        q = halo[half * 16 + j]
        for m in range(3):
            out[pl.ds(first + m * 16 + j, 1), :] = pos[m, pl.ds(q, 1), :]


def faces_kernel(halo, fv, pos, down_out, up_out, left_out, right_out):
    sx = fv.shape[1]
    for out, x, half in ((down_out, 0, 0), (up_out, sx - 1, 1)):
        for m in range(3):
            for h in range(2):
                out[(m * 2 + h) * 16 : (m * 2 + h + 1) * 16, :] = fv[m, x, :, h * 128 : (h + 1) * 128]
        pack_rows(halo, pos, out, 96, half)
    for out, y in ((left_out, 0), (right_out, fv.shape[2] - 1)):
        for m in range(3):
            out[m, :, :] = fv[m, :, y, :]


def deposit_kernel(owner, local, cell, vel, out, slot_out, taken):
    blocks = cell.shape[0]
    lanes = lax.broadcasted_iota(jnp.int32, (4, 128), 1)
    rows4 = lax.broadcasted_iota(jnp.int32, (4, 128), 0)
    mark = (lanes == 127) & (rows4 == 0)
    out[...] = jnp.broadcast_to(jnp.where(mark, -1.0, 0.0).astype(F32)[None], out.shape)

    def clear(t, c):
        taken[t] = 0
        return c

    lax.fori_loop(0, taken.shape[0], clear, 0, unroll=8)
    r8 = lax.broadcasted_iota(jnp.int32, (8, 128), 0)

    def group(g, c):
        base = pl.multiple_of(g * 8, 8)
        cells8 = cell[pl.ds(base, 8), :]
        v = [vel[m, pl.ds(base, 8), :] for m in range(3)]
        for k in range(8):
            q = base + k
            hot = onehot_cells(cells8[k : k + 1, :])
            rows = [jnp.broadcast_to(v[m][k : k + 1, :], (8, 128)) for m in range(3)]
            load = jnp.where(r8 == 1, rows[0], jnp.where(r8 == 2, rows[1], rows[2]))
            load = jnp.where(r8 == 0, 1.0, jnp.where(r8 < 4, load, 0.0))
            hi = load.astype(BF16).astype(F32)
            lhs = jnp.concatenate([hi, load - hi], axis=0).astype(BF16)
            both = dot(lhs, hot, ((1,), (1,)))
            both = both[0:8] + both[8:16]
            tile = owner[q]
            rank = taken[tile]
            taken[tile] = rank + 1
            slot = tile * CAP + rank
            slot_out[q] = slot
            ident = jnp.full((4, 128), local[q], jnp.int32).astype(F32)
            out[slot] = jnp.where(mark, ident, both[0:4])
        return c

    lax.fori_loop(0, blocks // 8, group, 0)


def swap_groups(v):
    row = lax.broadcasted_iota(jnp.int32, v.shape, 1)
    grp = lax.broadcasted_iota(jnp.int32, v.shape, 2) // 16
    for s in range(3):
        step = 1 << s
        ra, gb = (row >> s) & 1, (grp >> s) & 1
        up = pltpu.roll(pltpu.roll(v, 8 - step, 1), 16 * step, 2)
        dn = pltpu.roll(pltpu.roll(v, step, 1), 128 - 16 * step, 2)
        v = jnp.where(ra == gb, v, jnp.where(ra < gb, up, dn))
    return v


def fluid_kernel(xlo_on, recv, fv, from_low, from_high, from_left, from_right, fluid, answer, grid):
    sx, sy, sz = fv.shape[1:]
    slots = recv.shape[0] // 4
    bricks = sx // 2 * (sy // 4) * (sz // 16)
    count = recv[pl.ds(0, slots, stride=4), :]
    lane = lax.broadcasted_iota(jnp.int32, (slots, 128), 1)
    ident = count[:, 127:128]
    ident_row = count.T[127:128, :]
    wide = lax.broadcasted_iota(jnp.int32, (slots, bricks), 1).astype(F32)
    by_slot = (wide == jnp.broadcast_to(ident, (slots, bricks))).astype(F32).astype(BF16)
    tall = lax.broadcasted_iota(jnp.int32, (bricks, slots), 0).astype(F32)
    by_brick = (tall == jnp.broadcast_to(ident_row, (bricks, slots))).astype(F32).astype(BF16)
    parts = [jnp.where(lane == 127, 1.0, count).astype(BF16)]
    for m in range(3):
        parts += list(split2(recv[pl.ds(m + 1, slots, stride=4), :]))
    summed = dot(by_brick, jnp.concatenate(parts, axis=1))
    cnt = summed[:, 0:128]
    momentum = [summed[:, (1 + 2 * m) * 128 : (2 + 2 * m) * 128] + summed[:, (2 + 2 * m) * 128 : (3 + 2 * m) * 128] for m in range(3)]
    last = lax.broadcasted_iota(jnp.int32, (bricks, 128), 1) == 127
    others = jnp.sum(jnp.where(last, 0.0, cnt), axis=1, keepdims=True)
    cnt = jnp.where(last, 128.0 * cnt - others, cnt)
    solid = 0.5 * cnt
    voids = 1.0 - 0.6 * solid / (1.0 + solid)
    beta = (1.0 - voids) / (voids * voids)
    scale = 0.15 * beta
    sources = [scale * momentum[m] for m in range(3)] + [scale * cnt]
    for c in range(4):
        moved = swap_groups(sources[c].reshape(bricks // 8, 8, 128))
        for bx in range(sx // 2):
            for by in range(sy // 4):
                for h in range(2):
                    v = moved[(bx * 4 + by) * 2 + h]
                    for x in range(2):
                        grid[c, bx * 2 + x, by * 4 : by * 4 + 4, h * 128 : h * 128 + 128] = v[x * 4 : x * 4 + 4, :]
    yrow = lax.broadcasted_iota(jnp.int32, (sy, sz), 0)
    zlane = lax.broadcasted_iota(jnp.int32, (sy, sz), 1)
    low_on = (xlo_on[0]).astype(F32)
    high_on = (xlo_on[1]).astype(F32)
    for m in range(3):
        low = jnp.concatenate([from_low[(m * 2 + h) * 16 : (m * 2 + h + 1) * 16, :] for h in range(2)], axis=1) * low_on
        high = jnp.concatenate([from_high[(m * 2 + h) * 16 : (m * 2 + h + 1) * 16, :] for h in range(2)], axis=1) * high_on
        for x in range(sx):
            f = fv[m, x]
            beside = (fv[m, x + 1] if x < sx - 1 else high) + (fv[m, x - 1] if x > 0 else low)
            right = jnp.broadcast_to(from_right[m, x : x + 1, :], (sy, sz))
            left = jnp.broadcast_to(from_left[m, x : x + 1, :], (sy, sz))
            beside = beside + jnp.where(yrow == sy - 1, right, pltpu.roll(f, sy - 1, 0))
            beside = beside + jnp.where(yrow == 0, left, pltpu.roll(f, 1, 0))
            beside = beside + jnp.where(zlane == sz - 1, 0.0, pltpu.roll(f, sz - 1, 1))
            beside = beside + jnp.where(zlane == 0, 0.0, pltpu.roll(f, 1, 1))
            fluid[m, x] = f + 0.1 * (beside - 6.0 * f) + (grid[m, x] - grid[3, x] * f)
    table = []
    for m in range(3):
        tiles = []
        for bx in range(sx // 2):
            for by in range(sy // 4):
                for h in range(2):
                    tiles.append(
                        jnp.concatenate(
                            [fluid[m, bx * 2 + x, by * 4 : by * 4 + 4, h * 128 : h * 128 + 128] for x in range(2)],
                            axis=0,
                        )
                    )
        v = swap_groups(jnp.stack(tiles, axis=0)).reshape(bricks, 128)
        table += list(split2(v))
    table += list(split2(beta))
    found = dot(by_slot, jnp.concatenate(table, axis=1))
    for c in range(4):
        answer[pl.ds(c, slots, stride=4), :] = (
            found[:, 2 * c * 128 : (2 * c + 1) * 128] + found[:, (2 * c + 1) * 128 : (2 * c + 2) * 128]
        )


def feature_rows(x):
    hi, lo, both = [], [], []
    for m in range(3):
        u = x[m] - 0.5
        h = u.astype(BF16).astype(F32)
        l = (u - h).astype(BF16).astype(F32)
        hi.append(h)
        lo.append(l)
        both.append(h + l)
    return hi, lo, both, both[0] * both[0] + both[1] * both[1] + both[2] * both[2]


def split3(n):
    a = n.astype(BF16).astype(F32)
    b = (n - a).astype(BF16).astype(F32)
    return a, b, n - a - b


def push_loop(step, first, second, pos, low, high, push, feat_b, feat_a, base_a):
    blocks = pos.shape[1]
    one = jnp.ones((8, 128), F32)
    zero = jnp.zeros((8, 128), F32)

    def put(ref, rows, stride, q0, feats):
        for k, v in enumerate(feats):
            ref[pl.ds(q0 * stride + k, 8, stride=stride), :] = v

    def own(g, c):
        q0 = pl.multiple_of(g * 8, 8)
        hi, lo, both, norm = feature_rows([pos[m, pl.ds(q0, 8), :] for m in range(3)])
        n = split3(norm)
        put(feat_b, 16, 16, q0, hi + [one, n[0], n[1], n[2], one] + lo + [zero, one, zero, zero, zero])
        n = split3(norm + EPS2)
        h2, l2 = [-2.0 * v for v in hi], [-2.0 * v for v in lo]
        put(
            feat_a, 32, 32, q0,
            h2 + [n[0], one, one, one, n[1]] + h2 + [zero, n[2], zero, zero, zero]
            + l2 + [zero] * 5 + l2 + [zero] * 5,
        )
        put(base_a, 8, 8, q0, both + [zero] * 5)
        return c

    lax.fori_loop(0, blocks // 8, own, 0)
    for i, (ref, at) in enumerate((low, high)):
        for g in range(2):
            hi, lo, _, norm = feature_rows([ref[at + m * 16 + g * 8 : at + m * 16 + g * 8 + 8, :] for m in range(3)])
            n = split3(norm)
            put(feat_b, 16, 16, blocks + i * 16 + g * 8, hi + [one, n[0], n[1], n[2], one] + lo + [zero, one, zero, zero, zero])
    push[...] = jnp.zeros(push.shape, F32)

    def one_pair(p):
        a = first[step, p]
        b = second[step, p]
        fb = feat_b[pl.ds(pl.multiple_of(b * 16, 16), 16), :]
        ga = feat_a[pl.ds(pl.multiple_of(a * 32, 32), 32), :].astype(BF16)
        fbt = jnp.concatenate([fb, fb], axis=0).T.astype(BF16)
        r2 = dot(fbt, ga)
        w = jnp.maximum(lax.rsqrt(jnp.maximum(r2, EPS2)) - 4.0, 0.0)
        hi, lo = split2(w)
        lhs = fb.astype(BF16)
        res = dot(lhs, hi) + dot(lhs, lo)
        res = res[0:8] + res[8:16]
        ua = base_a[pl.ds(pl.multiple_of(a * 8, 8), 8), :]
        return a, ua * jnp.broadcast_to(res[3:4], (8, 128)) - res

    unroll = 4

    def pairs(g, c):
        done = [one_pair(g * unroll + k) for k in range(unroll)]
        for a, f in done:
            rows = pl.ds(pl.multiple_of(a * 8, 8), 8)
            push[rows, :] = push[rows, :] + f
        return c

    lax.fori_loop(0, first.shape[1] // unroll, pairs, 0)


def push_kernel(first, second, pos, low, high, push, feat_b, feat_a, base_a):
    push_loop(0, first, second, pos, (low, 96), (high, 96), push, feat_b, feat_a, base_a)


def advance(pos, vel, push, flow, pos_out, vel_out):
    blocks = pos.shape[1]
    drift = 2.0 * flow[pl.ds(3, blocks, stride=8), :]
    for m in range(3):
        v = vel[m]
        force = 2.5 * push[pl.ds(m, blocks, stride=8), :] + drift * (flow[pl.ds(m, blocks, stride=8), :] - v)
        if m == 2:
            force = force - 1.0
        v = v + 0.1 * force
        vel_out[m] = v
        pos_out[m] = pos[m] + 0.1 * v


def pick_kernel(slot, halo, back, cell, pos, vel, push, flow, pos_out, vel_out, down_out, up_out):
    def group(g, c):
        base = pl.multiple_of(g * 8, 8)
        cells8 = cell[pl.ds(base, 8), :]
        for k in range(8):
            q = base + k
            hot = onehot_cells(cells8[k : k + 1, :])
            v = back[slot[q]]
            v = jnp.concatenate([v, v], axis=0)
            hi = v.astype(BF16).astype(F32)
            lhs = jnp.concatenate([hi, v - hi], axis=0).astype(BF16)
            both = dot(lhs, hot)
            flow[pl.ds(pl.multiple_of(q * 8, 8), 8), :] = both[0:8] + both[8:16]
        return c

    lax.fori_loop(0, cell.shape[0] // 8, group, 0)
    advance(pos, vel, push, flow, pos_out, vel_out)
    pack_rows(halo, pos_out, down_out, 0, 0)
    pack_rows(halo, pos_out, up_out, 0, 1)


def last_kernel(first, second, pos, vel, low, high, flow, pos_out, vel_out, push, feat_b, feat_a, base_a):
    push_loop(1, first, second, pos, (low, 0), (high, 0), push, feat_b, feat_a, base_a)
    advance(pos, vel, push, flow, pos_out, vel_out)


def call(kernel, in_specs, out_shape, out_specs, scratch=(), cost=None):
    return pl.pallas_call(
        kernel,
        in_specs=in_specs,
        out_shape=out_shape,
        out_specs=out_specs,
        scratch_shapes=list(scratch),
        compiler_params=pltpu.CompilerParams(**PARAMS),
        cost_estimate=cost,
    )


def shape(*dims, dtype=F32):
    return jax.ShapeDtypeStruct(dims, dtype)


def per_device(
    fluid_vel,
    part_pos,
    part_vel,
    brick_owner,
    brick_local,
    cell_in_brick,
    pair_self,
    pair_other,
    halo_list,
):
    nx, ny = lax.axis_size("gx"), lax.axis_size("gy")
    tiles = nx * ny
    blocks = part_pos.shape[0]
    slots = tiles * CAP
    sx, sy, sz = fluid_vel.shape[1:]
    pos = jnp.transpose(part_pos, (1, 0, 2))
    vel = jnp.transpose(part_vel, (1, 0, 2))

    down, up, left, right = call(
        faces_kernel,
        [SMEM, VMEM, VMEM],
        [shape(144, 128), shape(144, 128), shape(3, sx, sz), shape(3, sx, sz)],
        [VMEM] * 4,
    )(halo_list, fluid_vel, pos)
    fwd = [(i, (i + 1) % nx) for i in range(nx)]
    bwd = [((i + 1) % nx, i) for i in range(nx)]
    from_low = lax.ppermute(up, "gx", fwd)
    from_high = lax.ppermute(down, "gx", bwd)
    from_left = lax.ppermute(right, "gy", [(i, i + 1) for i in range(ny - 1)])
    from_right = lax.ppermute(left, "gy", [(i + 1, i) for i in range(ny - 1)])

    send, slot = call(
        deposit_kernel,
        [SMEM, SMEM, VMEM, VMEM],
        [shape(slots, 4, 128), shape(blocks, dtype=jnp.int32)],
        [VMEM, SMEM],
        [pltpu.SMEM((tiles,), jnp.int32)],
    )(brick_owner[:, 0], brick_local, cell_in_brick, vel)
    recv = lax.all_to_all(send.reshape(slots * 4, 128), ("gx", "gy"), split_axis=0, concat_axis=0, tiled=True)

    pair_scratch = [
        pltpu.VMEM(((blocks + 32) * 16, 128), F32),
        pltpu.VMEM((blocks * 32, 128), F32),
        pltpu.VMEM((blocks * 8, 128), F32),
    ]
    push = call(
        push_kernel,
        [SMEM, SMEM, VMEM, VMEM, VMEM],
        shape(blocks * 8, 128),
        VMEM,
        pair_scratch,
        pl.CostEstimate(flops=20_000_000_000, bytes_accessed=2_000_000, transcendentals=8_000_000),
    )(pair_self, pair_other, pos, from_low, from_high)

    me = lax.axis_index("gx")
    ends = jnp.stack([me > 0, me < nx - 1]).astype(jnp.int32)
    fluid, answer = call(
        fluid_kernel,
        [SMEM] + [VMEM] * 6,
        [shape(3, sx, sy, sz), shape(slots * 4, 128)],
        [VMEM] * 2,
        [pltpu.VMEM((4, sx, sy, sz), F32)],
    )(ends, recv, fluid_vel, from_low, from_high, from_left, from_right)
    back = lax.all_to_all(answer, ("gx", "gy"), split_axis=0, concat_axis=0, tiled=True)

    flow, pos, vel, down, up = call(
        pick_kernel,
        [SMEM, SMEM] + [VMEM] * 5,
        [shape(blocks * 8, 128), shape(3, blocks, 128), shape(3, blocks, 128), shape(48, 128), shape(48, 128)],
        [VMEM] * 5,
    )(slot, halo_list, back.reshape(slots, 4, 128), cell_in_brick, pos, vel, push)
    low = lax.ppermute(up, "gx", fwd)
    high = lax.ppermute(down, "gx", bwd)
    pos, vel = call(
        last_kernel,
        [SMEM, SMEM] + [VMEM] * 5,
        [shape(3, blocks, 128), shape(3, blocks, 128)],
        [VMEM] * 2,
        [pltpu.VMEM((blocks * 8, 128), F32)] + pair_scratch,
    )(pair_self, pair_other, pos, vel, low, high, flow)
    return fluid, jnp.transpose(pos, (1, 0, 2)), jnp.transpose(vel, (1, 0, 2))


def solution(mesh):
    in_specs = (
        P(None, "gx", "gy", None),
        P(("gx", "gy"), None, None),
        P(("gx", "gy"), None, None),
        P(("gx", "gy"), None),
        P(("gx", "gy")),
        P(("gx", "gy"), None),
        P(None, ("gx", "gy")),
        P(None, ("gx", "gy")),
        P(("gx", "gy")),
    )
    out_specs = (
        P(None, "gx", "gy", None),
        P(("gx", "gy"), None, None),
        P(("gx", "gy"), None, None),
    )
    return jax.shard_map(
        per_device, mesh=mesh, in_specs=in_specs, out_specs=out_specs, check_vma=False
    )
```

```python
import functools

import jax
import jax.numpy as jnp
from jax import lax
from jax.experimental import pallas as pl
from jax.experimental.pallas import tpu as pltpu
from jax.sharding import PartitionSpec as P

F32 = jnp.float32
BF16 = jnp.bfloat16
PAIR_GROUP = 64
BLOCK_GROUP = 32
CAP = 4
EPS2 = 0.0025
VMEM = pl.BlockSpec(memory_space=pltpu.VMEM)
SMEM = pl.BlockSpec(memory_space=pltpu.SMEM)
PARAMS = dict(vmem_limit_bytes=48 * 1024 * 1024)


def split2(x):
    hi = x.astype(BF16)
    return hi, (x - hi.astype(F32)).astype(BF16)


def onehot_cells(row):
    cells = lax.broadcasted_iota(jnp.int32, (128, 128), 0)
    return (cells == jnp.broadcast_to(row, (128, 128))).astype(F32).astype(BF16)


def dot(a, b, dims=((1,), (0,))):
    return lax.dot_general(a, b, (dims, ((), ())), preferred_element_type=F32)


def pack_rows(halo, pos, out, first, half):
    for j in range(16):
        q = halo[half * 16 + j]
        for m in range(3):
            out[pl.ds(first + m * 16 + j, 1), :] = pos[m, pl.ds(q, 1), :]


def faces_kernel(halo, fv, pos, down_out, up_out, left_out, right_out):
    sx = fv.shape[1]
    for out, x, half in ((down_out, 0, 0), (up_out, sx - 1, 1)):
        for m in range(3):
            for h in range(2):
                out[(m * 2 + h) * 16 : (m * 2 + h + 1) * 16, :] = fv[m, x, :, h * 128 : (h + 1) * 128]
        pack_rows(halo, pos, out, 96, half)
    for out, y in ((left_out, 0), (right_out, fv.shape[2] - 1)):
        for m in range(3):
            out[m, :, :] = fv[m, :, y, :]


def deposit_kernel(owner, local, cell, vel, after, out, slot_out, done, taken):
    blocks = cell.shape[0]
    lanes = lax.broadcasted_iota(jnp.int32, (4, 128), 1)
    rows4 = lax.broadcasted_iota(jnp.int32, (4, 128), 0)
    mark = (lanes == 127) & (rows4 == 0)
    done[...] = jnp.zeros(done.shape, F32)
    out[...] = jnp.broadcast_to(jnp.where(mark, -1.0, 0.0).astype(F32)[None], out.shape)

    def clear(t, c):
        taken[t] = 0
        return c

    lax.fori_loop(0, taken.shape[0], clear, 0, unroll=8)
    r8 = lax.broadcasted_iota(jnp.int32, (8, 128), 0)

    def group(g, c):
        base = pl.multiple_of(g * BLOCK_GROUP, BLOCK_GROUP)
        cells = cell[pl.ds(base, BLOCK_GROUP), :]
        v = [vel[m, pl.ds(base, BLOCK_GROUP), :] for m in range(3)]
        for k in range(BLOCK_GROUP):
            q = base + k
            hot = onehot_cells(cells[k : k + 1, :])
            rows = [jnp.broadcast_to(v[m][k : k + 1, :], (8, 128)) for m in range(3)]
            load = jnp.where(r8 == 1, rows[0], jnp.where(r8 == 2, rows[1], rows[2]))
            load = jnp.where(r8 == 0, 1.0, jnp.where(r8 < 4, load, 0.0))
            hi = load.astype(BF16).astype(F32)
            lhs = jnp.concatenate([hi, load - hi], axis=0).astype(BF16)
            both = dot(lhs, hot, ((1,), (1,)))
            both = both[0:8] + both[8:16]
            tile = owner[q]
            rank = taken[tile]
            taken[tile] = rank + 1
            slot = tile * CAP + rank
            slot_out[q] = slot
            ident = jnp.full((4, 128), local[q], jnp.int32).astype(F32)
            out[slot] = jnp.where(mark, ident, both[0:4])
        return c

    lax.fori_loop(0, blocks // BLOCK_GROUP, group, 0)


def swap_groups(v):
    row = lax.broadcasted_iota(jnp.int32, v.shape, 1)
    grp = lax.broadcasted_iota(jnp.int32, v.shape, 2) // 16
    for s in range(3):
        step = 1 << s
        ra, gb = (row >> s) & 1, (grp >> s) & 1
        up = pltpu.roll(pltpu.roll(v, 8 - step, 1), 16 * step, 2)
        dn = pltpu.roll(pltpu.roll(v, step, 1), 128 - 16 * step, 2)
        v = jnp.where(ra == gb, v, jnp.where(ra < gb, up, dn))
    return v


def fluid_kernel(xlo_on, recv, fv, from_low, from_high, from_left, from_right, after, fluid, answer, done, grid):
    sx, sy, sz = fv.shape[1:]
    slots = recv.shape[0] // 4
    bricks = sx // 2 * (sy // 4) * (sz // 16)
    count = recv[pl.ds(0, slots, stride=4), :]
    lane = lax.broadcasted_iota(jnp.int32, (slots, 128), 1)
    ident = count[:, 127:128]
    ident_row = count.T[127:128, :]
    wide = lax.broadcasted_iota(jnp.int32, (slots, bricks), 1).astype(F32)
    by_slot = (wide == jnp.broadcast_to(ident, (slots, bricks))).astype(F32).astype(BF16)
    tall = lax.broadcasted_iota(jnp.int32, (bricks, slots), 0).astype(F32)
    by_brick = (tall == jnp.broadcast_to(ident_row, (bricks, slots))).astype(F32).astype(BF16)
    parts = [jnp.where(lane == 127, 1.0, count).astype(BF16)]
    for m in range(3):
        parts += list(split2(recv[pl.ds(m + 1, slots, stride=4), :]))
    summed = dot(by_brick, jnp.concatenate(parts, axis=1))
    cnt = summed[:, 0:128]
    momentum = [summed[:, (1 + 2 * m) * 128 : (2 + 2 * m) * 128] + summed[:, (2 + 2 * m) * 128 : (3 + 2 * m) * 128] for m in range(3)]
    last = lax.broadcasted_iota(jnp.int32, (bricks, 128), 1) == 127
    others = jnp.sum(jnp.where(last, 0.0, cnt), axis=1, keepdims=True)
    cnt = jnp.where(last, 128.0 * cnt - others, cnt)
    solid = 0.5 * cnt
    voids = 1.0 - 0.6 * solid / (1.0 + solid)
    beta = (1.0 - voids) / (voids * voids)
    scale = 0.15 * beta
    sources = [scale * momentum[m] for m in range(3)] + [scale * cnt]
    for c in range(4):
        moved = swap_groups(sources[c].reshape(bricks // 8, 8, 128))
        for bx in range(sx // 2):
            for by in range(sy // 4):
                for h in range(2):
                    v = moved[(bx * 4 + by) * 2 + h]
                    for x in range(2):
                        grid[c, bx * 2 + x, by * 4 : by * 4 + 4, h * 128 : h * 128 + 128] = v[x * 4 : x * 4 + 4, :]
    yrow = lax.broadcasted_iota(jnp.int32, (sy, sz), 0)
    zlane = lax.broadcasted_iota(jnp.int32, (sy, sz), 1)
    low_on = (xlo_on[0]).astype(F32)
    high_on = (xlo_on[1]).astype(F32)
    for m in range(3):
        low = jnp.concatenate([from_low[(m * 2 + h) * 16 : (m * 2 + h + 1) * 16, :] for h in range(2)], axis=1) * low_on
        high = jnp.concatenate([from_high[(m * 2 + h) * 16 : (m * 2 + h + 1) * 16, :] for h in range(2)], axis=1) * high_on
        for x in range(sx):
            f = fv[m, x]
            beside = (fv[m, x + 1] if x < sx - 1 else high) + (fv[m, x - 1] if x > 0 else low)
            right = jnp.broadcast_to(from_right[m, x : x + 1, :], (sy, sz))
            left = jnp.broadcast_to(from_left[m, x : x + 1, :], (sy, sz))
            beside = beside + jnp.where(yrow == sy - 1, right, pltpu.roll(f, sy - 1, 0))
            beside = beside + jnp.where(yrow == 0, left, pltpu.roll(f, 1, 0))
            beside = beside + jnp.where(zlane == sz - 1, 0.0, pltpu.roll(f, sz - 1, 1))
            beside = beside + jnp.where(zlane == 0, 0.0, pltpu.roll(f, 1, 1))
            fluid[m, x] = f + 0.1 * (beside - 6.0 * f) + (grid[m, x] - grid[3, x] * f)
    table = []
    for m in range(3):
        tiles = []
        for bx in range(sx // 2):
            for by in range(sy // 4):
                for h in range(2):
                    tiles.append(
                        jnp.concatenate(
                            [fluid[m, bx * 2 + x, by * 4 : by * 4 + 4, h * 128 : h * 128 + 128] for x in range(2)],
                            axis=0,
                        )
                    )
        v = swap_groups(jnp.stack(tiles, axis=0)).reshape(bricks, 128)
        table += list(split2(v))
    table += list(split2(beta))
    found = dot(by_slot, jnp.concatenate(table, axis=1))
    for c in range(4):
        answer[pl.ds(c, slots, stride=4), :] = (
            found[:, 2 * c * 128 : (2 * c + 1) * 128] + found[:, (2 * c + 1) * 128 : (2 * c + 2) * 128]
        )
    done[...] = jnp.zeros(done.shape, F32)


def feature_rows(x):
    hi, lo, both = [], [], []
    for m in range(3):
        u = x[m] - 0.5
        h = u.astype(BF16).astype(F32)
        l = (u - h).astype(BF16).astype(F32)
        hi.append(h)
        lo.append(l)
        both.append(h + l)
    return hi, lo, both, both[0] * both[0] + both[1] * both[1] + both[2] * both[2]


def split3(n):
    a = n.astype(BF16).astype(F32)
    b = (n - a).astype(BF16).astype(F32)
    return a, b, n - a - b


def push_loop(step, begin, end, first, second, pos, low, high, push, feat_b, feat_a):
    blocks = pos.shape[1]
    one = jnp.ones((8, 128), F32)
    zero = jnp.zeros((8, 128), F32)

    def put(ref, q0, feats):
        for k, v in enumerate(feats):
            ref[pl.ds(q0 * 16 + k, 8, stride=16), :] = v

    def own(g, c):
        q0 = pl.multiple_of(g * 8, 8)
        hi, lo, both, norm = feature_rows([pos[m, pl.ds(q0, 8), :] for m in range(3)])
        n = split3(norm)
        put(feat_b, q0, hi + [one, n[0], n[1], n[2], one] + lo + [one, zero, zero, zero, zero])
        n = split3(norm + EPS2)
        h2, l2 = [-2.0 * v for v in hi], [-2.0 * v for v in lo]
        put(feat_a, q0, h2 + [n[0], one, one, one, n[1]] + l2 + [n[2], zero, zero, zero, zero])
        return c

    lax.fori_loop(0, blocks // 8, own, 0, unroll=2)
    for i, (ref, at) in enumerate((low, high)):
        for g in range(2):
            hi, lo, _, norm = feature_rows([ref[at + m * 16 + g * 8 : at + m * 16 + g * 8 + 8, :] for m in range(3)])
            n = split3(norm)
            put(feat_b, blocks + i * 16 + g * 8, hi + [one, n[0], n[1], n[2], one] + lo + [one, zero, zero, zero, zero])
    push[...] = jnp.zeros(push.shape, F32)
    top = lax.broadcasted_iota(jnp.int32, (8, 128), 0) < 3

    def one_pair(p):
        a = first[step, p]
        b = second[step, p]
        fb = feat_b[pl.ds(pl.multiple_of(b * 16, 16), 16), :]
        fa = feat_a[pl.ds(pl.multiple_of(a * 16, 16), 16), :]
        x, y = fa[0:8], fa[8:16]
        z = jnp.where(top, y, 0.0)
        ga = jnp.concatenate([x, jnp.where(top, x, y), z, z], axis=0).astype(BF16)
        fbt = jnp.concatenate([fb, fb], axis=0).T.astype(BF16)
        r2 = dot(fbt, ga)
        w = jnp.maximum(lax.rsqrt(jnp.maximum(r2, EPS2)) - 4.0, 0.0)
        lhs = fb.astype(BF16)
        res = dot(jnp.concatenate([lhs, lhs], axis=1), jnp.concatenate(split2(w), axis=0))
        total = jnp.broadcast_to(res[3:4], (8, 128))
        return a, (-0.5) * (x + z) * total - (res[0:8] + res[8:16])

    def pairs(g, c):
        done = [one_pair(g * PAIR_GROUP + k) for k in range(PAIR_GROUP)]
        for a, f in done:
            rows = pl.ds(pl.multiple_of(a * 8, 8), 8)
            push[rows, :] = push[rows, :] + f
        return c

    lax.fori_loop(begin // PAIR_GROUP, end // PAIR_GROUP, pairs, 0)


def push_kernel(begin, end, first, second, pos, low, high, after, push, done, feat_b, feat_a):
    push_loop(0, begin, end, first, second, pos, (low, 96), (high, 96), push, feat_b, feat_a)
    done[...] = jnp.zeros(done.shape, F32)


def advance(pos, vel, push, flow, pos_out, vel_out):
    blocks = pos.shape[1]
    drift = 2.0 * flow[pl.ds(3, blocks, stride=8), :]
    for m in range(3):
        v = vel[m]
        total = sum(part[pl.ds(m, blocks, stride=8), :] for part in push)
        force = 2.5 * total + drift * (flow[pl.ds(m, blocks, stride=8), :] - v)
        if m == 2:
            force = force - 1.0
        v = v + 0.1 * force
        vel_out[m] = v
        pos_out[m] = pos[m] + 0.1 * v


def pick(hot, v):
    v = jnp.concatenate([v, v], axis=0)
    hi = v.astype(BF16).astype(F32)
    both = dot(jnp.concatenate([hi, v - hi], axis=0).astype(BF16), hot)
    return both[0:8] + both[8:16]


def listed_kernel(slot, halo, back, cell, pos, vel, push_a, push_b, down_out, up_out):
    r8 = lax.broadcasted_iota(jnp.int32, (8, 128), 0)

    def tile(ref, q):
        rows = [jnp.broadcast_to(ref[m, pl.ds(q, 1), :], (8, 128)) for m in range(3)]
        return jnp.where(r8 == 0, rows[0], jnp.where(r8 == 1, rows[1], rows[2]))

    for half, out in ((0, down_out), (1, up_out)):
        for j in range(16):
            q = halo[half * 16 + j]
            flow = pick(onehot_cells(cell[pl.ds(q, 1), :]), back[slot[q]])
            v = tile(vel, q)
            rows = pl.ds(pl.multiple_of(q * 8, 8), 8)
            drift = 2.0 * jnp.broadcast_to(flow[3:4], (8, 128))
            force = 2.5 * (push_a[rows, :] + push_b[rows, :]) + drift * (flow - v)
            v = v + 0.1 * jnp.where(r8 == 2, force - 1.0, force)
            x = tile(pos, q) + 0.1 * v
            for m in range(3):
                out[m * 16 + j : m * 16 + j + 1, :] = x[m : m + 1, :]


def pick_kernel(slot, back, cell, pos, vel, push_a, push_b, after, flow, pos_out, vel_out):
    def group(g, c):
        base = pl.multiple_of(g * BLOCK_GROUP, BLOCK_GROUP)
        cells = cell[pl.ds(base, BLOCK_GROUP), :]
        for k in range(BLOCK_GROUP):
            q = base + k
            flow[pl.ds(pl.multiple_of(q * 8, 8), 8), :] = pick(onehot_cells(cells[k : k + 1, :]), back[slot[q]])
        return c

    lax.fori_loop(0, cell.shape[0] // BLOCK_GROUP, group, 0)
    advance(pos, vel, (push_a, push_b), flow, pos_out, vel_out)


def last_kernel(first, second, pos, vel, low, high, flow, pos_out, vel_out, push, feat_b, feat_a):
    push_loop(1, 0, first.shape[1], first, second, pos, (low, 0), (high, 0), push, feat_b, feat_a)
    advance(pos, vel, (push,), flow, pos_out, vel_out)


def call(kernel, in_specs, out_shape, out_specs, scratch=(), micros=1):
    return pl.pallas_call(
        kernel,
        in_specs=in_specs,
        out_shape=out_shape,
        out_specs=out_specs,
        scratch_shapes=list(scratch),
        compiler_params=pltpu.CompilerParams(**PARAMS),
        cost_estimate=pl.CostEstimate(flops=micros * 1_000_000_000, bytes_accessed=micros * 3_000_000, transcendentals=0),
    )


def shape(*dims, dtype=F32):
    return jax.ShapeDtypeStruct(dims, dtype)


def per_device(
    fluid_vel,
    part_pos,
    part_vel,
    brick_owner,
    brick_local,
    cell_in_brick,
    pair_self,
    pair_other,
    halo_list,
):
    nx, ny = lax.axis_size("gx"), lax.axis_size("gy")
    tiles = nx * ny
    blocks = part_pos.shape[0]
    slots = tiles * CAP
    sx, sy, sz = fluid_vel.shape[1:]
    pos = jnp.transpose(part_pos, (1, 0, 2))
    vel = jnp.transpose(part_vel, (1, 0, 2))

    down, up, left, right = call(
        faces_kernel,
        [SMEM, VMEM, VMEM],
        [shape(144, 128), shape(144, 128), shape(3, sx, sz), shape(3, sx, sz)],
        [VMEM] * 4,
    )(halo_list, fluid_vel, pos)
    fwd = [(i, (i + 1) % nx) for i in range(nx)]
    bwd = [((i + 1) % nx, i) for i in range(nx)]
    from_low = lax.ppermute(up, "gx", fwd)
    from_high = lax.ppermute(down, "gx", bwd)
    from_left = lax.ppermute(right, "gy", [(i, i + 1) for i in range(ny - 1)])
    from_right = lax.ppermute(left, "gy", [(i + 1, i) for i in range(ny - 1)])

    send, slot, placed = call(
        deposit_kernel,
        [SMEM, SMEM, VMEM, VMEM, VMEM],
        [shape(slots, 4, 128), shape(blocks, dtype=jnp.int32), shape(8, 128)],
        [VMEM, SMEM, VMEM],
        [pltpu.SMEM((tiles,), jnp.int32)],
        7,
    )(brick_owner[:, 0], brick_local, cell_in_brick, vel, down)
    recv = lax.all_to_all(send.reshape(slots * 4, 128), ("gx", "gy"), split_axis=0, concat_axis=0, tiled=True)

    pairs = pair_self.shape[1]
    pair_scratch = [pltpu.VMEM(((blocks + 32) * 16, 128), F32), pltpu.VMEM((blocks * 16, 128), F32)]

    def push(begin, end, after):
        return call(
            functools.partial(push_kernel, begin, end),
            [SMEM, SMEM, VMEM, VMEM, VMEM, VMEM],
            [shape(blocks * 8, 128), shape(8, 128)],
            [VMEM, VMEM],
            pair_scratch,
            8,
        )(pair_self, pair_other, pos, from_low, from_high, after)

    push_a, done_a = push(0, pairs // 2, placed)
    me = lax.axis_index("gx")
    ends = jnp.stack([me > 0, me < nx - 1]).astype(jnp.int32)
    fluid, answer, stepped = call(
        fluid_kernel,
        [SMEM] + [VMEM] * 7,
        [shape(3, sx, sy, sz), shape(slots * 4, 128), shape(8, 128)],
        [VMEM] * 3,
        [pltpu.VMEM((4, sx, sy, sz), F32)],
        4,
    )(ends, recv, fluid_vel, from_low, from_high, from_left, from_right, done_a)
    back = lax.all_to_all(answer, ("gx", "gy"), split_axis=0, concat_axis=0, tiled=True).reshape(slots, 4, 128)
    push_b, _ = push(pairs // 2, pairs, stepped)

    down, up = call(
        listed_kernel,
        [SMEM, SMEM] + [VMEM] * 6,
        [shape(48, 128), shape(48, 128)],
        [VMEM] * 2,
        (),
        2,
    )(slot, halo_list, back, cell_in_brick, pos, vel, push_a, push_b)
    low = lax.ppermute(up, "gx", fwd)
    high = lax.ppermute(down, "gx", bwd)
    flow, pos, vel = call(
        pick_kernel,
        [SMEM] + [VMEM] * 7,
        [shape(blocks * 8, 128), shape(3, blocks, 128), shape(3, blocks, 128)],
        [VMEM] * 3,
        (),
        6,
    )(slot, back, cell_in_brick, pos, vel, push_a, push_b, down)
    pos, vel = call(
        last_kernel,
        [SMEM, SMEM] + [VMEM] * 5,
        [shape(3, blocks, 128), shape(3, blocks, 128)],
        [VMEM] * 2,
        [pltpu.VMEM((blocks * 8, 128), F32)] + pair_scratch,
        15,
    )(pair_self, pair_other, pos, vel, low, high, flow)
    return fluid, jnp.transpose(pos, (1, 0, 2)), jnp.transpose(vel, (1, 0, 2))


def solution(mesh):
    in_specs = (
        P(None, "gx", "gy", None),
        P(("gx", "gy"), None, None),
        P(("gx", "gy"), None, None),
        P(("gx", "gy"), None),
        P(("gx", "gy")),
        P(("gx", "gy"), None),
        P(None, ("gx", "gy")),
        P(None, ("gx", "gy")),
        P(("gx", "gy")),
    )
    out_specs = (
        P(None, "gx", "gy", None),
        P(("gx", "gy"), None, None),
        P(("gx", "gy"), None, None),
    )
    return jax.shard_map(
        per_device, mesh=mesh, in_specs=in_specs, out_specs=out_specs, check_vma=False
    )
```

```python
import functools

import jax
import jax.numpy as jnp
from jax import lax
from jax.experimental import pallas as pl
from jax.experimental.pallas import tpu as pltpu
from jax.sharding import PartitionSpec as P

F32 = jnp.float32
BF16 = jnp.bfloat16
PAIR_GROUP = 128
BLOCK_GROUP = 32
CAP = 4
EPS2 = 0.0025
VMEM = pl.BlockSpec(memory_space=pltpu.VMEM)
SMEM = pl.BlockSpec(memory_space=pltpu.SMEM)
PARAMS = dict(vmem_limit_bytes=20 * 1024 * 1024)


def split2(x):
    hi = x.astype(BF16)
    return hi, (x - hi.astype(F32)).astype(BF16)


def onehot_cells(row):
    cells = lax.broadcasted_iota(jnp.int32, (128, 128), 0)
    return (cells == jnp.broadcast_to(row, (128, 128))).astype(F32).astype(BF16)


def dot(a, b, dims=((1,), (0,))):
    return lax.dot_general(a, b, (dims, ((), ())), preferred_element_type=F32)


def pack_rows(halo, pos, out, first, half):
    for j in range(16):
        q = halo[half * 16 + j]
        for m in range(3):
            out[pl.ds(first + m * 16 + j, 1), :] = pos[m, pl.ds(q, 1), :]


def faces_kernel(halo, fv, pos, after, down_out, up_out, left_out, right_out):
    sx = fv.shape[1]
    for out, x, half in ((down_out, 0, 0), (up_out, sx - 1, 1)):
        for m in range(3):
            for h in range(2):
                out[(m * 2 + h) * 16 : (m * 2 + h + 1) * 16, :] = fv[m, x, :, h * 128 : (h + 1) * 128]
        pack_rows(halo, pos, out, 96, half)
    for out, y in ((left_out, 0), (right_out, fv.shape[2] - 1)):
        for m in range(3):
            out[m, :, :] = fv[m, :, y, :]


def deposit_kernel(owner, local, cell, vel, out, slot_out, done, taken):
    blocks = cell.shape[0]
    lanes = lax.broadcasted_iota(jnp.int32, (4, 128), 1)
    rows4 = lax.broadcasted_iota(jnp.int32, (4, 128), 0)
    mark = (lanes == 127) & (rows4 == 0)
    done[...] = jnp.zeros(done.shape, F32)
    out[...] = jnp.broadcast_to(jnp.where(mark, -1.0, 0.0).astype(F32)[None], out.shape)

    def clear(t, c):
        taken[t] = 0
        return c

    lax.fori_loop(0, taken.shape[0], clear, 0, unroll=8)
    r8 = lax.broadcasted_iota(jnp.int32, (8, 128), 0)

    def group(g, c):
        base = pl.multiple_of(g * BLOCK_GROUP, BLOCK_GROUP)
        cells = cell[pl.ds(base, BLOCK_GROUP), :]
        v = [vel[m, pl.ds(base, BLOCK_GROUP), :] for m in range(3)]
        for k in range(BLOCK_GROUP):
            q = base + k
            hot = onehot_cells(cells[k : k + 1, :])
            rows = [jnp.broadcast_to(v[m][k : k + 1, :], (8, 128)) for m in range(3)]
            load = jnp.where(r8 == 1, rows[0], jnp.where(r8 == 2, rows[1], rows[2]))
            load = jnp.where(r8 == 0, 1.0, jnp.where(r8 < 4, load, 0.0))
            hi = load.astype(BF16).astype(F32)
            lhs = jnp.concatenate([hi, load - hi], axis=0).astype(BF16)
            both = dot(lhs, hot, ((1,), (1,)))
            both = both[0:8] + both[8:16]
            tile = owner[q]
            rank = taken[tile]
            taken[tile] = rank + 1
            slot = tile * CAP + rank
            slot_out[q] = slot
            ident = jnp.full((4, 128), local[q], jnp.int32).astype(F32)
            out[slot] = jnp.where(mark, ident, both[0:4])
        return c

    lax.fori_loop(0, blocks // BLOCK_GROUP, group, 0)


def swap_groups(v):
    row = lax.broadcasted_iota(jnp.int32, v.shape, 1)
    grp = lax.broadcasted_iota(jnp.int32, v.shape, 2) // 16
    for s in range(3):
        step = 1 << s
        ra, gb = (row >> s) & 1, (grp >> s) & 1
        up = pltpu.roll(pltpu.roll(v, 8 - step, 1), 16 * step, 2)
        dn = pltpu.roll(pltpu.roll(v, step, 1), 128 - 16 * step, 2)
        v = jnp.where(ra == gb, v, jnp.where(ra < gb, up, dn))
    return v


def spread_kernel(inside, fv, from_low, from_high, from_left, from_right, out):
    sx, sy, sz = fv.shape[1:]
    yrow = lax.broadcasted_iota(jnp.int32, (sy, sz), 0)
    zlane = lax.broadcasted_iota(jnp.int32, (sy, sz), 1)
    low_on = (inside[0]).astype(F32)
    high_on = (inside[1]).astype(F32)
    for m in range(3):
        low = jnp.concatenate([from_low[(m * 2 + h) * 16 : (m * 2 + h + 1) * 16, :] for h in range(2)], axis=1) * low_on
        high = jnp.concatenate([from_high[(m * 2 + h) * 16 : (m * 2 + h + 1) * 16, :] for h in range(2)], axis=1) * high_on
        for x in range(sx):
            f = fv[m, x]
            beside = (fv[m, x + 1] if x < sx - 1 else high) + (fv[m, x - 1] if x > 0 else low)
            right = jnp.broadcast_to(from_right[m, x : x + 1, :], (sy, sz))
            left = jnp.broadcast_to(from_left[m, x : x + 1, :], (sy, sz))
            beside = beside + jnp.where(yrow == sy - 1, right, pltpu.roll(f, sy - 1, 0))
            beside = beside + jnp.where(yrow == 0, left, pltpu.roll(f, 1, 0))
            beside = beside + jnp.where(zlane == sz - 1, 0.0, pltpu.roll(f, sz - 1, 1))
            beside = beside + jnp.where(zlane == 0, 0.0, pltpu.roll(f, 1, 1))
            out[m, x] = f + 0.1 * (beside - 6.0 * f)


def fluid_kernel(recv, fv, spread, fluid, answer, done, grid):
    sx, sy, sz = fv.shape[1:]
    slots = recv.shape[0] // 4
    bricks = sx // 2 * (sy // 4) * (sz // 16)
    count = recv[pl.ds(0, slots, stride=4), :]
    lane = lax.broadcasted_iota(jnp.int32, (slots, 128), 1)
    ident = count[:, 127:128]
    ident_row = count.T[127:128, :]
    wide = lax.broadcasted_iota(jnp.int32, (slots, bricks), 1).astype(F32)
    by_slot = (wide == jnp.broadcast_to(ident, (slots, bricks))).astype(F32).astype(BF16)
    tall = lax.broadcasted_iota(jnp.int32, (bricks, slots), 0).astype(F32)
    by_brick = (tall == jnp.broadcast_to(ident_row, (bricks, slots))).astype(F32).astype(BF16)
    parts = [jnp.where(lane == 127, 1.0, count).astype(BF16)]
    for m in range(3):
        parts += list(split2(recv[pl.ds(m + 1, slots, stride=4), :]))
    summed = dot(by_brick, jnp.concatenate(parts, axis=1))
    cnt = summed[:, 0:128]
    momentum = [summed[:, (1 + 2 * m) * 128 : (2 + 2 * m) * 128] + summed[:, (2 + 2 * m) * 128 : (3 + 2 * m) * 128] for m in range(3)]
    last = lax.broadcasted_iota(jnp.int32, (bricks, 128), 1) == 127
    others = jnp.sum(jnp.where(last, 0.0, cnt), axis=1, keepdims=True)
    cnt = jnp.where(last, 128.0 * cnt - others, cnt)
    solid = 0.5 * cnt
    voids = 1.0 - 0.6 * solid / (1.0 + solid)
    beta = (1.0 - voids) / (voids * voids)
    scale = 0.15 * beta
    sources = [scale * momentum[m] for m in range(3)] + [scale * cnt]
    for c in range(4):
        moved = swap_groups(sources[c].reshape(bricks // 8, 8, 128))
        for bx in range(sx // 2):
            for by in range(sy // 4):
                for h in range(2):
                    v = moved[(bx * 4 + by) * 2 + h]
                    for x in range(2):
                        grid[c, bx * 2 + x, by * 4 : by * 4 + 4, h * 128 : h * 128 + 128] = v[x * 4 : x * 4 + 4, :]
    for m in range(3):
        for x in range(sx):
            fluid[m, x] = spread[m, x] + (grid[m, x] - grid[3, x] * fv[m, x])
    table = []
    for m in range(3):
        tiles = []
        for bx in range(sx // 2):
            for by in range(sy // 4):
                for h in range(2):
                    tiles.append(
                        jnp.concatenate(
                            [fluid[m, bx * 2 + x, by * 4 : by * 4 + 4, h * 128 : h * 128 + 128] for x in range(2)],
                            axis=0,
                        )
                    )
        v = swap_groups(jnp.stack(tiles, axis=0)).reshape(bricks, 128)
        table += list(split2(v))
    table += list(split2(beta))
    found = dot(by_slot, jnp.concatenate(table, axis=1))
    for c in range(4):
        answer[pl.ds(c, slots, stride=4), :] = (
            found[:, 2 * c * 128 : (2 * c + 1) * 128] + found[:, (2 * c + 1) * 128 : (2 * c + 2) * 128]
        )
    done[...] = jnp.zeros(done.shape, F32)


def feature_rows(x):
    hi, lo, both = [], [], []
    for m in range(3):
        u = x[m] - 0.5
        h = u.astype(BF16).astype(F32)
        l = (u - h).astype(BF16).astype(F32)
        hi.append(h)
        lo.append(l)
        both.append(h + l)
    return hi, lo, both, both[0] * both[0] + both[1] * both[1] + both[2] * both[2]


def split3(n):
    a = n.astype(BF16).astype(F32)
    b = (n - a).astype(BF16).astype(F32)
    return a, b, n - a - b


def push_loop(step, first, second, pos, low, high, push, feat_b, feat_a):
    blocks = pos.shape[1]
    one = jnp.ones((8, 128), F32)
    zero = jnp.zeros((8, 128), F32)

    def put(ref, q0, feats):
        for k, v in enumerate(feats):
            ref[pl.ds(q0 * 16 + k, 8, stride=16), :] = v

    def own(g, c):
        q0 = pl.multiple_of(g * 8, 8)
        hi, lo, both, norm = feature_rows([pos[m, pl.ds(q0, 8), :] for m in range(3)])
        n = split3(norm)
        put(feat_b, q0, hi + [one, n[0], n[1], n[2], one] + lo + [one, zero, zero, zero, zero])
        n = split3(norm + EPS2)
        h2, l2 = [-2.0 * v for v in hi], [-2.0 * v for v in lo]
        put(feat_a, q0, h2 + [n[0], one, one, one, n[1]] + l2 + [n[2], zero, zero, zero, zero])
        return c

    lax.fori_loop(0, blocks // 8, own, 0, unroll=2)
    for i, (ref, at) in enumerate((low, high)):
        for g in range(2):
            hi, lo, _, norm = feature_rows([ref[at + m * 16 + g * 8 : at + m * 16 + g * 8 + 8, :] for m in range(3)])
            n = split3(norm)
            put(feat_b, blocks + i * 16 + g * 8, hi + [one, n[0], n[1], n[2], one] + lo + [one, zero, zero, zero, zero])
    push[...] = jnp.zeros(push.shape, F32)
    top = lax.broadcasted_iota(jnp.int32, (8, 128), 0) < 3

    def one_pair(p):
        a = first[step, p]
        b = second[step, p]
        fb = feat_b[pl.ds(pl.multiple_of(b * 16, 16), 16), :]
        fa = feat_a[pl.ds(pl.multiple_of(a * 16, 16), 16), :]
        x, y = fa[0:8], fa[8:16]
        z = jnp.where(top, y, 0.0)
        ga = jnp.concatenate([x, jnp.where(top, x, y), z, z], axis=0).astype(BF16)
        lhs = fb.astype(BF16)
        r2 = dot(jnp.concatenate([lhs, lhs], axis=0), ga, ((0,), (0,)))
        w = jnp.maximum(lax.rsqrt(jnp.maximum(r2, EPS2)) - 4.0, 0.0)
        res = dot(jnp.concatenate([lhs, lhs], axis=1), jnp.concatenate(split2(w), axis=0))
        total = jnp.broadcast_to(res[3:4], (8, 128))
        return a, (-0.5) * (x + z) * total - (res[0:8] + res[8:16])

    def pairs(g, c):
        done = [one_pair(g * PAIR_GROUP + k) for k in range(PAIR_GROUP)]
        for a, f in done:
            rows = pl.ds(pl.multiple_of(a * 8, 8), 8)
            push[rows, :] = push[rows, :] + f
        return c

    lax.fori_loop(0, first.shape[1] // PAIR_GROUP, pairs, 0)


def push_kernel(first, second, pos, low, high, after, push, feat_b, feat_a):
    push_loop(0, first, second, pos, (low, 96), (high, 96), push, feat_b, feat_a)


def advance(pos, vel, push, flow, pos_out, vel_out):
    blocks = pos.shape[1]
    drift = 2.0 * flow[pl.ds(3, blocks, stride=8), :]
    for m in range(3):
        v = vel[m]
        force = 2.5 * push[pl.ds(m, blocks, stride=8), :] + drift * (flow[pl.ds(m, blocks, stride=8), :] - v)
        if m == 2:
            force = force - 1.0
        v = v + 0.1 * force
        vel_out[m] = v
        pos_out[m] = pos[m] + 0.1 * v


def pick(hot, v):
    v = jnp.concatenate([v, v], axis=0)
    hi = v.astype(BF16).astype(F32)
    both = dot(jnp.concatenate([hi, v - hi], axis=0).astype(BF16), hot)
    return both[0:8] + both[8:16]


def listed_kernel(slot, halo, back, cell, pos, vel, push, down_out, up_out):
    r8 = lax.broadcasted_iota(jnp.int32, (8, 128), 0)

    def tile(ref, q):
        rows = [jnp.broadcast_to(ref[m, pl.ds(q, 1), :], (8, 128)) for m in range(3)]
        return jnp.where(r8 == 0, rows[0], jnp.where(r8 == 1, rows[1], rows[2]))

    for half, out in ((0, down_out), (1, up_out)):
        for j in range(16):
            q = halo[half * 16 + j]
            flow = pick(onehot_cells(cell[pl.ds(q, 1), :]), back[slot[q]])
            v = tile(vel, q)
            rows = pl.ds(pl.multiple_of(q * 8, 8), 8)
            drift = 2.0 * jnp.broadcast_to(flow[3:4], (8, 128))
            force = 2.5 * push[rows, :] + drift * (flow - v)
            v = v + 0.1 * jnp.where(r8 == 2, force - 1.0, force)
            x = tile(pos, q) + 0.1 * v
            for m in range(3):
                out[m * 16 + j : m * 16 + j + 1, :] = x[m : m + 1, :]


def pick_kernel(slot, back, cell, pos, vel, push, after, flow, pos_out, vel_out):
    def group(g, c):
        base = pl.multiple_of(g * BLOCK_GROUP, BLOCK_GROUP)
        cells = cell[pl.ds(base, BLOCK_GROUP), :]
        for k in range(BLOCK_GROUP):
            q = base + k
            flow[pl.ds(pl.multiple_of(q * 8, 8), 8), :] = pick(onehot_cells(cells[k : k + 1, :]), back[slot[q]])
        return c

    lax.fori_loop(0, cell.shape[0] // BLOCK_GROUP, group, 0)
    advance(pos, vel, push, flow, pos_out, vel_out)


def last_kernel(first, second, pos, vel, low, high, flow, pos_out, vel_out, push, feat_b, feat_a):
    push_loop(1, first, second, pos, (low, 0), (high, 0), push, feat_b, feat_a)
    advance(pos, vel, push, flow, pos_out, vel_out)


def call(kernel, in_specs, out_shape, out_specs, scratch=(), micros=1):
    return pl.pallas_call(
        kernel,
        in_specs=in_specs,
        out_shape=out_shape,
        out_specs=out_specs,
        scratch_shapes=list(scratch),
        compiler_params=pltpu.CompilerParams(**PARAMS),
        cost_estimate=pl.CostEstimate(flops=micros * 1_000_000_000, bytes_accessed=micros * 3_000_000, transcendentals=0),
    )


def shape(*dims, dtype=F32):
    return jax.ShapeDtypeStruct(dims, dtype)


def per_device(
    fluid_vel,
    part_pos,
    part_vel,
    brick_owner,
    brick_local,
    cell_in_brick,
    pair_self,
    pair_other,
    halo_list,
):
    nx, ny = lax.axis_size("gx"), lax.axis_size("gy")
    tiles = nx * ny
    blocks = part_pos.shape[0]
    slots = tiles * CAP
    sx, sy, sz = fluid_vel.shape[1:]
    pos = jnp.transpose(part_pos, (1, 0, 2))
    vel = jnp.transpose(part_vel, (1, 0, 2))

    send, slot, placed = call(
        deposit_kernel,
        [SMEM, SMEM, VMEM, VMEM],
        [shape(slots, 4, 128), shape(blocks, dtype=jnp.int32), shape(8, 128)],
        [VMEM, SMEM, VMEM],
        [pltpu.SMEM((tiles,), jnp.int32)],
        7,
    )(brick_owner[:, 0], brick_local, cell_in_brick, vel)
    recv = lax.all_to_all(send.reshape(slots * 4, 128), ("gx", "gy"), split_axis=0, concat_axis=0, tiled=True)
    down, up, left, right = call(
        faces_kernel,
        [SMEM, VMEM, VMEM, VMEM],
        [shape(144, 128), shape(144, 128), shape(3, sx, sz), shape(3, sx, sz)],
        [VMEM] * 4,
    )(halo_list, fluid_vel, pos, placed)
    fwd = [(i, (i + 1) % nx) for i in range(nx)]
    bwd = [((i + 1) % nx, i) for i in range(nx)]
    from_low = lax.ppermute(up, "gx", fwd)
    from_high = lax.ppermute(down, "gx", bwd)
    from_left = lax.ppermute(right, "gy", [(i, i + 1) for i in range(ny - 1)])
    from_right = lax.ppermute(left, "gy", [(i + 1, i) for i in range(ny - 1)])


    pair_scratch = [pltpu.VMEM(((blocks + 32) * 16, 128), F32), pltpu.VMEM((blocks * 16, 128), F32)]

    me = lax.axis_index("gx")
    ends = jnp.stack([me > 0, me < nx - 1]).astype(jnp.int32)
    spread = call(
        spread_kernel,
        [SMEM] + [VMEM] * 5,
        shape(3, sx, sy, sz),
        VMEM,
    )(ends, fluid_vel, from_low, from_high, from_left, from_right)
    fluid, answer, stepped = call(
        fluid_kernel,
        [VMEM] * 3,
        [shape(3, sx, sy, sz), shape(slots * 4, 128), shape(8, 128)],
        [VMEM] * 3,
        [pltpu.VMEM((4, sx, sy, sz), F32)],
        4,
    )(recv, fluid_vel, spread)
    back = lax.all_to_all(answer, ("gx", "gy"), split_axis=0, concat_axis=0, tiled=True).reshape(slots, 4, 128)
    push = call(
        push_kernel,
        [SMEM, SMEM, VMEM, VMEM, VMEM, VMEM],
        shape(blocks * 8, 128),
        VMEM,
        pair_scratch,
        14,
    )(pair_self, pair_other, pos, from_low, from_high, stepped)

    down, up = call(
        listed_kernel,
        [SMEM, SMEM] + [VMEM] * 5,
        [shape(48, 128), shape(48, 128)],
        [VMEM] * 2,
        (),
        2,
    )(slot, halo_list, back, cell_in_brick, pos, vel, push)
    low = lax.ppermute(up, "gx", fwd)
    high = lax.ppermute(down, "gx", bwd)
    flow, pos, vel = call(
        pick_kernel,
        [SMEM] + [VMEM] * 6,
        [shape(blocks * 8, 128), shape(3, blocks, 128), shape(3, blocks, 128)],
        [VMEM] * 3,
        (),
        6,
    )(slot, back, cell_in_brick, pos, vel, push, down)
    pos, vel = call(
        last_kernel,
        [SMEM, SMEM] + [VMEM] * 5,
        [shape(3, blocks, 128), shape(3, blocks, 128)],
        [VMEM] * 2,
        [pltpu.VMEM((blocks * 8, 128), F32)] + pair_scratch,
        15,
    )(pair_self, pair_other, pos, vel, low, high, flow)
    return fluid, jnp.transpose(pos, (1, 0, 2)), jnp.transpose(vel, (1, 0, 2))


def solution(mesh):
    in_specs = (
        P(None, "gx", "gy", None),
        P(("gx", "gy"), None, None),
        P(("gx", "gy"), None, None),
        P(("gx", "gy"), None),
        P(("gx", "gy")),
        P(("gx", "gy"), None),
        P(None, ("gx", "gy")),
        P(None, ("gx", "gy")),
        P(("gx", "gy")),
    )
    out_specs = (
        P(None, "gx", "gy", None),
        P(("gx", "gy"), None, None),
        P(("gx", "gy"), None, None),
    )
    return jax.shard_map(
        per_device, mesh=mesh, in_specs=in_specs, out_specs=out_specs, check_vma=False
    )
```

```python
import functools

import jax
import jax.numpy as jnp
from jax import lax
from jax.experimental import pallas as pl
from jax.experimental.pallas import tpu as pltpu
from jax.sharding import PartitionSpec as P

F32 = jnp.float32
BF16 = jnp.bfloat16
PAIR_GROUP = 128
BLOCK_GROUP = 32
DEPOSIT_GROUP = 64
CAP = 4
EPS2 = 0.0025
VMEM = pl.BlockSpec(memory_space=pltpu.VMEM)
SMEM = pl.BlockSpec(memory_space=pltpu.SMEM)
HBM = pl.BlockSpec(memory_space=pltpu.HBM)


def split2(x):
    hi = x.astype(BF16)
    return hi, (x - hi.astype(F32)).astype(BF16)


def onehot_cells(row):
    cells = lax.broadcasted_iota(jnp.int32, (128, 128), 0)
    return (cells == jnp.broadcast_to(row, (128, 128))).astype(F32).astype(BF16)


def dot(a, b, dims=((1,), (0,))):
    return lax.dot_general(a, b, (dims, ((), ())), preferred_element_type=F32)


def faces_kernel(fv, after, down_out, up_out, left_out, right_out):
    for out, x in ((down_out, 0), (up_out, fv.shape[1] - 1)):
        for m in range(3):
            out[m] = fv[m, x]
    for out, y in ((left_out, 0), (right_out, fv.shape[2] - 1)):
        for m in range(3):
            out[m] = fv[m, :, y, :]


def send_kernel(halo, pos, after, down_out, up_out):
    for half, out in ((0, down_out), (1, up_out)):
        for j in range(16):
            q = halo[half * 16 + j]
            for m in range(3):
                out[m * 16 + j : m * 16 + j + 1, :] = pos[m, pl.ds(q, 1), :]


def deposit_kernel(owner_in, local_in, cell_in, vel_in, out, slot_out, done, taken, owner, local, cell, vel, sems):
    blocks = cell.shape[0]
    copies = [
        pltpu.make_async_copy(src, dst, sems.at[i])
        for i, (src, dst) in enumerate(((vel_in, vel), (cell_in, cell), (owner_in, owner), (local_in, local)))
    ]
    for c in copies:
        c.start()
    lanes = lax.broadcasted_iota(jnp.int32, (4, 128), 1)
    rows4 = lax.broadcasted_iota(jnp.int32, (4, 128), 0)
    mark = (lanes == 127) & (rows4 == 0)
    done[...] = jnp.zeros(done.shape, F32)
    out[...] = jnp.broadcast_to(jnp.where(mark, -1.0, 0.0).astype(F32)[None], out.shape)

    def clear(t, c):
        taken[t] = 0
        return c

    lax.fori_loop(0, taken.shape[0], clear, 0, unroll=8)
    r8 = lax.broadcasted_iota(jnp.int32, (8, 128), 0)
    for c in copies:
        c.wait()

    def group(g, c):
        base = pl.multiple_of(g * DEPOSIT_GROUP, DEPOSIT_GROUP)
        cells = cell[pl.ds(base, DEPOSIT_GROUP), :]
        v = [vel[m, pl.ds(base, DEPOSIT_GROUP), :] for m in range(3)]
        for k in range(DEPOSIT_GROUP):
            q = base + k
            rows = [jnp.broadcast_to(v[m][k : k + 1, :], (8, 128)) for m in range(3)]
            load = jnp.where(r8 == 1, rows[0], jnp.where(r8 == 2, rows[1], rows[2]))
            load = jnp.where(r8 == 0, 1.0, jnp.where(r8 < 4, load, 0.0))
            hi = load.astype(BF16).astype(F32)
            lhs = jnp.concatenate([hi, load - hi], axis=0).astype(BF16)
            both = dot(lhs, onehot_cells(cells[k : k + 1, :]), ((1,), (1,)))
            both = both[0:8] + both[8:16]
            tile = owner[q]
            rank = taken[tile]
            taken[tile] = rank + 1
            slot = tile * CAP + rank
            slot_out[q] = slot
            ident = jnp.full((4, 128), local[q], jnp.int32).astype(F32)
            out[slot] = jnp.where(mark, ident, both[0:4])
        return c

    lax.fori_loop(0, blocks // DEPOSIT_GROUP, group, 0)


def swap_groups(v):
    row = lax.broadcasted_iota(jnp.int32, v.shape, 1)
    grp = lax.broadcasted_iota(jnp.int32, v.shape, 2) // 16
    for s in range(3):
        step = 1 << s
        ra, gb = (row >> s) & 1, (grp >> s) & 1
        up = pltpu.roll(pltpu.roll(v, 8 - step, 1), 16 * step, 2)
        dn = pltpu.roll(pltpu.roll(v, step, 1), 128 - 16 * step, 2)
        v = jnp.where(ra == gb, v, jnp.where(ra < gb, up, dn))
    return v


def places(sx, sy):
    return [
        (bx * 2, slice(by * 4, by * 4 + 4), slice(h * 128, h * 128 + 128))
        for bx in range(sx // 2)
        for by in range(sy // 4)
        for h in range(2)
    ]


def to_bricks(grid, m):
    tiles = [jnp.concatenate([grid[m, x, y, z], grid[m, x + 1, y, z]], axis=0) for x, y, z in places(*grid.shape[1:3])]
    return swap_groups(jnp.stack(tiles, axis=0)).reshape(len(tiles) * 8, 128)


def old_kernel(fv, bricks):
    for m in range(3):
        bricks[m] = to_bricks(fv, m)


def spread_kernel(fv, from_low, from_high, from_left, from_right, bricks, grid):
    sx, sy, sz = fv.shape[1:]
    yrow = lax.broadcasted_iota(jnp.int32, (sy, sz), 0)
    zlane = lax.broadcasted_iota(jnp.int32, (sy, sz), 1)
    for m in range(3):
        for x in range(sx):
            f = fv[m, x]
            high = fv[m, x + 1] if x < sx - 1 else from_high[m]
            low = fv[m, x - 1] if x > 0 else from_low[m]
            beside = high + low
            right = jnp.broadcast_to(from_right[m, x : x + 1, :], (sy, sz))
            left = jnp.broadcast_to(from_left[m, x : x + 1, :], (sy, sz))
            beside = beside + jnp.where(yrow == sy - 1, right, pltpu.roll(f, sy - 1, 0))
            beside = beside + jnp.where(yrow == 0, left, pltpu.roll(f, 1, 0))
            beside = beside + jnp.where(zlane == sz - 1, 0.0, pltpu.roll(f, sz - 1, 1))
            beside = beside + jnp.where(zlane == 0, 0.0, pltpu.roll(f, 1, 1))
            grid[m, x] = f + 0.1 * (beside - 6.0 * f)
    for m in range(3):
        bricks[m] = to_bricks(grid, m)


def fluid_kernel(recv, old, spread, answer, new):
    slots = recv.shape[0] // 4
    bricks = old.shape[1]
    count = recv[pl.ds(0, slots, stride=4), :]
    lane = lax.broadcasted_iota(jnp.int32, (slots, 128), 1)
    ident = count[:, 127:128]
    ident_row = count.T[127:128, :]
    wide = lax.broadcasted_iota(jnp.int32, (slots, bricks), 1).astype(F32)
    by_slot = (wide == jnp.broadcast_to(ident, (slots, bricks))).astype(F32).astype(BF16)
    tall = lax.broadcasted_iota(jnp.int32, (bricks, slots), 0).astype(F32)
    by_brick = (tall == jnp.broadcast_to(ident_row, (bricks, slots))).astype(F32).astype(BF16)
    parts = [jnp.where(lane == 127, 1.0, count).astype(BF16)]
    for m in range(3):
        parts += list(split2(recv[pl.ds(m + 1, slots, stride=4), :]))
    summed = dot(by_brick, jnp.concatenate(parts, axis=1))
    cnt = summed[:, 0:128]
    momentum = [summed[:, (1 + 2 * m) * 128 : (2 + 2 * m) * 128] + summed[:, (2 + 2 * m) * 128 : (3 + 2 * m) * 128] for m in range(3)]
    last = lax.broadcasted_iota(jnp.int32, (bricks, 128), 1) == 127
    others = jnp.sum(jnp.where(last, 0.0, cnt), axis=1, keepdims=True)
    cnt = jnp.where(last, 128.0 * cnt - others, cnt)
    solid = 0.5 * cnt
    voids = 1.0 - 0.6 * solid / (1.0 + solid)
    beta = (1.0 - voids) / (voids * voids)
    scale = 0.15 * beta
    table = []
    for m in range(3):
        fluid = spread[m] + scale * (momentum[m] - cnt * old[m])
        new[m] = fluid
        table += list(split2(fluid))
    table += list(split2(beta))
    found = dot(by_slot, jnp.concatenate(table, axis=1))
    for c in range(4):
        answer[pl.ds(c, slots, stride=4), :] = (
            found[:, 2 * c * 128 : (2 * c + 1) * 128] + found[:, (2 * c + 1) * 128 : (2 * c + 2) * 128]
        )


def feature_rows(x):
    hi, lo, both = [], [], []
    for m in range(3):
        u = x[m] - 0.5
        h = u.astype(BF16).astype(F32)
        l = (u - h).astype(BF16).astype(F32)
        hi.append(h)
        lo.append(l)
        both.append(h + l)
    return hi, lo, both, both[0] * both[0] + both[1] * both[1] + both[2] * both[2]


def split3(n):
    a = n.astype(BF16).astype(F32)
    b = (n - a).astype(BF16).astype(F32)
    return a, b, n - a - b


def push_loop(step, first, second, pos, low, high, push, feat_b, feat_a):
    blocks = pos.shape[1]
    one = jnp.ones((8, 128), F32)
    zero = jnp.zeros((8, 128), F32)

    def put(ref, q0, feats):
        for k, v in enumerate(feats):
            ref[pl.ds(q0 * 16 + k, 8, stride=16), :] = v

    def own(g, c):
        q0 = pl.multiple_of(g * 8, 8)
        hi, lo, both, norm = feature_rows([pos[m, pl.ds(q0, 8), :] for m in range(3)])
        n = split3(norm)
        put(feat_b, q0, hi + [one, n[0], n[1], n[2], one] + lo + [one, zero, zero, zero, zero])
        n = split3(norm + EPS2)
        h2, l2 = [-2.0 * v for v in hi], [-2.0 * v for v in lo]
        put(feat_a, q0, h2 + [n[0], one, one, one, n[1]] + l2 + [n[2], zero, zero, zero, zero])
        return c

    lax.fori_loop(0, blocks // 8, own, 0, unroll=2)
    for i, ref in enumerate((low, high)):
        for g in range(2):
            hi, lo, _, norm = feature_rows([ref[m * 16 + g * 8 : m * 16 + g * 8 + 8, :] for m in range(3)])
            n = split3(norm)
            put(feat_b, blocks + i * 16 + g * 8, hi + [one, n[0], n[1], n[2], one] + lo + [one, zero, zero, zero, zero])
    push[...] = jnp.zeros(push.shape, F32)
    top = lax.broadcasted_iota(jnp.int32, (8, 128), 0) < 3

    def one_pair(p):
        a = first[step, p]
        b = second[step, p]
        fb = feat_b[pl.ds(pl.multiple_of(b * 16, 16), 16), :]
        fa = feat_a[pl.ds(pl.multiple_of(a * 16, 16), 16), :]
        x, y = fa[0:8], fa[8:16]
        z = jnp.where(top, y, 0.0)
        ga = jnp.concatenate([x, jnp.where(top, x, y), z, z], axis=0).astype(BF16)
        lhs = fb.astype(BF16)
        r2 = dot(jnp.concatenate([lhs, lhs], axis=0), ga, ((0,), (0,)))
        w = jnp.maximum(lax.rsqrt(jnp.maximum(r2, EPS2)) - 4.0, 0.0)
        res = dot(jnp.concatenate([lhs, lhs], axis=1), jnp.concatenate(split2(w), axis=0))
        total = jnp.broadcast_to(res[3:4], (8, 128))
        return a, (-0.5) * (x + z) * total - (res[0:8] + res[8:16])

    def pairs(g, c):
        done = [one_pair(g * PAIR_GROUP + k) for k in range(PAIR_GROUP)]
        for a, f in done:
            rows = pl.ds(pl.multiple_of(a * 8, 8), 8)
            push[rows, :] = push[rows, :] + f
        return c

    lax.fori_loop(0, first.shape[1] // PAIR_GROUP, pairs, 0)


def push_kernel(first, second, pos, low, high, new, push, fluid, feat_b, feat_a):
    for m in range(3):
        moved = swap_groups(new[m].reshape(new.shape[1] // 8, 8, 128))
        for i, (x, y, z) in enumerate(places(*fluid.shape[1:3])):
            fluid[m, x, y, z] = moved[i, 0:4]
            fluid[m, x + 1, y, z] = moved[i, 4:8]
    push_loop(0, first, second, pos, low, high, push, feat_b, feat_a)


def advance(pos, vel, push, flow, pos_out, vel_out):
    blocks = pos.shape[1]
    drift = 2.0 * flow[pl.ds(3, blocks, stride=8), :]
    for m in range(3):
        v = vel[m]
        force = 2.5 * push[pl.ds(m, blocks, stride=8), :] + drift * (flow[pl.ds(m, blocks, stride=8), :] - v)
        if m == 2:
            force = force - 1.0
        v = v + 0.1 * force
        vel_out[m] = v
        pos_out[m] = pos[m] + 0.1 * v


def pick(hot, v):
    v = jnp.concatenate([v, v], axis=0)
    hi = v.astype(BF16).astype(F32)
    both = dot(jnp.concatenate([hi, v - hi], axis=0).astype(BF16), hot)
    return both[0:8] + both[8:16]


def listed_kernel(slot, halo, back, cell, pos, vel, push, down_out, up_out):
    r8 = lax.broadcasted_iota(jnp.int32, (8, 128), 0)

    def tile(ref, q):
        rows = [jnp.broadcast_to(ref[m, pl.ds(q, 1), :], (8, 128)) for m in range(3)]
        return jnp.where(r8 == 0, rows[0], jnp.where(r8 == 1, rows[1], rows[2]))

    for half, out in ((0, down_out), (1, up_out)):
        for j in range(16):
            q = halo[half * 16 + j]
            flow = pick(onehot_cells(cell[pl.ds(q, 1), :]), back[slot[q]])
            v = tile(vel, q)
            rows = pl.ds(pl.multiple_of(q * 8, 8), 8)
            drift = 2.0 * jnp.broadcast_to(flow[3:4], (8, 128))
            force = 2.5 * push[rows, :] + drift * (flow - v)
            v = v + 0.1 * jnp.where(r8 == 2, force - 1.0, force)
            x = tile(pos, q) + 0.1 * v
            for m in range(3):
                out[m * 16 + j : m * 16 + j + 1, :] = x[m : m + 1, :]


def pick_kernel(slot, back, cell, pos, vel, push, after, flow, pos_out, vel_out):
    def group(g, c):
        base = pl.multiple_of(g * BLOCK_GROUP, BLOCK_GROUP)
        cells = cell[pl.ds(base, BLOCK_GROUP), :]
        for k in range(BLOCK_GROUP):
            q = base + k
            flow[pl.ds(pl.multiple_of(q * 8, 8), 8), :] = pick(onehot_cells(cells[k : k + 1, :]), back[slot[q]])
        return c

    lax.fori_loop(0, cell.shape[0] // BLOCK_GROUP, group, 0)
    advance(pos, vel, push, flow, pos_out, vel_out)


def last_kernel(first, second, pos, vel, low, high, flow, pos_out, vel_out, push, feat_b, feat_a):
    push_loop(1, first, second, pos, low, high, push, feat_b, feat_a)
    advance(pos, vel, push, flow, pos_out, vel_out)


def call(kernel, in_specs, out_shape, out_specs, scratch=(), micros=1, vmem=20 * 1024 * 1024):
    return pl.pallas_call(
        kernel,
        in_specs=in_specs,
        out_shape=out_shape,
        out_specs=out_specs,
        scratch_shapes=list(scratch),
        compiler_params=pltpu.CompilerParams(vmem_limit_bytes=vmem),
        cost_estimate=pl.CostEstimate(flops=micros * 1_000_000_000, bytes_accessed=micros * 3_000_000, transcendentals=0),
    )


def shape(*dims, dtype=F32):
    return jax.ShapeDtypeStruct(dims, dtype)


def per_device(
    fluid_vel,
    part_pos,
    part_vel,
    brick_owner,
    brick_local,
    cell_in_brick,
    pair_self,
    pair_other,
    halo_list,
):
    nx, ny = lax.axis_size("gx"), lax.axis_size("gy")
    tiles = nx * ny
    blocks = part_pos.shape[0]
    slots = tiles * CAP
    sx, sy, sz = fluid_vel.shape[1:]
    pos = jnp.transpose(part_pos, (1, 0, 2))
    vel = jnp.transpose(part_vel, (1, 0, 2))

    send, slot, placed = call(
        deposit_kernel,
        [HBM] * 4,
        [shape(slots, 4, 128), shape(blocks, dtype=jnp.int32), shape(8, 128)],
        [VMEM, SMEM, VMEM],
        [
            pltpu.SMEM((tiles,), jnp.int32),
            pltpu.SMEM((blocks,), jnp.int32),
            pltpu.SMEM((blocks,), jnp.int32),
            pltpu.VMEM((blocks, 128), jnp.int32),
            pltpu.VMEM((3, blocks, 128), F32),
            pltpu.SemaphoreType.DMA((4,)),
        ],
        7,
        63_000_000,
    )(brick_owner[:, 0], brick_local, cell_in_brick, vel)
    recv = lax.all_to_all(send.reshape(slots * 4, 128), ("gx", "gy"), split_axis=0, concat_axis=0, tiled=True)

    down, up, left, right = call(
        faces_kernel,
        [VMEM, VMEM],
        [shape(3, sy, sz), shape(3, sy, sz), shape(3, sx, sz), shape(3, sx, sz)],
        [VMEM] * 4,
    )(fluid_vel, placed)
    from_low = lax.ppermute(up, "gx", [(i, i + 1) for i in range(nx - 1)])
    from_high = lax.ppermute(down, "gx", [(i + 1, i) for i in range(nx - 1)])
    from_left = lax.ppermute(right, "gy", [(i, i + 1) for i in range(ny - 1)])
    from_right = lax.ppermute(left, "gy", [(i + 1, i) for i in range(ny - 1)])
    down, up = call(
        send_kernel,
        [SMEM, VMEM, VMEM],
        [shape(48, 128), shape(48, 128)],
        [VMEM] * 2,
    )(halo_list, pos, left)
    fwd = [(i, (i + 1) % nx) for i in range(nx)]
    bwd = [((i + 1) % nx, i) for i in range(nx)]
    low = lax.ppermute(up, "gx", fwd)
    high = lax.ppermute(down, "gx", bwd)

    bricks = sx // 2 * (sy // 4) * (sz // 16)
    old = call(old_kernel, [VMEM], shape(3, bricks, 128), VMEM)(fluid_vel)
    spread = call(
        spread_kernel,
        [VMEM] * 5,
        shape(3, bricks, 128),
        VMEM,
        [pltpu.VMEM((3, sx, sy, sz), F32)],
        2,
    )(fluid_vel, from_low, from_high, from_left, from_right)
    answer, new = call(
        fluid_kernel,
        [VMEM] * 3,
        [shape(slots * 4, 128), shape(3, bricks, 128)],
        [VMEM] * 2,
        (),
        3,
    )(recv, old, spread)
    back = lax.all_to_all(answer, ("gx", "gy"), split_axis=0, concat_axis=0, tiled=True).reshape(slots, 4, 128)
    pair_scratch = [pltpu.VMEM(((blocks + 32) * 16, 128), F32), pltpu.VMEM((blocks * 16, 128), F32)]
    push, fluid = call(
        push_kernel,
        [SMEM, SMEM, VMEM, VMEM, VMEM, VMEM],
        [shape(blocks * 8, 128), shape(3, sx, sy, sz)],
        [VMEM, VMEM],
        pair_scratch,
        14,
    )(pair_self, pair_other, pos, low, high, new)

    down, up = call(
        listed_kernel,
        [SMEM, SMEM] + [VMEM] * 5,
        [shape(48, 128), shape(48, 128)],
        [VMEM] * 2,
        (),
        2,
    )(slot, halo_list, back, cell_in_brick, pos, vel, push)
    low = lax.ppermute(up, "gx", fwd)
    high = lax.ppermute(down, "gx", bwd)
    flow, pos, vel = call(
        pick_kernel,
        [SMEM] + [VMEM] * 6,
        [shape(blocks * 8, 128), shape(3, blocks, 128), shape(3, blocks, 128)],
        [VMEM] * 3,
        (),
        6,
    )(slot, back, cell_in_brick, pos, vel, push, down)
    pos, vel = call(
        last_kernel,
        [SMEM, SMEM] + [VMEM] * 5,
        [shape(3, blocks, 128), shape(3, blocks, 128)],
        [VMEM] * 2,
        [pltpu.VMEM((blocks * 8, 128), F32)] + pair_scratch,
        15,
    )(pair_self, pair_other, pos, vel, low, high, flow)
    return fluid, jnp.transpose(pos, (1, 0, 2)), jnp.transpose(vel, (1, 0, 2))


def solution(mesh):
    in_specs = (
        P(None, "gx", "gy", None),
        P(("gx", "gy"), None, None),
        P(("gx", "gy"), None, None),
        P(("gx", "gy"), None),
        P(("gx", "gy")),
        P(("gx", "gy"), None),
        P(None, ("gx", "gy")),
        P(None, ("gx", "gy")),
        P(("gx", "gy")),
    )
    out_specs = (
        P(None, "gx", "gy", None),
        P(("gx", "gy"), None, None),
        P(("gx", "gy"), None, None),
    )
    return jax.shard_map(
        per_device, mesh=mesh, in_specs=in_specs, out_specs=out_specs, check_vma=False
    )
```

```python
import functools

import jax
import jax.numpy as jnp
from jax import lax
from jax.experimental import pallas as pl
from jax.experimental.pallas import tpu as pltpu
from jax.sharding import PartitionSpec as P

F32 = jnp.float32
BF16 = jnp.bfloat16
PAIR_GROUP = 128
BLOCK_GROUP = 32
DEPOSIT_GROUP = 64
CAP = 4
EPS2 = 0.0025
VMEM = pl.BlockSpec(memory_space=pltpu.VMEM)
SMEM = pl.BlockSpec(memory_space=pltpu.SMEM)
HBM = pl.BlockSpec(memory_space=pltpu.HBM)


def split2(x):
    hi = x.astype(BF16)
    return hi, (x - hi.astype(F32)).astype(BF16)


def onehot_cells(row):
    cells = lax.broadcasted_iota(jnp.int32, (128, 128), 0)
    return (cells == jnp.broadcast_to(row, (128, 128))).astype(F32).astype(BF16)


def dot(a, b, dims=((1,), (0,))):
    return lax.dot_general(a, b, (dims, ((), ())), preferred_element_type=F32)


def swaps(n, closed):
    first = [(i, i ^ 1) for i in range(n)]
    second = [(i, (i + 1 if i % 2 else i - 1) % n) for i in range(n)]
    return first, (second if closed else second[1:-1])


def put_listed(halo, half, pos, out, at):
    for j in range(16):
        q = halo[half * 16 + j]
        for m in range(3):
            out[at + m * 16 + j : at + m * 16 + j + 1, :] = pos[m, pl.ds(q, 1), :]


def faces_kernel(side, halo, fv, pos, after, first_x, second_x, first_y, second_y):
    sx, sy, sz = fv.shape[1:]
    for out, upper in ((first_x, 1 - side[0]), (second_x, side[0])):
        x = upper * (sx - 1)
        for m in range(3):
            for h in range(2):
                out[(m * 2 + h) * 16 : (m * 2 + h + 1) * 16, :] = fv[m, x, :, h * 128 : (h + 1) * 128]
        put_listed(halo, upper, pos, out, 96)
    odd = jnp.full((sx, sz), side[1], jnp.int32) == 1
    for m in range(3):
        begin, end = fv[m, :, 0, :], fv[m, :, sy - 1, :]
        first_y[m] = jnp.where(odd, begin, end)
        second_y[m] = jnp.where(odd, end, begin)


def deposit_kernel(owner_in, local_in, cell_in, vel_in, out, slot_out, done, taken, owner, local, cell, vel, sems):
    blocks = cell.shape[0]
    copies = [
        pltpu.make_async_copy(src, dst, sems.at[i])
        for i, (src, dst) in enumerate(((vel_in, vel), (cell_in, cell), (owner_in, owner), (local_in, local)))
    ]
    for c in copies:
        c.start()
    lanes = lax.broadcasted_iota(jnp.int32, (4, 128), 1)
    rows4 = lax.broadcasted_iota(jnp.int32, (4, 128), 0)
    mark = (lanes == 127) & (rows4 == 0)
    done[...] = jnp.zeros(done.shape, F32)
    out[...] = jnp.broadcast_to(jnp.where(mark, -1.0, 0.0).astype(F32)[None], out.shape)

    def clear(t, c):
        taken[t] = 0
        return c

    lax.fori_loop(0, taken.shape[0], clear, 0, unroll=8)
    r8 = lax.broadcasted_iota(jnp.int32, (8, 128), 0)
    for c in copies:
        c.wait()

    def group(g, c):
        base = pl.multiple_of(g * DEPOSIT_GROUP, DEPOSIT_GROUP)
        cells = cell[pl.ds(base, DEPOSIT_GROUP), :]
        v = [vel[m, pl.ds(base, DEPOSIT_GROUP), :] for m in range(3)]
        for k in range(DEPOSIT_GROUP):
            q = base + k
            rows = [jnp.broadcast_to(v[m][k : k + 1, :], (8, 128)) for m in range(3)]
            load = jnp.where(r8 == 1, rows[0], jnp.where(r8 == 2, rows[1], rows[2]))
            load = jnp.where(r8 == 0, 1.0, jnp.where(r8 < 4, load, 0.0))
            hi = load.astype(BF16).astype(F32)
            lhs = jnp.concatenate([hi, load - hi], axis=0).astype(BF16)
            both = dot(lhs, onehot_cells(cells[k : k + 1, :]), ((1,), (1,)))
            both = both[0:8] + both[8:16]
            tile = owner[q]
            rank = taken[tile]
            taken[tile] = rank + 1
            slot = tile * CAP + rank
            slot_out[q] = slot
            ident = jnp.full((4, 128), local[q], jnp.int32).astype(F32)
            out[slot] = jnp.where(mark, ident, both[0:4])
        return c

    lax.fori_loop(0, blocks // DEPOSIT_GROUP, group, 0)


def swap_groups(v):
    row = lax.broadcasted_iota(jnp.int32, v.shape, 1)
    grp = lax.broadcasted_iota(jnp.int32, v.shape, 2) // 16
    for s in range(3):
        step = 1 << s
        ra, gb = (row >> s) & 1, (grp >> s) & 1
        up = pltpu.roll(pltpu.roll(v, 8 - step, 1), 16 * step, 2)
        dn = pltpu.roll(pltpu.roll(v, step, 1), 128 - 16 * step, 2)
        v = jnp.where(ra == gb, v, jnp.where(ra < gb, up, dn))
    return v


def places(sx, sy):
    return [
        (bx * 2, slice(by * 4, by * 4 + 4), slice(h * 128, h * 128 + 128))
        for bx in range(sx // 2)
        for by in range(sy // 4)
        for h in range(2)
    ]


def to_bricks(grid, m):
    tiles = [jnp.concatenate([grid[m, x, y, z], grid[m, x + 1, y, z]], axis=0) for x, y, z in places(*grid.shape[1:3])]
    return swap_groups(jnp.stack(tiles, axis=0)).reshape(len(tiles) * 8, 128)


def old_kernel(fv, bricks):
    for m in range(3):
        bricks[m] = to_bricks(fv, m)


def spread_kernel(side, fv, first_x, second_x, first_y, second_y, bricks, grid):
    sx, sy, sz = fv.shape[1:]
    odd = side[0].astype(F32)
    has_low, has_high = side[2].astype(F32), side[3].astype(F32)
    odd_y = jnp.full((sx, sz), side[1], jnp.int32) == 1
    yrow = lax.broadcasted_iota(jnp.int32, (sy, sz), 0)
    zlane = lax.broadcasted_iota(jnp.int32, (sy, sz), 1)
    for m in range(3):
        first, second = [
            jnp.concatenate([ref[(m * 2 + h) * 16 : (m * 2 + h + 1) * 16, :] for h in range(2)], axis=1)
            for ref in (first_x, second_x)
        ]
        from_low = (odd * has_low) * first + ((1.0 - odd) * has_low) * second
        from_high = ((1.0 - odd) * has_high) * first + (odd * has_high) * second
        lefts = jnp.where(odd_y, first_y[m], second_y[m])
        rights = jnp.where(odd_y, second_y[m], first_y[m])
        for x in range(sx):
            f = fv[m, x]
            high = fv[m, x + 1] if x < sx - 1 else from_high
            low = fv[m, x - 1] if x > 0 else from_low
            beside = high + low
            right = jnp.broadcast_to(rights[x : x + 1, :], (sy, sz))
            left = jnp.broadcast_to(lefts[x : x + 1, :], (sy, sz))
            beside = beside + jnp.where(yrow == sy - 1, right, pltpu.roll(f, sy - 1, 0))
            beside = beside + jnp.where(yrow == 0, left, pltpu.roll(f, 1, 0))
            beside = beside + jnp.where(zlane == sz - 1, 0.0, pltpu.roll(f, sz - 1, 1))
            beside = beside + jnp.where(zlane == 0, 0.0, pltpu.roll(f, 1, 1))
            grid[m, x] = f + 0.1 * (beside - 6.0 * f)
    for m in range(3):
        bricks[m] = to_bricks(grid, m)


def fluid_kernel(recv, old, spread, answer, new):
    slots = recv.shape[0] // 4
    bricks = old.shape[1]
    count = recv[pl.ds(0, slots, stride=4), :]
    lane = lax.broadcasted_iota(jnp.int32, (slots, 128), 1)
    ident = count[:, 127:128]
    ident_row = count.T[127:128, :]
    wide = lax.broadcasted_iota(jnp.int32, (slots, bricks), 1).astype(F32)
    by_slot = (wide == jnp.broadcast_to(ident, (slots, bricks))).astype(F32).astype(BF16)
    tall = lax.broadcasted_iota(jnp.int32, (bricks, slots), 0).astype(F32)
    by_brick = (tall == jnp.broadcast_to(ident_row, (bricks, slots))).astype(F32).astype(BF16)
    parts = [jnp.where(lane == 127, 1.0, count).astype(BF16)]
    for m in range(3):
        parts += list(split2(recv[pl.ds(m + 1, slots, stride=4), :]))
    summed = dot(by_brick, jnp.concatenate(parts, axis=1))
    cnt = summed[:, 0:128]
    momentum = [summed[:, (1 + 2 * m) * 128 : (2 + 2 * m) * 128] + summed[:, (2 + 2 * m) * 128 : (3 + 2 * m) * 128] for m in range(3)]
    last = lax.broadcasted_iota(jnp.int32, (bricks, 128), 1) == 127
    others = jnp.sum(jnp.where(last, 0.0, cnt), axis=1, keepdims=True)
    cnt = jnp.where(last, 128.0 * cnt - others, cnt)
    solid = 0.5 * cnt
    voids = 1.0 - 0.6 * solid / (1.0 + solid)
    beta = (1.0 - voids) / (voids * voids)
    scale = 0.15 * beta
    table = []
    for m in range(3):
        fluid = spread[m] + scale * (momentum[m] - cnt * old[m])
        new[m] = fluid
        table += list(split2(fluid))
    table += list(split2(beta))
    found = dot(by_slot, jnp.concatenate(table, axis=1))
    for c in range(4):
        answer[pl.ds(c, slots, stride=4), :] = (
            found[:, 2 * c * 128 : (2 * c + 1) * 128] + found[:, (2 * c + 1) * 128 : (2 * c + 2) * 128]
        )


def feature_rows(x):
    hi, lo, both = [], [], []
    for m in range(3):
        u = x[m] - 0.5
        h = u.astype(BF16).astype(F32)
        l = (u - h).astype(BF16).astype(F32)
        hi.append(h)
        lo.append(l)
        both.append(h + l)
    return hi, lo, both, both[0] * both[0] + both[1] * both[1] + both[2] * both[2]


def split3(n):
    a = n.astype(BF16).astype(F32)
    b = (n - a).astype(BF16).astype(F32)
    return a, b, n - a - b


def push_loop(step, side, first, second, pos, listed, at, push, feat_b, feat_a):
    blocks = pos.shape[1]
    one = jnp.ones((8, 128), F32)
    zero = jnp.zeros((8, 128), F32)

    def put(ref, q0, feats):
        for k, v in enumerate(feats):
            ref[pl.ds(q0 * 16 + k, 8, stride=16), :] = v

    def own(g, c):
        q0 = pl.multiple_of(g * 8, 8)
        hi, lo, both, norm = feature_rows([pos[m, pl.ds(q0, 8), :] for m in range(3)])
        n = split3(norm)
        put(feat_b, q0, hi + [one, n[0], n[1], n[2], one] + lo + [one, zero, zero, zero, zero])
        n = split3(norm + EPS2)
        h2, l2 = [-2.0 * v for v in hi], [-2.0 * v for v in lo]
        put(feat_a, q0, h2 + [n[0], one, one, one, n[1]] + l2 + [n[2], zero, zero, zero, zero])
        return c

    lax.fori_loop(0, blocks // 8, own, 0, unroll=2)
    for ref, upper in zip(listed, (1 - side[0], side[0])):
        for g in range(2):
            hi, lo, _, norm = feature_rows([ref[at + m * 16 + g * 8 : at + m * 16 + g * 8 + 8, :] for m in range(3)])
            n = split3(norm)
            put(feat_b, pl.multiple_of(blocks + upper * 16 + g * 8, 8), hi + [one, n[0], n[1], n[2], one] + lo + [one, zero, zero, zero, zero])
    push[...] = jnp.zeros(push.shape, F32)
    top = lax.broadcasted_iota(jnp.int32, (8, 128), 0) < 3

    def one_pair(p):
        a = first[step, p]
        b = second[step, p]
        fb = feat_b[pl.ds(pl.multiple_of(b * 16, 16), 16), :]
        fa = feat_a[pl.ds(pl.multiple_of(a * 16, 16), 16), :]
        x, y = fa[0:8], fa[8:16]
        z = jnp.where(top, y, 0.0)
        ga = jnp.concatenate([x, jnp.where(top, x, y), z, z], axis=0).astype(BF16)
        lhs = fb.astype(BF16)
        r2 = dot(jnp.concatenate([lhs, lhs], axis=0), ga, ((0,), (0,)))
        w = jnp.maximum(lax.rsqrt(jnp.maximum(r2, EPS2)) - 4.0, 0.0)
        res = dot(jnp.concatenate([lhs, lhs], axis=1), jnp.concatenate(split2(w), axis=0))
        total = jnp.broadcast_to(res[3:4], (8, 128))
        return a, (-0.5) * (x + z) * total - (res[0:8] + res[8:16])

    def pairs(g, c):
        done = [one_pair(g * PAIR_GROUP + k) for k in range(PAIR_GROUP)]
        for a, f in done:
            rows = pl.ds(pl.multiple_of(a * 8, 8), 8)
            push[rows, :] = push[rows, :] + f
        return c

    lax.fori_loop(0, first.shape[1] // PAIR_GROUP, pairs, 0)


def push_kernel(side, first, second, slot, pos, listed_a, listed_b, new, push, fluid, slot_out, feat_b, feat_a):
    def hand_on(q, c):
        slot_out[q] = slot[q]
        return c

    lax.fori_loop(0, slot.shape[0], hand_on, 0, unroll=8)
    for m in range(3):
        moved = swap_groups(new[m].reshape(new.shape[1] // 8, 8, 128))
        for i, (x, y, z) in enumerate(places(*fluid.shape[1:3])):
            fluid[m, x, y, z] = moved[i, 0:4]
            fluid[m, x + 1, y, z] = moved[i, 4:8]
    push_loop(0, side, first, second, pos, (listed_a, listed_b), 96, push, feat_b, feat_a)


def advance(pos, vel, push, flow, pos_out, vel_out):
    blocks = pos.shape[1]
    drift = 2.0 * flow[pl.ds(3, blocks, stride=8), :]
    for m in range(3):
        v = vel[m]
        force = 2.5 * push[pl.ds(m, blocks, stride=8), :] + drift * (flow[pl.ds(m, blocks, stride=8), :] - v)
        if m == 2:
            force = force - 1.0
        v = v + 0.1 * force
        vel_out[m] = v
        pos_out[m] = pos[m] + 0.1 * v


def pick(hot, v):
    v = jnp.concatenate([v, v], axis=0)
    hi = v.astype(BF16).astype(F32)
    both = dot(jnp.concatenate([hi, v - hi], axis=0).astype(BF16), hot)
    return both[0:8] + both[8:16]


def listed_kernel(side, slot, halo, back, cell, pos, vel, push, first_out, second_out):
    r8 = lax.broadcasted_iota(jnp.int32, (8, 128), 0)

    def tile(ref, q):
        rows = [jnp.broadcast_to(ref[m, pl.ds(q, 1), :], (8, 128)) for m in range(3)]
        return jnp.where(r8 == 0, rows[0], jnp.where(r8 == 1, rows[1], rows[2]))

    for out, upper in ((first_out, 1 - side[0]), (second_out, side[0])):
        for j in range(16):
            q = halo[upper * 16 + j]
            flow = pick(onehot_cells(cell[pl.ds(q, 1), :]), back[slot[q]])
            v = tile(vel, q)
            rows = pl.ds(pl.multiple_of(q * 8, 8), 8)
            drift = 2.0 * jnp.broadcast_to(flow[3:4], (8, 128))
            force = 2.5 * push[rows, :] + drift * (flow - v)
            v = v + 0.1 * jnp.where(r8 == 2, force - 1.0, force)
            x = tile(pos, q) + 0.1 * v
            for m in range(3):
                out[m * 16 + j : m * 16 + j + 1, :] = x[m : m + 1, :]


def pick_kernel(slot, back, cell, pos, vel, push, after, flow, pos_out, vel_out):
    def group(g, c):
        base = pl.multiple_of(g * BLOCK_GROUP, BLOCK_GROUP)
        cells = cell[pl.ds(base, BLOCK_GROUP), :]
        for k in range(BLOCK_GROUP):
            q = base + k
            flow[pl.ds(pl.multiple_of(q * 8, 8), 8), :] = pick(onehot_cells(cells[k : k + 1, :]), back[slot[q]])
        return c

    lax.fori_loop(0, cell.shape[0] // BLOCK_GROUP, group, 0)
    advance(pos, vel, push, flow, pos_out, vel_out)


def last_kernel(side, first, second, pos, vel, listed_a, listed_b, flow, pos_out, vel_out, push, feat_b, feat_a):
    push_loop(1, side, first, second, pos, (listed_a, listed_b), 0, push, feat_b, feat_a)
    advance(pos, vel, push, flow, pos_out, vel_out)


def call(kernel, in_specs, out_shape, out_specs, scratch=(), micros=1, vmem=20 * 1024 * 1024):
    return pl.pallas_call(
        kernel,
        in_specs=in_specs,
        out_shape=out_shape,
        out_specs=out_specs,
        scratch_shapes=list(scratch),
        compiler_params=pltpu.CompilerParams(vmem_limit_bytes=vmem),
        cost_estimate=pl.CostEstimate(flops=micros * 1_000_000_000, bytes_accessed=micros * 3_000_000, transcendentals=0),
    )


def shape(*dims, dtype=F32):
    return jax.ShapeDtypeStruct(dims, dtype)


def per_device(
    fluid_vel,
    part_pos,
    part_vel,
    brick_owner,
    brick_local,
    cell_in_brick,
    pair_self,
    pair_other,
    halo_list,
):
    nx, ny = lax.axis_size("gx"), lax.axis_size("gy")
    tiles = nx * ny
    blocks = part_pos.shape[0]
    slots = tiles * CAP
    sx, sy, sz = fluid_vel.shape[1:]
    pos = jnp.transpose(part_pos, (1, 0, 2))
    vel = jnp.transpose(part_vel, (1, 0, 2))

    send, slot, placed = call(
        deposit_kernel,
        [HBM] * 4,
        [shape(slots, 4, 128), shape(blocks, dtype=jnp.int32), shape(8, 128)],
        [VMEM, SMEM, VMEM],
        [
            pltpu.SMEM((tiles,), jnp.int32),
            pltpu.SMEM((blocks,), jnp.int32),
            pltpu.SMEM((blocks,), jnp.int32),
            pltpu.VMEM((blocks, 128), jnp.int32),
            pltpu.VMEM((3, blocks, 128), F32),
            pltpu.SemaphoreType.DMA((4,)),
        ],
        7,
        63_000_000,
    )(brick_owner[:, 0], brick_local, cell_in_brick, vel)
    recv = lax.all_to_all(send.reshape(slots * 4, 128), ("gx", "gy"), split_axis=0, concat_axis=0, tiled=True)

    me_x, me_y = lax.axis_index("gx"), lax.axis_index("gy")
    side = jnp.stack([me_x % 2, me_y % 2, me_x > 0, me_x < nx - 1]).astype(jnp.int32)
    first_x, second_x, first_y, second_y = call(
        faces_kernel,
        [SMEM, SMEM, VMEM, VMEM, VMEM],
        [shape(144, 128), shape(144, 128), shape(3, sx, sz), shape(3, sx, sz)],
        [VMEM] * 4,
    )(side, halo_list, fluid_vel, pos, placed)
    perms_x, perms_y = swaps(nx, True), swaps(ny, False)
    first_x = lax.ppermute(first_x, "gx", perms_x[0])
    second_x = lax.ppermute(second_x, "gx", perms_x[1])
    first_y = lax.ppermute(first_y, "gy", perms_y[0])
    second_y = lax.ppermute(second_y, "gy", perms_y[1])

    bricks = sx // 2 * (sy // 4) * (sz // 16)
    old = call(old_kernel, [VMEM], shape(3, bricks, 128), VMEM)(fluid_vel)
    spread = call(
        spread_kernel,
        [SMEM] + [VMEM] * 5,
        shape(3, bricks, 128),
        VMEM,
        [pltpu.VMEM((3, sx, sy, sz), F32)],
        2,
    )(side, fluid_vel, first_x, second_x, first_y, second_y)
    answer, new = call(
        fluid_kernel,
        [VMEM] * 3,
        [shape(slots * 4, 128), shape(3, bricks, 128)],
        [VMEM] * 2,
        (),
        3,
    )(recv, old, spread)
    back = lax.all_to_all(answer, ("gx", "gy"), split_axis=0, concat_axis=0, tiled=True).reshape(slots, 4, 128)
    pair_scratch = [pltpu.VMEM(((blocks + 32) * 16, 128), F32), pltpu.VMEM((blocks * 16, 128), F32)]
    push, fluid, slot = call(
        push_kernel,
        [SMEM] * 4 + [VMEM] * 4,
        [shape(blocks * 8, 128), shape(3, sx, sy, sz), shape(blocks, dtype=jnp.int32)],
        [VMEM, VMEM, SMEM],
        pair_scratch,
        14,
    )(side, pair_self, pair_other, slot, pos, first_x, second_x, new)

    first, second = call(
        listed_kernel,
        [SMEM] * 3 + [VMEM] * 5,
        [shape(48, 128), shape(48, 128)],
        [VMEM] * 2,
        (),
        2,
    )(side, slot, halo_list, back, cell_in_brick, pos, vel, push)
    listed_a = lax.ppermute(first, "gx", perms_x[0])
    listed_b = lax.ppermute(second, "gx", perms_x[1])
    flow, pos, vel = call(
        pick_kernel,
        [SMEM] + [VMEM] * 6,
        [shape(blocks * 8, 128), shape(3, blocks, 128), shape(3, blocks, 128)],
        [VMEM] * 3,
        (),
        6,
    )(slot, back, cell_in_brick, pos, vel, push, first)
    pos, vel = call(
        last_kernel,
        [SMEM] * 3 + [VMEM] * 5,
        [shape(3, blocks, 128), shape(3, blocks, 128)],
        [VMEM] * 2,
        [pltpu.VMEM((blocks * 8, 128), F32)] + pair_scratch,
        15,
    )(side, pair_self, pair_other, pos, vel, listed_a, listed_b, flow)
    return fluid, jnp.transpose(pos, (1, 0, 2)), jnp.transpose(vel, (1, 0, 2))


def solution(mesh):
    in_specs = (
        P(None, "gx", "gy", None),
        P(("gx", "gy"), None, None),
        P(("gx", "gy"), None, None),
        P(("gx", "gy"), None),
        P(("gx", "gy")),
        P(("gx", "gy"), None),
        P(None, ("gx", "gy")),
        P(None, ("gx", "gy")),
        P(("gx", "gy")),
    )
    out_specs = (
        P(None, "gx", "gy", None),
        P(("gx", "gy"), None, None),
        P(("gx", "gy"), None, None),
    )
    return jax.shard_map(
        per_device, mesh=mesh, in_specs=in_specs, out_specs=out_specs, check_vma=False
    )
```

```python
import functools

import jax
import jax.numpy as jnp
from jax import lax
from jax.experimental import pallas as pl
from jax.experimental.pallas import tpu as pltpu
from jax.sharding import PartitionSpec as P

F32 = jnp.float32
BF16 = jnp.bfloat16
PAIR_GROUP = 128
BLOCK_GROUP = 32
DEPOSIT_GROUP = 128
CAP = 4
EPS2 = 0.0025
VMEM = pl.BlockSpec(memory_space=pltpu.VMEM)
SMEM = pl.BlockSpec(memory_space=pltpu.SMEM)
HBM = pl.BlockSpec(memory_space=pltpu.HBM)


def split2(x):
    hi = x.astype(BF16)
    return hi, (x - hi.astype(F32)).astype(BF16)


def onehot_cells(row):
    cells = lax.broadcasted_iota(jnp.int32, (128, 128), 0)
    return (cells == jnp.broadcast_to(row, (128, 128))).astype(F32).astype(BF16)


def dot(a, b, dims=((1,), (0,))):
    return lax.dot_general(a, b, (dims, ((), ())), preferred_element_type=F32)


def swaps(n, closed):
    first = [(i, i ^ 1) for i in range(n)]
    second = [(i, (i + 1 if i % 2 else i - 1) % n) for i in range(n)]
    return first, (second if closed else second[1:-1])


def put_listed(halo, half, pos, out, at):
    for j in range(16):
        q = halo[half * 16 + j]
        for m in range(3):
            out[at + m * 16 + j : at + m * 16 + j + 1, :] = pos[m, pl.ds(q, 1), :]


def faces_kernel(side, halo, fv, pos, after, first_x, second_x, first_y, second_y):
    sx, sy, sz = fv.shape[1:]
    for out, upper in ((first_x, 1 - side[0]), (second_x, side[0])):
        x = upper * (sx - 1)
        for m in range(3):
            for h in range(2):
                out[(m * 2 + h) * 16 : (m * 2 + h + 1) * 16, :] = fv[m, x, :, h * 128 : (h + 1) * 128]
        put_listed(halo, upper, pos, out, 96)
    odd = jnp.full((sx, sz), side[1], jnp.int32) == 1
    for m in range(3):
        begin, end = fv[m, :, 0, :], fv[m, :, sy - 1, :]
        first_y[m] = jnp.where(odd, begin, end)
        second_y[m] = jnp.where(odd, end, begin)


def deposit_kernel(owner_in, local_in, cell_in, vel_in, out, slot_out, done, taken, owner, local, cell, vel, sems):
    blocks = cell.shape[0]
    copies = [
        pltpu.make_async_copy(src, dst, sems.at[i])
        for i, (src, dst) in enumerate(((vel_in, vel), (cell_in, cell), (owner_in, owner), (local_in, local)))
    ]
    for c in copies:
        c.start()
    lanes = lax.broadcasted_iota(jnp.int32, (4, 128), 1)
    rows4 = lax.broadcasted_iota(jnp.int32, (4, 128), 0)
    mark = (lanes == 127) & (rows4 == 0)
    done[...] = jnp.zeros(done.shape, F32)
    out[...] = jnp.broadcast_to(jnp.where(mark, -1.0, 0.0).astype(F32)[None], out.shape)

    def clear(t, c):
        taken[t] = 0
        return c

    lax.fori_loop(0, taken.shape[0], clear, 0, unroll=8)
    r8 = lax.broadcasted_iota(jnp.int32, (8, 128), 0)
    lane16 = lax.broadcasted_iota(jnp.int32, (128, 128), 1) // 16
    for c in copies:
        c.wait()

    def group(g, c):
        base = pl.multiple_of(g * DEPOSIT_GROUP, DEPOSIT_GROUP)
        cells = cell[pl.ds(base, DEPOSIT_GROUP), :]
        v = [vel[m, pl.ds(base, DEPOSIT_GROUP), :] for m in range(3)]
        for start in range(0, DEPOSIT_GROUP, 8):
            loads, hots = [], []
            for k in range(start, start + 8):
                rows = [jnp.broadcast_to(v[m][k : k + 1, :], (8, 128)) for m in range(3)]
                load = jnp.where(r8 == 1, rows[0], jnp.where(r8 == 2, rows[1], rows[2]))
                load = jnp.where(r8 == 0, 1.0, jnp.where(r8 < 4, load, 0.0))
                hi = load.astype(BF16).astype(F32)
                loads += [hi, load - hi]
                hots.append(onehot_cells(cells[k : k + 1, :]))
            turned = jnp.concatenate(loads, axis=0).T
            turned = turned.astype(BF16)
            apart = [jnp.where(lane16 == k, turned, jnp.zeros_like(turned)) for k in range(8)]
            found = dot(jnp.concatenate(hots, axis=1), jnp.concatenate(apart, axis=0)).T
            for k in range(8):
                q = base + start + k
                both = found[k * 16 : k * 16 + 8] + found[k * 16 + 8 : k * 16 + 16]
                tile = owner[q]
                rank = taken[tile]
                taken[tile] = rank + 1
                slot = tile * CAP + rank
                slot_out[q] = slot
                ident = jnp.full((4, 128), local[q], jnp.int32).astype(F32)
                out[slot] = jnp.where(mark, ident, both[0:4])
        return c

    lax.fori_loop(0, blocks // DEPOSIT_GROUP, group, 0)


def swap_groups(v):
    row = lax.broadcasted_iota(jnp.int32, v.shape, 1)
    grp = lax.broadcasted_iota(jnp.int32, v.shape, 2) // 16
    for s in range(3):
        step = 1 << s
        ra, gb = (row >> s) & 1, (grp >> s) & 1
        up = pltpu.roll(pltpu.roll(v, 8 - step, 1), 16 * step, 2)
        dn = pltpu.roll(pltpu.roll(v, step, 1), 128 - 16 * step, 2)
        v = jnp.where(ra == gb, v, jnp.where(ra < gb, up, dn))
    return v


def places(sx, sy):
    return [
        (bx * 2, slice(by * 4, by * 4 + 4), slice(h * 128, h * 128 + 128))
        for bx in range(sx // 2)
        for by in range(sy // 4)
        for h in range(2)
    ]


def to_bricks(grid, m):
    tiles = [jnp.concatenate([grid[m, x, y, z], grid[m, x + 1, y, z]], axis=0) for x, y, z in places(*grid.shape[1:3])]
    return swap_groups(jnp.stack(tiles, axis=0)).reshape(len(tiles) * 8, 128)


def old_kernel(fv, bricks):
    for m in range(3):
        bricks[m] = to_bricks(fv, m)


def spread_kernel(side, fv, first_x, second_x, first_y, second_y, bricks, grid):
    sx, sy, sz = fv.shape[1:]
    odd = side[0].astype(F32)
    has_low, has_high = side[2].astype(F32), side[3].astype(F32)
    odd_y = jnp.full((sx, sz), side[1], jnp.int32) == 1
    yrow = lax.broadcasted_iota(jnp.int32, (sy, sz), 0)
    zlane = lax.broadcasted_iota(jnp.int32, (sy, sz), 1)
    for m in range(3):
        first, second = [
            jnp.concatenate([ref[(m * 2 + h) * 16 : (m * 2 + h + 1) * 16, :] for h in range(2)], axis=1)
            for ref in (first_x, second_x)
        ]
        from_low = (odd * has_low) * first + ((1.0 - odd) * has_low) * second
        from_high = ((1.0 - odd) * has_high) * first + (odd * has_high) * second
        lefts = jnp.where(odd_y, first_y[m], second_y[m])
        rights = jnp.where(odd_y, second_y[m], first_y[m])
        for x in range(sx):
            f = fv[m, x]
            high = fv[m, x + 1] if x < sx - 1 else from_high
            low = fv[m, x - 1] if x > 0 else from_low
            beside = high + low
            right = jnp.broadcast_to(rights[x : x + 1, :], (sy, sz))
            left = jnp.broadcast_to(lefts[x : x + 1, :], (sy, sz))
            beside = beside + jnp.where(yrow == sy - 1, right, pltpu.roll(f, sy - 1, 0))
            beside = beside + jnp.where(yrow == 0, left, pltpu.roll(f, 1, 0))
            beside = beside + jnp.where(zlane == sz - 1, 0.0, pltpu.roll(f, sz - 1, 1))
            beside = beside + jnp.where(zlane == 0, 0.0, pltpu.roll(f, 1, 1))
            grid[m, x] = f + 0.1 * (beside - 6.0 * f)
    for m in range(3):
        bricks[m] = to_bricks(grid, m)


def fluid_kernel(recv, old, spread, answer, fluid, done):
    done[...] = jnp.zeros(done.shape, F32)
    slots = recv.shape[0] // 4
    bricks = old.shape[1]
    count = recv[pl.ds(0, slots, stride=4), :]
    lane = lax.broadcasted_iota(jnp.int32, (slots, 128), 1)
    ident = count[:, 127:128]
    ident_row = count.T[127:128, :]
    wide = lax.broadcasted_iota(jnp.int32, (slots, bricks), 1).astype(F32)
    by_slot = (wide == jnp.broadcast_to(ident, (slots, bricks))).astype(F32).astype(BF16)
    tall = lax.broadcasted_iota(jnp.int32, (bricks, slots), 0).astype(F32)
    by_brick = (tall == jnp.broadcast_to(ident_row, (bricks, slots))).astype(F32).astype(BF16)
    parts = [jnp.where(lane == 127, 1.0, count).astype(BF16)]
    for m in range(3):
        parts += list(split2(recv[pl.ds(m + 1, slots, stride=4), :]))
    summed = dot(by_brick, jnp.concatenate(parts, axis=1))
    cnt = summed[:, 0:128]
    momentum = [summed[:, (1 + 2 * m) * 128 : (2 + 2 * m) * 128] + summed[:, (2 + 2 * m) * 128 : (3 + 2 * m) * 128] for m in range(3)]
    last = lax.broadcasted_iota(jnp.int32, (bricks, 128), 1) == 127
    others = jnp.sum(jnp.where(last, 0.0, cnt), axis=1, keepdims=True)
    cnt = jnp.where(last, 128.0 * cnt - others, cnt)
    solid = 0.5 * cnt
    voids = 1.0 - 0.6 * solid / (1.0 + solid)
    beta = (1.0 - voids) / (voids * voids)
    scale = 0.15 * beta
    table = []
    for m in range(3):
        new = spread[m] + scale * (momentum[m] - cnt * old[m])
        table += list(split2(new))
        moved = swap_groups(new.reshape(bricks // 8, 8, 128))
        for i, (x, y, z) in enumerate(places(*fluid.shape[1:3])):
            fluid[m, x, y, z] = moved[i, 0:4]
            fluid[m, x + 1, y, z] = moved[i, 4:8]
    table += list(split2(beta))
    found = dot(by_slot, jnp.concatenate(table, axis=1))
    for c in range(4):
        answer[pl.ds(c, slots, stride=4), :] = (
            found[:, 2 * c * 128 : (2 * c + 1) * 128] + found[:, (2 * c + 1) * 128 : (2 * c + 2) * 128]
        )


def feature_rows(x):
    hi, lo, both = [], [], []
    for m in range(3):
        u = x[m] - 0.5
        h = u.astype(BF16).astype(F32)
        l = (u - h).astype(BF16).astype(F32)
        hi.append(h)
        lo.append(l)
        both.append(h + l)
    return hi, lo, both, both[0] * both[0] + both[1] * both[1] + both[2] * both[2]


def split3(n):
    a = n.astype(BF16).astype(F32)
    b = (n - a).astype(BF16).astype(F32)
    return a, b, n - a - b


def push_loop(step, side, first, second, pos, listed, at, push, feat_b, feat_a):
    blocks = pos.shape[1]
    one = jnp.ones((8, 128), F32)
    zero = jnp.zeros((8, 128), F32)

    def put(ref, q0, feats):
        for k, v in enumerate(feats):
            ref[pl.ds(q0 * 16 + k, 8, stride=16), :] = v

    def own(g, c):
        q0 = pl.multiple_of(g * 8, 8)
        hi, lo, both, norm = feature_rows([pos[m, pl.ds(q0, 8), :] for m in range(3)])
        n = split3(norm)
        put(feat_b, q0, hi + [one, n[0], n[1], n[2], one] + lo + [one, zero, zero, zero, zero])
        n = split3(norm + EPS2)
        h2, l2 = [-2.0 * v for v in hi], [-2.0 * v for v in lo]
        put(feat_a, q0, h2 + [n[0], one, one, one, n[1]] + l2 + [n[2], zero, zero, zero, zero])
        return c

    lax.fori_loop(0, blocks // 8, own, 0, unroll=2)
    for ref, upper in zip(listed, (1 - side[0], side[0])):
        for g in range(2):
            hi, lo, _, norm = feature_rows([ref[at + m * 16 + g * 8 : at + m * 16 + g * 8 + 8, :] for m in range(3)])
            n = split3(norm)
            put(feat_b, pl.multiple_of(blocks + upper * 16 + g * 8, 8), hi + [one, n[0], n[1], n[2], one] + lo + [one, zero, zero, zero, zero])
    push[...] = jnp.zeros(push.shape, F32)
    top = lax.broadcasted_iota(jnp.int32, (8, 128), 0) < 3

    def one_pair(p):
        a = first[step, p]
        b = second[step, p]
        fb = feat_b[pl.ds(pl.multiple_of(b * 16, 16), 16), :]
        fa = feat_a[pl.ds(pl.multiple_of(a * 16, 16), 16), :]
        x, y = fa[0:8], fa[8:16]
        z = jnp.where(top, y, 0.0)
        ga = jnp.concatenate([x, jnp.where(top, x, y), z, z], axis=0).astype(BF16)
        lhs = fb.astype(BF16)
        r2 = dot(jnp.concatenate([lhs, lhs], axis=0), ga, ((0,), (0,)))
        w = jnp.maximum(lax.rsqrt(jnp.maximum(r2, EPS2)) - 4.0, 0.0)
        res = dot(jnp.concatenate([lhs, lhs], axis=1), jnp.concatenate(split2(w), axis=0))
        total = jnp.broadcast_to(res[3:4], (8, 128))
        return a, (-0.5) * (x + z) * total - (res[0:8] + res[8:16])

    def pairs(g, c):
        done = [one_pair(g * PAIR_GROUP + k) for k in range(PAIR_GROUP)]
        for a, f in done:
            rows = pl.ds(pl.multiple_of(a * 8, 8), 8)
            push[rows, :] = push[rows, :] + f
        return c

    lax.fori_loop(0, first.shape[1] // PAIR_GROUP, pairs, 0)


def push_kernel(side, first, second, slot, pos, listed_a, listed_b, after, push, slot_out, feat_b, feat_a):
    def hand_on(q, c):
        slot_out[q] = slot[q]
        return c

    lax.fori_loop(0, slot.shape[0], hand_on, 0, unroll=8)
    push_loop(0, side, first, second, pos, (listed_a, listed_b), 96, push, feat_b, feat_a)


def advance(pos, vel, push, flow, pos_out, vel_out):
    blocks = pos.shape[1]
    drift = 2.0 * flow[pl.ds(3, blocks, stride=8), :]
    for m in range(3):
        v = vel[m]
        force = 2.5 * push[pl.ds(m, blocks, stride=8), :] + drift * (flow[pl.ds(m, blocks, stride=8), :] - v)
        if m == 2:
            force = force - 1.0
        v = v + 0.1 * force
        vel_out[m] = v
        pos_out[m] = pos[m] + 0.1 * v


def pick(hot, v):
    v = jnp.concatenate([v, v], axis=0)
    hi = v.astype(BF16).astype(F32)
    both = dot(jnp.concatenate([hi, v - hi], axis=0).astype(BF16), hot)
    return both[0:8] + both[8:16]


def listed_kernel(side, slot, halo, back, cell, pos, vel, push, first_out, second_out):
    r8 = lax.broadcasted_iota(jnp.int32, (8, 128), 0)

    def tile(ref, q):
        rows = [jnp.broadcast_to(ref[m, pl.ds(q, 1), :], (8, 128)) for m in range(3)]
        return jnp.where(r8 == 0, rows[0], jnp.where(r8 == 1, rows[1], rows[2]))

    for out, upper in ((first_out, 1 - side[0]), (second_out, side[0])):
        for j in range(16):
            q = halo[upper * 16 + j]
            flow = pick(onehot_cells(cell[pl.ds(q, 1), :]), back[slot[q]])
            v = tile(vel, q)
            rows = pl.ds(pl.multiple_of(q * 8, 8), 8)
            drift = 2.0 * jnp.broadcast_to(flow[3:4], (8, 128))
            force = 2.5 * push[rows, :] + drift * (flow - v)
            v = v + 0.1 * jnp.where(r8 == 2, force - 1.0, force)
            x = tile(pos, q) + 0.1 * v
            for m in range(3):
                out[m * 16 + j : m * 16 + j + 1, :] = x[m : m + 1, :]


def pick_kernel(slot, back, cell, pos, vel, push, after, flow, pos_out, vel_out):
    def group(g, c):
        base = pl.multiple_of(g * BLOCK_GROUP, BLOCK_GROUP)
        cells = cell[pl.ds(base, BLOCK_GROUP), :]
        for k in range(BLOCK_GROUP):
            q = base + k
            flow[pl.ds(pl.multiple_of(q * 8, 8), 8), :] = pick(onehot_cells(cells[k : k + 1, :]), back[slot[q]])
        return c

    lax.fori_loop(0, cell.shape[0] // BLOCK_GROUP, group, 0)
    advance(pos, vel, push, flow, pos_out, vel_out)


def last_kernel(side, first, second, pos, vel, listed_a, listed_b, flow, pos_out, vel_out, push, feat_b, feat_a):
    push_loop(1, side, first, second, pos, (listed_a, listed_b), 0, push, feat_b, feat_a)
    advance(pos, vel, push, flow, pos_out, vel_out)


def call(kernel, in_specs, out_shape, out_specs, scratch=(), micros=1, vmem=20 * 1024 * 1024):
    return pl.pallas_call(
        kernel,
        in_specs=in_specs,
        out_shape=out_shape,
        out_specs=out_specs,
        scratch_shapes=list(scratch),
        compiler_params=pltpu.CompilerParams(vmem_limit_bytes=vmem),
        cost_estimate=pl.CostEstimate(flops=micros * 1_000_000_000, bytes_accessed=micros * 3_000_000, transcendentals=0),
    )


def shape(*dims, dtype=F32):
    return jax.ShapeDtypeStruct(dims, dtype)


def per_device(
    fluid_vel,
    part_pos,
    part_vel,
    brick_owner,
    brick_local,
    cell_in_brick,
    pair_self,
    pair_other,
    halo_list,
):
    nx, ny = lax.axis_size("gx"), lax.axis_size("gy")
    tiles = nx * ny
    blocks = part_pos.shape[0]
    slots = tiles * CAP
    sx, sy, sz = fluid_vel.shape[1:]
    pos = jnp.transpose(part_pos, (1, 0, 2))
    vel = jnp.transpose(part_vel, (1, 0, 2))

    send, slot, placed = call(
        deposit_kernel,
        [HBM] * 4,
        [shape(slots, 4, 128), shape(blocks, dtype=jnp.int32), shape(8, 128)],
        [VMEM, SMEM, VMEM],
        [
            pltpu.SMEM((tiles,), jnp.int32),
            pltpu.SMEM((blocks,), jnp.int32),
            pltpu.SMEM((blocks,), jnp.int32),
            pltpu.VMEM((blocks, 128), jnp.int32),
            pltpu.VMEM((3, blocks, 128), F32),
            pltpu.SemaphoreType.DMA((4,)),
        ],
        7,
        63_000_000,
    )(brick_owner[:, 0], brick_local, cell_in_brick, vel)
    recv = lax.all_to_all(send.reshape(slots * 4, 128), ("gx", "gy"), split_axis=0, concat_axis=0, tiled=True)

    me_x, me_y = lax.axis_index("gx"), lax.axis_index("gy")
    side = jnp.stack([me_x % 2, me_y % 2, me_x > 0, me_x < nx - 1]).astype(jnp.int32)
    first_x, second_x, first_y, second_y = call(
        faces_kernel,
        [SMEM, SMEM, VMEM, VMEM, VMEM],
        [shape(144, 128), shape(144, 128), shape(3, sx, sz), shape(3, sx, sz)],
        [VMEM] * 4,
    )(side, halo_list, fluid_vel, pos, placed)
    perms_x, perms_y = swaps(nx, True), swaps(ny, False)
    first_x = lax.ppermute(first_x, "gx", perms_x[0])
    second_x = lax.ppermute(second_x, "gx", perms_x[1])
    first_y = lax.ppermute(first_y, "gy", perms_y[0])
    second_y = lax.ppermute(second_y, "gy", perms_y[1])

    bricks = sx // 2 * (sy // 4) * (sz // 16)
    old = call(old_kernel, [VMEM], shape(3, bricks, 128), VMEM)(fluid_vel)
    spread = call(
        spread_kernel,
        [SMEM] + [VMEM] * 5,
        shape(3, bricks, 128),
        VMEM,
        [pltpu.VMEM((3, sx, sy, sz), F32)],
        2,
    )(side, fluid_vel, first_x, second_x, first_y, second_y)
    answer, fluid, stepped = call(
        fluid_kernel,
        [VMEM] * 3,
        [shape(slots * 4, 128), shape(3, sx, sy, sz), shape(8, 128)],
        [VMEM] * 3,
        (),
        3,
    )(recv, old, spread)
    back = lax.all_to_all(answer, ("gx", "gy"), split_axis=0, concat_axis=0, tiled=True).reshape(slots, 4, 128)
    pair_scratch = [pltpu.VMEM(((blocks + 32) * 16, 128), F32), pltpu.VMEM((blocks * 16, 128), F32)]
    push, slot = call(
        push_kernel,
        [SMEM] * 4 + [VMEM] * 4,
        [shape(blocks * 8, 128), shape(blocks, dtype=jnp.int32)],
        [VMEM, SMEM],
        pair_scratch,
        14,
    )(side, pair_self, pair_other, slot, pos, first_x, second_x, stepped)

    first, second = call(
        listed_kernel,
        [SMEM] * 3 + [VMEM] * 5,
        [shape(48, 128), shape(48, 128)],
        [VMEM] * 2,
        (),
        2,
    )(side, slot, halo_list, back, cell_in_brick, pos, vel, push)
    listed_a = lax.ppermute(first, "gx", perms_x[0])
    listed_b = lax.ppermute(second, "gx", perms_x[1])
    flow, pos, vel = call(
        pick_kernel,
        [SMEM] + [VMEM] * 6,
        [shape(blocks * 8, 128), shape(3, blocks, 128), shape(3, blocks, 128)],
        [VMEM] * 3,
        (),
        6,
    )(slot, back, cell_in_brick, pos, vel, push, first)
    pos, vel = call(
        last_kernel,
        [SMEM] * 3 + [VMEM] * 5,
        [shape(3, blocks, 128), shape(3, blocks, 128)],
        [VMEM] * 2,
        [pltpu.VMEM((blocks * 8, 128), F32)] + pair_scratch,
        15,
    )(side, pair_self, pair_other, pos, vel, listed_a, listed_b, flow)
    return fluid, jnp.transpose(pos, (1, 0, 2)), jnp.transpose(vel, (1, 0, 2))


def solution(mesh):
    in_specs = (
        P(None, "gx", "gy", None),
        P(("gx", "gy"), None, None),
        P(("gx", "gy"), None, None),
        P(("gx", "gy"), None),
        P(("gx", "gy")),
        P(("gx", "gy"), None),
        P(None, ("gx", "gy")),
        P(None, ("gx", "gy")),
        P(("gx", "gy")),
    )
    out_specs = (
        P(None, "gx", "gy", None),
        P(("gx", "gy"), None, None),
        P(("gx", "gy"), None, None),
    )
    return jax.shard_map(
        per_device, mesh=mesh, in_specs=in_specs, out_specs=out_specs, check_vma=False
    )
```

```python
import functools

import jax
import jax.numpy as jnp
from jax import lax
from jax.experimental import pallas as pl
from jax.experimental.pallas import tpu as pltpu
from jax.sharding import PartitionSpec as P

F32 = jnp.float32
BF16 = jnp.bfloat16
PAIR_GROUP = 256
BLOCK_GROUP = 128
DEPOSIT_GROUP = 128
CAP = 4
EPS2 = 0.0025
VMEM = pl.BlockSpec(memory_space=pltpu.VMEM)
SMEM = pl.BlockSpec(memory_space=pltpu.SMEM)
HBM = pl.BlockSpec(memory_space=pltpu.HBM)


def split2(x):
    hi = x.astype(BF16)
    return hi, (x - hi.astype(F32)).astype(BF16)


def onehot_cells(row):
    cells = lax.broadcasted_iota(jnp.int32, (128, 128), 0)
    return (cells == jnp.broadcast_to(row, (128, 128))).astype(F32).astype(BF16)


def dot(a, b, dims=((1,), (0,))):
    return lax.dot_general(a, b, (dims, ((), ())), preferred_element_type=F32)


def swaps(n, closed):
    first = [(i, i ^ 1) for i in range(n)]
    second = [(i, (i + 1 if i % 2 else i - 1) % n) for i in range(n)]
    return first, (second if closed else second[1:-1])


def put_listed(halo, half, pos, out, at):
    for j in range(16):
        q = halo[half * 16 + j]
        for m in range(3):
            out[at + m * 16 + j : at + m * 16 + j + 1, :] = pos[m, pl.ds(q, 1), :]


def faces_kernel(side, halo, fv, pos, after, first_x, second_x, first_y, second_y):
    sx, sy, sz = fv.shape[1:]
    for out, upper in ((first_x, 1 - side[0]), (second_x, side[0])):
        x = upper * (sx - 1)
        for m in range(3):
            for h in range(2):
                out[(m * 2 + h) * 16 : (m * 2 + h + 1) * 16, :] = fv[m, x, :, h * 128 : (h + 1) * 128]
        put_listed(halo, upper, pos, out, 96)
    odd = jnp.full((sx, sz), side[1], jnp.int32) == 1
    for m in range(3):
        begin, end = fv[m, :, 0, :], fv[m, :, sy - 1, :]
        first_y[m] = jnp.where(odd, begin, end)
        second_y[m] = jnp.where(odd, end, begin)


def deposit_kernel(owner_in, local_in, cell_in, vel_in, out, slot_out, done, taken, owner, local, cell, vel, sems):
    blocks = cell.shape[0]
    copies = [
        pltpu.make_async_copy(src, dst, sems.at[i])
        for i, (src, dst) in enumerate(((vel_in, vel), (cell_in, cell), (owner_in, owner), (local_in, local)))
    ]
    for c in copies:
        c.start()
    lanes = lax.broadcasted_iota(jnp.int32, (4, 128), 1)
    rows4 = lax.broadcasted_iota(jnp.int32, (4, 128), 0)
    mark = (lanes == 127) & (rows4 == 0)
    done[...] = jnp.zeros(done.shape, F32)
    out[...] = jnp.broadcast_to(jnp.where(mark, -1.0, 0.0).astype(F32)[None], out.shape)

    def clear(t, c):
        taken[t] = 0
        return c

    lax.fori_loop(0, taken.shape[0], clear, 0, unroll=8)
    r8 = lax.broadcasted_iota(jnp.int32, (8, 128), 0)
    lane16 = lax.broadcasted_iota(jnp.int32, (128, 128), 1) // 16
    for c in copies:
        c.wait()

    def group(g, c):
        base = pl.multiple_of(g * DEPOSIT_GROUP, DEPOSIT_GROUP)
        cells = cell[pl.ds(base, DEPOSIT_GROUP), :]
        v = [vel[m, pl.ds(base, DEPOSIT_GROUP), :] for m in range(3)]
        for start in range(0, DEPOSIT_GROUP, 8):
            loads, hots = [], []
            for k in range(start, start + 8):
                rows = [jnp.broadcast_to(v[m][k : k + 1, :], (8, 128)) for m in range(3)]
                load = jnp.where(r8 == 1, rows[0], jnp.where(r8 == 2, rows[1], rows[2]))
                load = jnp.where(r8 == 0, 1.0, jnp.where(r8 < 4, load, 0.0))
                hi = load.astype(BF16).astype(F32)
                loads += [hi, load - hi]
                hots.append(onehot_cells(cells[k : k + 1, :]))
            turned = jnp.concatenate(loads, axis=0).T
            turned = turned.astype(BF16)
            apart = [jnp.where(lane16 == k, turned, jnp.zeros_like(turned)) for k in range(8)]
            found = dot(jnp.concatenate(hots, axis=1), jnp.concatenate(apart, axis=0)).T
            for k in range(8):
                q = base + start + k
                both = found[k * 16 : k * 16 + 8] + found[k * 16 + 8 : k * 16 + 16]
                tile = owner[q]
                rank = taken[tile]
                taken[tile] = rank + 1
                slot = tile * CAP + rank
                slot_out[q] = slot
                ident = jnp.full((4, 128), local[q], jnp.int32).astype(F32)
                out[slot] = jnp.where(mark, ident, both[0:4])
        return c

    lax.fori_loop(0, blocks // DEPOSIT_GROUP, group, 0)


def swap_groups(v):
    row = lax.broadcasted_iota(jnp.int32, v.shape, 1)
    grp = lax.broadcasted_iota(jnp.int32, v.shape, 2) // 16
    for s in range(3):
        step = 1 << s
        ra, gb = (row >> s) & 1, (grp >> s) & 1
        up = pltpu.roll(pltpu.roll(v, 8 - step, 1), 16 * step, 2)
        dn = pltpu.roll(pltpu.roll(v, step, 1), 128 - 16 * step, 2)
        v = jnp.where(ra == gb, v, jnp.where(ra < gb, up, dn))
    return v


def places(sx, sy):
    return [
        (bx * 2, slice(by * 4, by * 4 + 4), slice(h * 128, h * 128 + 128))
        for bx in range(sx // 2)
        for by in range(sy // 4)
        for h in range(2)
    ]


def to_bricks(grid, m):
    tiles = [jnp.concatenate([grid[m, x, y, z], grid[m, x + 1, y, z]], axis=0) for x, y, z in places(*grid.shape[1:3])]
    return swap_groups(jnp.stack(tiles, axis=0)).reshape(len(tiles) * 8, 128)


def old_kernel(fv, sent, bricks, around):
    around[...] = sent[96:144, :]
    for m in range(3):
        bricks[m] = to_bricks(fv, m)


def spread_kernel(side, fv, first_x, second_x, first_y, second_y, bricks, grid):
    sx, sy, sz = fv.shape[1:]
    odd = side[0].astype(F32)
    odd_y = jnp.full((sx, sz), side[1], jnp.int32) == 1
    yrow = lax.broadcasted_iota(jnp.int32, (sy, sz), 0)
    zlane = lax.broadcasted_iota(jnp.int32, (sy, sz), 1)
    for m in range(3):
        first, second = [
            jnp.concatenate([ref[(m * 2 + h) * 16 : (m * 2 + h + 1) * 16, :] for h in range(2)], axis=1)
            for ref in (first_x, second_x)
        ]
        from_low = odd * first + (1.0 - odd) * second
        from_high = (1.0 - odd) * first + odd * second
        lefts = jnp.where(odd_y, first_y[m], second_y[m])
        rights = jnp.where(odd_y, second_y[m], first_y[m])
        for x in range(sx):
            f = fv[m, x]
            high = fv[m, x + 1] if x < sx - 1 else from_high
            low = fv[m, x - 1] if x > 0 else from_low
            beside = high + low
            right = jnp.broadcast_to(rights[x : x + 1, :], (sy, sz))
            left = jnp.broadcast_to(lefts[x : x + 1, :], (sy, sz))
            beside = beside + jnp.where(yrow == sy - 1, right, pltpu.roll(f, sy - 1, 0))
            beside = beside + jnp.where(yrow == 0, left, pltpu.roll(f, 1, 0))
            beside = beside + jnp.where(zlane == sz - 1, 0.0, pltpu.roll(f, sz - 1, 1))
            beside = beside + jnp.where(zlane == 0, 0.0, pltpu.roll(f, 1, 1))
            grid[m, x] = f + 0.1 * (beside - 6.0 * f)
    for m in range(3):
        bricks[m] = to_bricks(grid, m)


def fluid_kernel(recv, old, spread, answer, fluid, done):
    done[...] = jnp.zeros(done.shape, F32)
    slots = recv.shape[0] // 4
    bricks = old.shape[1]
    count = recv[pl.ds(0, slots, stride=4), :]
    lane = lax.broadcasted_iota(jnp.int32, (slots, 128), 1)
    ident = count[:, 127:128]
    ident_row = count.T[127:128, :]
    wide = lax.broadcasted_iota(jnp.int32, (slots, bricks), 1).astype(F32)
    by_slot = (wide == jnp.broadcast_to(ident, (slots, bricks))).astype(F32).astype(BF16)
    tall = lax.broadcasted_iota(jnp.int32, (bricks, slots), 0).astype(F32)
    by_brick = (tall == jnp.broadcast_to(ident_row, (bricks, slots))).astype(F32).astype(BF16)
    parts = [jnp.where(lane == 127, 1.0, count).astype(BF16)]
    for m in range(3):
        parts += list(split2(recv[pl.ds(m + 1, slots, stride=4), :]))
    summed = dot(by_brick, jnp.concatenate(parts, axis=1))
    cnt = summed[:, 0:128]
    momentum = [summed[:, (1 + 2 * m) * 128 : (2 + 2 * m) * 128] + summed[:, (2 + 2 * m) * 128 : (3 + 2 * m) * 128] for m in range(3)]
    last = lax.broadcasted_iota(jnp.int32, (bricks, 128), 1) == 127
    others = jnp.sum(jnp.where(last, 0.0, cnt), axis=1, keepdims=True)
    cnt = jnp.where(last, 128.0 * cnt - others, cnt)
    solid = 0.5 * cnt
    voids = 1.0 - 0.6 * solid / (1.0 + solid)
    beta = (1.0 - voids) / (voids * voids)
    scale = 0.15 * beta
    table = []
    for m in range(3):
        new = spread[m] + scale * (momentum[m] - cnt * old[m])
        table += list(split2(new))
        moved = swap_groups(new.reshape(bricks // 8, 8, 128))
        for i, (x, y, z) in enumerate(places(*fluid.shape[1:3])):
            fluid[m, x, y, z] = moved[i, 0:4]
            fluid[m, x + 1, y, z] = moved[i, 4:8]
    table += list(split2(beta))
    found = dot(by_slot, jnp.concatenate(table, axis=1))
    for c in range(4):
        answer[pl.ds(c, slots, stride=4), :] = (
            found[:, 2 * c * 128 : (2 * c + 1) * 128] + found[:, (2 * c + 1) * 128 : (2 * c + 2) * 128]
        )


def feature_rows(x):
    hi, lo, both = [], [], []
    for m in range(3):
        u = x[m] - 0.5
        h = u.astype(BF16).astype(F32)
        l = (u - h).astype(BF16).astype(F32)
        hi.append(h)
        lo.append(l)
        both.append(h + l)
    return hi, lo, both, both[0] * both[0] + both[1] * both[1] + both[2] * both[2]


def split3(n):
    a = n.astype(BF16).astype(F32)
    b = (n - a).astype(BF16).astype(F32)
    return a, b, n - a - b


def push_loop(step, side, first, second, pos, listed, push, feat_b, feat_a):
    blocks = pos.shape[1]
    one = jnp.ones((8, 128), F32)
    zero = jnp.zeros((8, 128), F32)

    def put(ref, q0, feats):
        for k, v in enumerate(feats):
            ref[pl.ds(q0 * 16 + k, 8, stride=16), :] = v

    def own(g, c):
        q0 = pl.multiple_of(g * 8, 8)
        hi, lo, both, norm = feature_rows([pos[m, pl.ds(q0, 8), :] for m in range(3)])
        n = split3(norm)
        put(feat_b, q0, hi + [one, n[0], n[1], n[2], one] + lo + [one, zero, zero, zero, zero])
        n = split3(norm + EPS2)
        h2, l2 = [-2.0 * v for v in hi], [-2.0 * v for v in lo]
        put(feat_a, q0, h2 + [n[0], one, one, one, n[1]] + l2 + [n[2], zero, zero, zero, zero])
        return c

    lax.fori_loop(0, blocks // 8, own, 0, unroll=2)
    for refs, upper in zip(listed, (1 - side[0], side[0])):
        for g in range(2):
            hi, lo, _, norm = feature_rows([sum(ref[at + m * 16 + g * 8 : at + m * 16 + g * 8 + 8, :] for ref, at in refs) for m in range(3)])
            n = split3(norm)
            put(feat_b, pl.multiple_of(blocks + upper * 16 + g * 8, 8), hi + [one, n[0], n[1], n[2], one] + lo + [one, zero, zero, zero, zero])
    push[...] = jnp.zeros(push.shape, F32)
    top = lax.broadcasted_iota(jnp.int32, (8, 128), 0) < 3

    def one_pair(p):
        a = first[step, p]
        b = second[step, p]
        fb = feat_b[pl.ds(pl.multiple_of(b * 16, 16), 16), :]
        fa = feat_a[pl.ds(pl.multiple_of(a * 16, 16), 16), :]
        x, y = fa[0:8], fa[8:16]
        z = jnp.where(top, y, 0.0)
        ga = jnp.concatenate([x, jnp.where(top, x, y), z, z], axis=0).astype(BF16)
        lhs = fb.astype(BF16)
        r2 = dot(jnp.concatenate([lhs, lhs], axis=0), ga, ((0,), (0,)))
        w = jnp.maximum(lax.rsqrt(jnp.maximum(r2, EPS2)) - 4.0, 0.0)
        res = dot(jnp.concatenate([lhs, lhs], axis=1), jnp.concatenate(split2(w), axis=0))
        total = jnp.broadcast_to(res[3:4], (8, 128))
        return a, (-0.5) * (x + z) * total - (res[0:8] + res[8:16])

    def pairs(g, c):
        done = [one_pair(g * PAIR_GROUP + k) for k in range(PAIR_GROUP)]
        for a, f in done:
            rows = pl.ds(pl.multiple_of(a * 8, 8), 8)
            push[rows, :] = push[rows, :] + f
        return c

    lax.fori_loop(0, first.shape[1] // PAIR_GROUP, pairs, 0)


def push_kernel(side, first, second, slot, pos, listed_a, listed_b, around, after, push, slot_out, feat_b, feat_a):
    def hand_on(q, c):
        slot_out[q] = slot[q]
        return c

    lax.fori_loop(0, slot.shape[0], hand_on, 0, unroll=8)
    listed = (((listed_a, 96),), ((listed_b, 96), (around, 0)))
    push_loop(0, side, first, second, pos, listed, push, feat_b, feat_a)


def advance(pos, vel, push, flow, pos_out, vel_out):
    blocks = pos.shape[1]
    drift = 2.0 * flow[pl.ds(3, blocks, stride=8), :]
    for m in range(3):
        v = vel[m]
        force = 2.5 * push[pl.ds(m, blocks, stride=8), :] + drift * (flow[pl.ds(m, blocks, stride=8), :] - v)
        if m == 2:
            force = force - 1.0
        v = v + 0.1 * force
        vel_out[m] = v
        pos_out[m] = pos[m] + 0.1 * v


def pick(hot, v):
    v = jnp.concatenate([v, v], axis=0)
    hi = v.astype(BF16).astype(F32)
    both = dot(jnp.concatenate([hi, v - hi], axis=0).astype(BF16), hot)
    return both[0:8] + both[8:16]


def listed_kernel(side, slot, halo, back, cell, pos, vel, push, first_out, second_out):
    r8 = lax.broadcasted_iota(jnp.int32, (8, 128), 0)

    def tile(ref, q):
        rows = [jnp.broadcast_to(ref[m, pl.ds(q, 1), :], (8, 128)) for m in range(3)]
        return jnp.where(r8 == 0, rows[0], jnp.where(r8 == 1, rows[1], rows[2]))

    for out, upper in ((first_out, 1 - side[0]), (second_out, side[0])):
        for j in range(16):
            q = halo[upper * 16 + j]
            flow = pick(onehot_cells(cell[pl.ds(q, 1), :]), back[slot[q]])
            v = tile(vel, q)
            rows = pl.ds(pl.multiple_of(q * 8, 8), 8)
            drift = 2.0 * jnp.broadcast_to(flow[3:4], (8, 128))
            force = 2.5 * push[rows, :] + drift * (flow - v)
            v = v + 0.1 * jnp.where(r8 == 2, force - 1.0, force)
            x = tile(pos, q) + 0.1 * v
            for m in range(3):
                out[m * 16 + j : m * 16 + j + 1, :] = x[m : m + 1, :]


def pick_kernel(slot, back, cell, pos, vel, push, after, flow, pos_out, vel_out):
    def group(g, c):
        base = pl.multiple_of(g * BLOCK_GROUP, BLOCK_GROUP)
        cells = cell[pl.ds(base, BLOCK_GROUP), :]
        for k in range(BLOCK_GROUP):
            q = base + k
            flow[pl.ds(pl.multiple_of(q * 8, 8), 8), :] = pick(onehot_cells(cells[k : k + 1, :]), back[slot[q]])
        return c

    lax.fori_loop(0, cell.shape[0] // BLOCK_GROUP, group, 0)
    advance(pos, vel, push, flow, pos_out, vel_out)


def last_kernel(side, first, second, pos, vel, listed_a, listed_b, flow, pos_out, vel_out, push, feat_b, feat_a):
    push_loop(1, side, first, second, pos, (((listed_a, 0),), ((listed_b, 0),)), push, feat_b, feat_a)
    advance(pos, vel, push, flow, pos_out, vel_out)


def call(kernel, in_specs, out_shape, out_specs, scratch=(), micros=1, vmem=20 * 1024 * 1024):
    return pl.pallas_call(
        kernel,
        in_specs=in_specs,
        out_shape=out_shape,
        out_specs=out_specs,
        scratch_shapes=list(scratch),
        compiler_params=pltpu.CompilerParams(vmem_limit_bytes=vmem),
        cost_estimate=pl.CostEstimate(flops=micros * 1_000_000_000, bytes_accessed=micros * 3_000_000, transcendentals=0),
    )


def shape(*dims, dtype=F32):
    return jax.ShapeDtypeStruct(dims, dtype)


def per_device(
    fluid_vel,
    part_pos,
    part_vel,
    brick_owner,
    brick_local,
    cell_in_brick,
    pair_self,
    pair_other,
    halo_list,
):
    nx, ny = lax.axis_size("gx"), lax.axis_size("gy")
    tiles = nx * ny
    blocks = part_pos.shape[0]
    slots = tiles * CAP
    sx, sy, sz = fluid_vel.shape[1:]
    pos = jnp.transpose(part_pos, (1, 0, 2))
    vel = jnp.transpose(part_vel, (1, 0, 2))

    send, slot, placed = call(
        deposit_kernel,
        [HBM] * 4,
        [shape(slots, 4, 128), shape(blocks, dtype=jnp.int32), shape(8, 128)],
        [VMEM, SMEM, VMEM],
        [
            pltpu.SMEM((tiles,), jnp.int32),
            pltpu.SMEM((blocks,), jnp.int32),
            pltpu.SMEM((blocks,), jnp.int32),
            pltpu.VMEM((blocks, 128), jnp.int32),
            pltpu.VMEM((3, blocks, 128), F32),
            pltpu.SemaphoreType.DMA((4,)),
        ],
        7,
        63_000_000,
    )(brick_owner[:, 0], brick_local, cell_in_brick, vel)
    recv = lax.all_to_all(send.reshape(slots * 4, 128), ("gx", "gy"), split_axis=0, concat_axis=0, tiled=True)

    me_x, me_y = lax.axis_index("gx"), lax.axis_index("gy")
    side = jnp.stack([me_x % 2, me_y % 2]).astype(jnp.int32)
    first_x, second_x, first_y, second_y = call(
        faces_kernel,
        [SMEM, SMEM, VMEM, VMEM, VMEM],
        [shape(144, 128), shape(144, 128), shape(3, sx, sz), shape(3, sx, sz)],
        [VMEM] * 4,
    )(side, halo_list, fluid_vel, pos, placed)
    bricks = sx // 2 * (sy // 4) * (sz // 16)
    old, around = call(
        old_kernel, [VMEM, VMEM], [shape(3, bricks, 128), shape(48, 128)], [VMEM, VMEM]
    )(fluid_vel, second_x)
    perms_x, perms_y = swaps(nx, True), swaps(ny, False)
    first_x = lax.ppermute(first_x, "gx", perms_x[0])
    second_x = lax.ppermute(second_x, "gx", perms_x[1][1:-1])
    around = lax.ppermute(around, "gx", [(0, nx - 1), (nx - 1, 0)])
    first_y = lax.ppermute(first_y, "gy", perms_y[0])
    second_y = lax.ppermute(second_y, "gy", perms_y[1])

    spread = call(
        spread_kernel,
        [SMEM] + [VMEM] * 5,
        shape(3, bricks, 128),
        VMEM,
        [pltpu.VMEM((3, sx, sy, sz), F32)],
        2,
    )(side, fluid_vel, first_x, second_x, first_y, second_y)
    answer, fluid, stepped = call(
        fluid_kernel,
        [VMEM] * 3,
        [shape(slots * 4, 128), shape(3, sx, sy, sz), shape(8, 128)],
        [VMEM] * 3,
        (),
        3,
    )(recv, old, spread)
    back = lax.all_to_all(answer, ("gx", "gy"), split_axis=0, concat_axis=0, tiled=True).reshape(slots, 4, 128)
    pair_scratch = [pltpu.VMEM(((blocks + 32) * 16, 128), F32), pltpu.VMEM((blocks * 16, 128), F32)]
    push, slot = call(
        push_kernel,
        [SMEM] * 4 + [VMEM] * 5,
        [shape(blocks * 8, 128), shape(blocks, dtype=jnp.int32)],
        [VMEM, SMEM],
        pair_scratch,
        14,
    )(side, pair_self, pair_other, slot, pos, first_x, second_x, around, stepped)

    first, second = call(
        listed_kernel,
        [SMEM] * 3 + [VMEM] * 5,
        [shape(48, 128), shape(48, 128)],
        [VMEM] * 2,
        (),
        2,
    )(side, slot, halo_list, back, cell_in_brick, pos, vel, push)
    listed_a = lax.ppermute(first, "gx", perms_x[0])
    listed_b = lax.ppermute(second, "gx", perms_x[1])
    flow, pos, vel = call(
        pick_kernel,
        [SMEM] + [VMEM] * 6,
        [shape(blocks * 8, 128), shape(3, blocks, 128), shape(3, blocks, 128)],
        [VMEM] * 3,
        (),
        6,
    )(slot, back, cell_in_brick, pos, vel, push, first)
    pos, vel = call(
        last_kernel,
        [SMEM] * 3 + [VMEM] * 5,
        [shape(3, blocks, 128), shape(3, blocks, 128)],
        [VMEM] * 2,
        [pltpu.VMEM((blocks * 8, 128), F32)] + pair_scratch,
        15,
    )(side, pair_self, pair_other, pos, vel, listed_a, listed_b, flow)
    return fluid, jnp.transpose(pos, (1, 0, 2)), jnp.transpose(vel, (1, 0, 2))


def solution(mesh):
    in_specs = (
        P(None, "gx", "gy", None),
        P(("gx", "gy"), None, None),
        P(("gx", "gy"), None, None),
        P(("gx", "gy"), None),
        P(("gx", "gy")),
        P(("gx", "gy"), None),
        P(None, ("gx", "gy")),
        P(None, ("gx", "gy")),
        P(("gx", "gy")),
    )
    out_specs = (
        P(None, "gx", "gy", None),
        P(("gx", "gy"), None, None),
        P(("gx", "gy"), None, None),
    )
    return jax.shard_map(
        per_device, mesh=mesh, in_specs=in_specs, out_specs=out_specs, check_vma=False
    )
```

```python
import functools

import jax
import jax.numpy as jnp
from jax import lax
from jax.experimental import pallas as pl
from jax.experimental.pallas import tpu as pltpu
from jax.sharding import PartitionSpec as P

F32 = jnp.float32
BF16 = jnp.bfloat16
PAIR_GROUP = 256
ORDERED_GROUP = 128
BLOCK_GROUP = 128
DEPOSIT_GROUP = 128
CAP = 4
EPS2 = 0.0025
VMEM = pl.BlockSpec(memory_space=pltpu.VMEM)
SMEM = pl.BlockSpec(memory_space=pltpu.SMEM)
HBM = pl.BlockSpec(memory_space=pltpu.HBM)


def split2(x):
    hi = x.astype(BF16)
    return hi, (x - hi.astype(F32)).astype(BF16)


def onehot_cells(row):
    cells = lax.broadcasted_iota(jnp.int32, (128, 128), 0)
    return (cells == jnp.broadcast_to(row, (128, 128))).astype(F32).astype(BF16)


def dot(a, b, dims=((1,), (0,))):
    return lax.dot_general(a, b, (dims, ((), ())), preferred_element_type=F32)


def swaps(n, closed):
    first = [(i, i ^ 1) for i in range(n)]
    second = [(i, (i + 1 if i % 2 else i - 1) % n) for i in range(n)]
    return first, (second if closed else second[1:-1])


def put_listed(halo, half, pos, out, at):
    for j in range(16):
        q = halo[half * 16 + j]
        for m in range(3):
            out[at + m * 16 + j : at + m * 16 + j + 1, :] = pos[m, pl.ds(q, 1), :]


def faces_kernel(side, halo, fv, pos, after, first_x, second_x, first_y, second_y):
    sx, sy, sz = fv.shape[1:]
    for out, upper in ((first_x, 1 - side[0]), (second_x, side[0])):
        x = upper * (sx - 1)
        for m in range(3):
            for h in range(2):
                out[(m * 2 + h) * 16 : (m * 2 + h + 1) * 16, :] = fv[m, x, :, h * 128 : (h + 1) * 128]
        put_listed(halo, upper, pos, out, 96)
    odd = jnp.full((sx, sz), side[1], jnp.int32) == 1
    for m in range(3):
        begin, end = fv[m, :, 0, :], fv[m, :, sy - 1, :]
        first_y[m] = jnp.where(odd, begin, end)
        second_y[m] = jnp.where(odd, end, begin)


def deposit_kernel(owner_in, local_in, cell_in, vel_in, out, slot_out, done, taken, owner, local, cell, vel, sems):
    blocks = cell.shape[0]
    copies = [
        pltpu.make_async_copy(src, dst, sems.at[i])
        for i, (src, dst) in enumerate(((vel_in, vel), (cell_in, cell), (owner_in, owner), (local_in, local)))
    ]
    for c in copies:
        c.start()
    lanes = lax.broadcasted_iota(jnp.int32, (4, 128), 1)
    rows4 = lax.broadcasted_iota(jnp.int32, (4, 128), 0)
    mark = (lanes == 127) & (rows4 == 0)
    done[...] = jnp.zeros(done.shape, F32)
    out[...] = jnp.broadcast_to(jnp.where(mark, -1.0, 0.0).astype(F32)[None], out.shape)

    def clear(t, c):
        taken[t] = 0
        return c

    lax.fori_loop(0, taken.shape[0], clear, 0, unroll=8)
    r8 = lax.broadcasted_iota(jnp.int32, (8, 128), 0)
    lane16 = lax.broadcasted_iota(jnp.int32, (128, 128), 1) // 16
    for c in copies:
        c.wait()

    def group(g, c):
        base = pl.multiple_of(g * DEPOSIT_GROUP, DEPOSIT_GROUP)
        cells = cell[pl.ds(base, DEPOSIT_GROUP), :]
        v = [vel[m, pl.ds(base, DEPOSIT_GROUP), :] for m in range(3)]
        for start in range(0, DEPOSIT_GROUP, 8):
            loads, hots = [], []
            for k in range(start, start + 8):
                rows = [jnp.broadcast_to(v[m][k : k + 1, :], (8, 128)) for m in range(3)]
                load = jnp.where(r8 == 1, rows[0], jnp.where(r8 == 2, rows[1], rows[2]))
                load = jnp.where(r8 == 0, 1.0, jnp.where(r8 < 4, load, 0.0))
                hi = load.astype(BF16).astype(F32)
                loads += [hi, load - hi]
                hots.append(onehot_cells(cells[k : k + 1, :]))
            turned = jnp.concatenate(loads, axis=0).T
            turned = turned.astype(BF16)
            apart = [jnp.where(lane16 == k, turned, jnp.zeros_like(turned)) for k in range(8)]
            found = dot(jnp.concatenate(hots, axis=1), jnp.concatenate(apart, axis=0)).T
            for k in range(8):
                q = base + start + k
                both = found[k * 16 : k * 16 + 8] + found[k * 16 + 8 : k * 16 + 16]
                tile = owner[q]
                rank = taken[tile]
                taken[tile] = rank + 1
                slot = tile * CAP + rank
                slot_out[q] = slot
                ident = jnp.full((4, 128), local[q], jnp.int32).astype(F32)
                out[slot] = jnp.where(mark, ident, both[0:4])
        return c

    lax.fori_loop(0, blocks // DEPOSIT_GROUP, group, 0)


def swap_groups(v):
    row = lax.broadcasted_iota(jnp.int32, v.shape, 1)
    grp = lax.broadcasted_iota(jnp.int32, v.shape, 2) // 16
    for s in range(3):
        step = 1 << s
        ra, gb = (row >> s) & 1, (grp >> s) & 1
        up = pltpu.roll(pltpu.roll(v, 8 - step, 1), 16 * step, 2)
        dn = pltpu.roll(pltpu.roll(v, step, 1), 128 - 16 * step, 2)
        v = jnp.where(ra == gb, v, jnp.where(ra < gb, up, dn))
    return v


def places(sx, sy):
    return [
        (bx * 2, slice(by * 4, by * 4 + 4), slice(h * 128, h * 128 + 128))
        for bx in range(sx // 2)
        for by in range(sy // 4)
        for h in range(2)
    ]


def to_bricks(grid, m):
    tiles = [jnp.concatenate([grid[m, x, y, z], grid[m, x + 1, y, z]], axis=0) for x, y, z in places(*grid.shape[1:3])]
    return swap_groups(jnp.stack(tiles, axis=0)).reshape(len(tiles) * 8, 128)


def old_kernel(fv, sent, bricks, around):
    around[...] = sent[96:144, :]
    for m in range(3):
        bricks[m] = to_bricks(fv, m)


def spread_kernel(side, ordered, fv, first_x, second_x, first_y, second_y, bricks, grid):
    sx, sy, sz = fv.shape[1:]
    odd = side[0].astype(F32)
    odd_y = jnp.full((sx, sz), side[1], jnp.int32) == 1
    yrow = lax.broadcasted_iota(jnp.int32, (sy, sz), 0)
    zlane = lax.broadcasted_iota(jnp.int32, (sy, sz), 1)
    for m in range(3):
        first, second = [
            jnp.concatenate([ref[(m * 2 + h) * 16 : (m * 2 + h + 1) * 16, :] for h in range(2)], axis=1)
            for ref in (first_x, second_x)
        ]
        from_low = odd * first + (1.0 - odd) * second
        from_high = (1.0 - odd) * first + odd * second
        lefts = jnp.where(odd_y, first_y[m], second_y[m])
        rights = jnp.where(odd_y, second_y[m], first_y[m])
        for x in range(sx):
            f = fv[m, x]
            high = fv[m, x + 1] if x < sx - 1 else from_high
            low = fv[m, x - 1] if x > 0 else from_low
            beside = high + low
            right = jnp.broadcast_to(rights[x : x + 1, :], (sy, sz))
            left = jnp.broadcast_to(lefts[x : x + 1, :], (sy, sz))
            beside = beside + jnp.where(yrow == sy - 1, right, pltpu.roll(f, sy - 1, 0))
            beside = beside + jnp.where(yrow == 0, left, pltpu.roll(f, 1, 0))
            beside = beside + jnp.where(zlane == sz - 1, 0.0, pltpu.roll(f, sz - 1, 1))
            beside = beside + jnp.where(zlane == 0, 0.0, pltpu.roll(f, 1, 1))
            grid[m, x] = f + 0.1 * (beside - 6.0 * f)
    for m in range(3):
        bricks[m] = to_bricks(grid, m)


def fluid_kernel(recv, old, spread, answer, fluid, done):
    done[...] = jnp.zeros(done.shape, F32)
    slots = recv.shape[0] // 4
    bricks = old.shape[1]
    count = recv[pl.ds(0, slots, stride=4), :]
    lane = lax.broadcasted_iota(jnp.int32, (slots, 128), 1)
    ident = count[:, 127:128]
    ident_row = count.T[127:128, :]
    wide = lax.broadcasted_iota(jnp.int32, (slots, bricks), 1).astype(F32)
    by_slot = (wide == jnp.broadcast_to(ident, (slots, bricks))).astype(F32).astype(BF16)
    tall = lax.broadcasted_iota(jnp.int32, (bricks, slots), 0).astype(F32)
    by_brick = (tall == jnp.broadcast_to(ident_row, (bricks, slots))).astype(F32).astype(BF16)
    parts = [jnp.where(lane == 127, 1.0, count).astype(BF16)]
    for m in range(3):
        parts += list(split2(recv[pl.ds(m + 1, slots, stride=4), :]))
    summed = dot(by_brick, jnp.concatenate(parts, axis=1))
    cnt = summed[:, 0:128]
    momentum = [summed[:, (1 + 2 * m) * 128 : (2 + 2 * m) * 128] + summed[:, (2 + 2 * m) * 128 : (3 + 2 * m) * 128] for m in range(3)]
    last = lax.broadcasted_iota(jnp.int32, (bricks, 128), 1) == 127
    others = jnp.sum(jnp.where(last, 0.0, cnt), axis=1, keepdims=True)
    cnt = jnp.where(last, 128.0 * cnt - others, cnt)
    solid = 0.5 * cnt
    voids = 1.0 - 0.6 * solid / (1.0 + solid)
    beta = (1.0 - voids) / (voids * voids)
    scale = 0.15 * beta
    table = []
    for m in range(3):
        new = spread[m] + scale * (momentum[m] - cnt * old[m])
        table += list(split2(new))
        moved = swap_groups(new.reshape(bricks // 8, 8, 128))
        for i, (x, y, z) in enumerate(places(*fluid.shape[1:3])):
            fluid[m, x, y, z] = moved[i, 0:4]
            fluid[m, x + 1, y, z] = moved[i, 4:8]
    table += list(split2(beta))
    found = dot(by_slot, jnp.concatenate(table, axis=1))
    for c in range(4):
        answer[pl.ds(c, slots, stride=4), :] = (
            found[:, 2 * c * 128 : (2 * c + 1) * 128] + found[:, (2 * c + 1) * 128 : (2 * c + 2) * 128]
        )


def feature_rows(x):
    hi, lo, both = [], [], []
    for m in range(3):
        u = x[m] - 0.5
        h = u.astype(BF16).astype(F32)
        l = (u - h).astype(BF16).astype(F32)
        hi.append(h)
        lo.append(l)
        both.append(h + l)
    return hi, lo, both, both[0] * both[0] + both[1] * both[1] + both[2] * both[2]


def split3(n):
    a = n.astype(BF16).astype(F32)
    b = (n - a).astype(BF16).astype(F32)
    return a, b, n - a - b


def order_kernel(first, second, after, ordered):
    n = first.shape[1]
    blocks = n // 2

    def place(p, own):
        b = second[1, p]
        inside = (b < blocks).astype(jnp.int32)
        at = jnp.where(inside == 1, own, n - 1 - p + own)
        ordered[at] = first[1, p]
        ordered[n + at] = b
        return own + inside

    own = lax.fori_loop(0, n, place, jnp.int32(0), unroll=8)
    ordered[2 * n] = own // ORDERED_GROUP


def features(side, pos, listed, feat_b, feat_a):
    blocks = pos.shape[1]
    one = jnp.ones((8, 128), F32)
    zero = jnp.zeros((8, 128), F32)

    def put(ref, q0, feats):
        for k, v in enumerate(feats):
            ref[pl.ds(q0 * 16 + k, 8, stride=16), :] = v

    def own(g, c):
        q0 = pl.multiple_of(g * 8, 8)
        hi, lo, both, norm = feature_rows([pos[m, pl.ds(q0, 8), :] for m in range(3)])
        n = split3(norm)
        put(feat_b, q0, hi + [one, n[0], n[1], n[2], one] + lo + [one, zero, zero, zero, zero])
        n = split3(norm + EPS2)
        h2, l2 = [-2.0 * v for v in hi], [-2.0 * v for v in lo]
        put(feat_a, q0, h2 + [n[0], one, one, one, n[1]] + l2 + [n[2], zero, zero, zero, zero])
        return c

    lax.fori_loop(0, blocks // 8, own, 0, unroll=2)
    for i, refs in enumerate(listed):
        upper = side[0] if i else 1 - side[0]
        for g in range(2):
            hi, lo, _, norm = feature_rows([sum(ref[at + m * 16 + g * 8 : at + m * 16 + g * 8 + 8, :] for ref, at in refs) for m in range(3)])
            n = split3(norm)
            put(feat_b, pl.multiple_of(blocks + upper * 16 + g * 8, 8), hi + [one, n[0], n[1], n[2], one] + lo + [one, zero, zero, zero, zero])


def push_pairs(pair, begin, end, group, push, feat_b, feat_a):
    top = lax.broadcasted_iota(jnp.int32, (8, 128), 0) < 3

    def one_pair(p):
        a, b = pair(p)
        fb = feat_b[pl.ds(pl.multiple_of(b * 16, 16), 16), :]
        fa = feat_a[pl.ds(pl.multiple_of(a * 16, 16), 16), :]
        x, y = fa[0:8], fa[8:16]
        z = jnp.where(top, y, 0.0)
        ga = jnp.concatenate([x, jnp.where(top, x, y), z, z], axis=0).astype(BF16)
        lhs = fb.astype(BF16)
        r2 = dot(jnp.concatenate([lhs, lhs], axis=0), ga, ((0,), (0,)))
        w = jnp.maximum(lax.rsqrt(jnp.maximum(r2, EPS2)) - 4.0, 0.0)
        res = dot(jnp.concatenate([lhs, lhs], axis=1), jnp.concatenate(split2(w), axis=0))
        total = jnp.broadcast_to(res[3:4], (8, 128))
        return a, (-0.5) * (x + z) * total - (res[0:8] + res[8:16])

    def pairs(g, c):
        done = [one_pair(g * group + k) for k in range(group)]
        for a, f in done:
            rows = pl.ds(pl.multiple_of(a * 8, 8), 8)
            push[rows, :] = push[rows, :] + f
        return c

    lax.fori_loop(begin, end, pairs, 0)


def push_kernel(side, first, second, slot, pos, listed_a, listed_b, around, after, push, slot_out, feat_b, feat_a):
    def hand_on(q, c):
        slot_out[q] = slot[q]
        return c

    lax.fori_loop(0, slot.shape[0], hand_on, 0, unroll=8)
    listed = (((listed_a, 96),), ((listed_b, 96), (around, 0)))
    features(side, pos, listed, feat_b, feat_a)
    push[...] = jnp.zeros(push.shape, F32)
    groups = first.shape[1] // PAIR_GROUP
    push_pairs(lambda p: (first[0, p], second[0, p]), 0, groups, PAIR_GROUP, push, feat_b, feat_a)


def advance(pos, vel, push, flow, pos_out, vel_out):
    blocks = pos.shape[1]
    drift = 2.0 * flow[pl.ds(3, blocks, stride=8), :]
    for m in range(3):
        v = vel[m]
        force = 2.5 * push[pl.ds(m, blocks, stride=8), :] + drift * (flow[pl.ds(m, blocks, stride=8), :] - v)
        if m == 2:
            force = force - 1.0
        v = v + 0.1 * force
        vel_out[m] = v
        pos_out[m] = pos[m] + 0.1 * v


def pick(hot, v):
    v = jnp.concatenate([v, v], axis=0)
    hi = v.astype(BF16).astype(F32)
    both = dot(jnp.concatenate([hi, v - hi], axis=0).astype(BF16), hot)
    return both[0:8] + both[8:16]


def pick_kernel(side, slot, halo, back, cell, pos, vel, push, flow, pos_out, vel_out, first_x, second_x):
    def group(g, c):
        base = pl.multiple_of(g * BLOCK_GROUP, BLOCK_GROUP)
        cells = cell[pl.ds(base, BLOCK_GROUP), :]
        for k in range(BLOCK_GROUP):
            q = base + k
            flow[pl.ds(pl.multiple_of(q * 8, 8), 8), :] = pick(onehot_cells(cells[k : k + 1, :]), back[slot[q]])
        return c

    lax.fori_loop(0, cell.shape[0] // BLOCK_GROUP, group, 0)
    advance(pos, vel, push, flow, pos_out, vel_out)
    put_listed(halo, 1 - side[0], pos_out, first_x, 0)
    put_listed(halo, side[0], pos_out, second_x, 0)


def inner_kernel(ordered, pos, push, feat_b, feat_a):
    n = pos.shape[1] * 2
    features(None, pos, (), feat_b, feat_a)
    push[...] = jnp.zeros(push.shape, F32)
    push_pairs(lambda p: (ordered[p], ordered[n + p]), 0, ordered[2 * n], ORDERED_GROUP, push, feat_b, feat_a)


def last_kernel(side, ordered, pos, vel, listed_a, listed_b, flow, inner, pos_out, vel_out, push, feat_b, feat_a):
    n = pos.shape[1] * 2
    features(side, pos, (((listed_a, 0),), ((listed_b, 0),)), feat_b, feat_a)
    push[...] = inner[...]
    groups = n // ORDERED_GROUP
    push_pairs(lambda p: (ordered[p], ordered[n + p]), ordered[2 * n], groups, ORDERED_GROUP, push, feat_b, feat_a)
    advance(pos, vel, push, flow, pos_out, vel_out)


def call(kernel, in_specs, out_shape, out_specs, scratch=(), micros=1, vmem=20 * 1024 * 1024):
    return pl.pallas_call(
        kernel,
        in_specs=in_specs,
        out_shape=out_shape,
        out_specs=out_specs,
        scratch_shapes=list(scratch),
        compiler_params=pltpu.CompilerParams(vmem_limit_bytes=vmem),
        cost_estimate=pl.CostEstimate(flops=micros * 1_000_000_000, bytes_accessed=micros * 3_000_000, transcendentals=0),
    )


def shape(*dims, dtype=F32):
    return jax.ShapeDtypeStruct(dims, dtype)


def per_device(
    fluid_vel,
    part_pos,
    part_vel,
    brick_owner,
    brick_local,
    cell_in_brick,
    pair_self,
    pair_other,
    halo_list,
):
    nx, ny = lax.axis_size("gx"), lax.axis_size("gy")
    tiles = nx * ny
    blocks = part_pos.shape[0]
    slots = tiles * CAP
    sx, sy, sz = fluid_vel.shape[1:]
    pos = jnp.transpose(part_pos, (1, 0, 2))
    vel = jnp.transpose(part_vel, (1, 0, 2))

    send, slot, placed = call(
        deposit_kernel,
        [HBM] * 4,
        [shape(slots, 4, 128), shape(blocks, dtype=jnp.int32), shape(8, 128)],
        [VMEM, SMEM, VMEM],
        [
            pltpu.SMEM((tiles,), jnp.int32),
            pltpu.SMEM((blocks,), jnp.int32),
            pltpu.SMEM((blocks,), jnp.int32),
            pltpu.VMEM((blocks, 128), jnp.int32),
            pltpu.VMEM((3, blocks, 128), F32),
            pltpu.SemaphoreType.DMA((4,)),
        ],
        7,
        63_000_000,
    )(brick_owner[:, 0], brick_local, cell_in_brick, vel)
    recv = lax.all_to_all(send.reshape(slots * 4, 128), ("gx", "gy"), split_axis=0, concat_axis=0, tiled=True)

    me_x, me_y = lax.axis_index("gx"), lax.axis_index("gy")
    side = jnp.stack([me_x % 2, me_y % 2]).astype(jnp.int32)
    first_x, second_x, first_y, second_y = call(
        faces_kernel,
        [SMEM, SMEM, VMEM, VMEM, VMEM],
        [shape(144, 128), shape(144, 128), shape(3, sx, sz), shape(3, sx, sz)],
        [VMEM] * 4,
    )(side, halo_list, fluid_vel, pos, placed)
    bricks = sx // 2 * (sy // 4) * (sz // 16)
    old, around = call(
        old_kernel, [VMEM, VMEM], [shape(3, bricks, 128), shape(48, 128)], [VMEM, VMEM]
    )(fluid_vel, second_x)
    ordered = call(
        order_kernel,
        [SMEM, SMEM, VMEM],
        shape(2 * pair_self.shape[1] + 128, dtype=jnp.int32),
        SMEM,
        (),
        2,
    )(pair_self, pair_other, around)
    perms_x, perms_y = swaps(nx, True), swaps(ny, False)
    first_x = lax.ppermute(first_x, "gx", perms_x[0])
    second_x = lax.ppermute(second_x, "gx", perms_x[1][1:-1])
    around = lax.ppermute(around, "gx", [(0, nx - 1), (nx - 1, 0)])
    first_y = lax.ppermute(first_y, "gy", perms_y[0])
    second_y = lax.ppermute(second_y, "gy", perms_y[1])

    spread = call(
        spread_kernel,
        [SMEM] * 2 + [VMEM] * 5,
        shape(3, bricks, 128),
        VMEM,
        [pltpu.VMEM((3, sx, sy, sz), F32)],
        2,
    )(side, ordered, fluid_vel, first_x, second_x, first_y, second_y)
    answer, fluid, stepped = call(
        fluid_kernel,
        [VMEM] * 3,
        [shape(slots * 4, 128), shape(3, sx, sy, sz), shape(8, 128)],
        [VMEM] * 3,
        (),
        3,
    )(recv, old, spread)
    back = lax.all_to_all(answer, ("gx", "gy"), split_axis=0, concat_axis=0, tiled=True).reshape(slots, 4, 128)
    pair_scratch = [pltpu.VMEM(((blocks + 32) * 16, 128), F32), pltpu.VMEM((blocks * 16, 128), F32)]
    push, slot = call(
        push_kernel,
        [SMEM] * 4 + [VMEM] * 5,
        [shape(blocks * 8, 128), shape(blocks, dtype=jnp.int32)],
        [VMEM, SMEM],
        pair_scratch,
        14,
    )(side, pair_self, pair_other, slot, pos, first_x, second_x, around, stepped)

    flow, pos, vel, listed_a, listed_b = call(
        pick_kernel,
        [SMEM] * 3 + [VMEM] * 5,
        [shape(blocks * 8, 128), shape(3, blocks, 128), shape(3, blocks, 128), shape(48, 128), shape(48, 128)],
        [VMEM] * 5,
        (),
        4,
    )(side, slot, halo_list, back, cell_in_brick, pos, vel, push)
    listed_a = lax.ppermute(listed_a, "gx", perms_x[0])
    listed_b = lax.ppermute(listed_b, "gx", perms_x[1])
    inner = call(
        inner_kernel,
        [SMEM, VMEM],
        shape(blocks * 8, 128),
        VMEM,
        pair_scratch,
        10,
    )(ordered, pos)
    pos, vel = call(
        last_kernel,
        [SMEM] * 2 + [VMEM] * 6,
        [shape(3, blocks, 128), shape(3, blocks, 128)],
        [VMEM] * 2,
        [pltpu.VMEM((blocks * 8, 128), F32)] + pair_scratch,
        5,
    )(side, ordered, pos, vel, listed_a, listed_b, flow, inner)
    return fluid, jnp.transpose(pos, (1, 0, 2)), jnp.transpose(vel, (1, 0, 2))


def solution(mesh):
    in_specs = (
        P(None, "gx", "gy", None),
        P(("gx", "gy"), None, None),
        P(("gx", "gy"), None, None),
        P(("gx", "gy"), None),
        P(("gx", "gy")),
        P(("gx", "gy"), None),
        P(None, ("gx", "gy")),
        P(None, ("gx", "gy")),
        P(("gx", "gy")),
    )
    out_specs = (
        P(None, "gx", "gy", None),
        P(("gx", "gy"), None, None),
        P(("gx", "gy"), None, None),
    )
    return jax.shard_map(
        per_device, mesh=mesh, in_specs=in_specs, out_specs=out_specs, check_vma=False
    )
```

```python
import functools

import jax
import jax.numpy as jnp
from jax import lax
from jax.experimental import pallas as pl
from jax.experimental.pallas import tpu as pltpu
from jax.sharding import PartitionSpec as P

F32 = jnp.float32
BF16 = jnp.bfloat16
PAIR_GROUP = 256
ORDERED_GROUP = 128
BLOCK_GROUP = 128
DEPOSIT_GROUP = 128
CAP = 4
EPS2 = 0.0025
VMEM = pl.BlockSpec(memory_space=pltpu.VMEM)
SMEM = pl.BlockSpec(memory_space=pltpu.SMEM)
HBM = pl.BlockSpec(memory_space=pltpu.HBM)


def split2(x):
    hi = x.astype(BF16)
    return hi, (x - hi.astype(F32)).astype(BF16)


def onehot_cells(row):
    cells = lax.broadcasted_iota(jnp.int32, (128, 128), 0)
    return (cells == jnp.broadcast_to(row, (128, 128))).astype(F32).astype(BF16)


def dot(a, b, dims=((1,), (0,))):
    return lax.dot_general(a, b, (dims, ((), ())), preferred_element_type=F32)


def swaps(n, closed):
    first = [(i, i ^ 1) for i in range(n)]
    second = [(i, (i + 1 if i % 2 else i - 1) % n) for i in range(n)]
    return first, (second if closed else second[1:-1])


def put_listed(halo, half, pos, out, at):
    for j in range(16):
        q = halo[half * 16 + j]
        for m in range(3):
            out[at + m * 16 + j : at + m * 16 + j + 1, :] = pos[m, pl.ds(q, 1), :]


def faces_kernel(side, halo, fv, pos, after, first_x, second_x, first_y, second_y):
    sx, sy, sz = fv.shape[1:]
    for out, upper in ((first_x, 1 - side[0]), (second_x, side[0])):
        x = upper * (sx - 1)
        for m in range(3):
            for h in range(2):
                out[(m * 2 + h) * 16 : (m * 2 + h + 1) * 16, :] = fv[m, x, :, h * 128 : (h + 1) * 128]
        put_listed(halo, upper, pos, out, 96)
    odd = jnp.full((sx, sz), side[1], jnp.int32) == 1
    for m in range(3):
        begin, end = fv[m, :, 0, :], fv[m, :, sy - 1, :]
        first_y[m] = jnp.where(odd, begin, end)
        second_y[m] = jnp.where(odd, end, begin)


def deposit_kernel(owner_in, local_in, cell_in, vel_in, out, slot_out, done, taken, owner, local, cell, vel, sems):
    blocks = cell.shape[0]
    copies = [
        pltpu.make_async_copy(src, dst, sems.at[i])
        for i, (src, dst) in enumerate(((vel_in, vel), (cell_in, cell), (owner_in, owner), (local_in, local)))
    ]
    for c in copies:
        c.start()
    lanes = lax.broadcasted_iota(jnp.int32, (4, 128), 1)
    rows4 = lax.broadcasted_iota(jnp.int32, (4, 128), 0)
    mark = (lanes == 127) & (rows4 == 0)
    done[...] = jnp.zeros(done.shape, F32)
    out[...] = jnp.broadcast_to(jnp.where(mark, -1.0, 0.0).astype(F32)[None], out.shape)

    def clear(t, c):
        taken[t] = 0
        return c

    lax.fori_loop(0, taken.shape[0], clear, 0, unroll=8)
    r8 = lax.broadcasted_iota(jnp.int32, (8, 128), 0)
    lane16 = lax.broadcasted_iota(jnp.int32, (128, 128), 1) // 16
    for c in copies:
        c.wait()

    def group(g, c):
        base = pl.multiple_of(g * DEPOSIT_GROUP, DEPOSIT_GROUP)
        cells = cell[pl.ds(base, DEPOSIT_GROUP), :]
        v = [vel[m, pl.ds(base, DEPOSIT_GROUP), :] for m in range(3)]
        for start in range(0, DEPOSIT_GROUP, 8):
            loads, hots = [], []
            for k in range(start, start + 8):
                rows = [jnp.broadcast_to(v[m][k : k + 1, :], (8, 128)) for m in range(3)]
                load = jnp.where(r8 == 1, rows[0], jnp.where(r8 == 2, rows[1], rows[2]))
                load = jnp.where(r8 == 0, 1.0, jnp.where(r8 < 4, load, 0.0))
                hi = load.astype(BF16).astype(F32)
                loads += [hi, load - hi]
                hots.append(onehot_cells(cells[k : k + 1, :]))
            turned = jnp.concatenate(loads, axis=0).T
            turned = turned.astype(BF16)
            apart = [jnp.where(lane16 == k, turned, jnp.zeros_like(turned)) for k in range(8)]
            found = dot(jnp.concatenate(hots, axis=1), jnp.concatenate(apart, axis=0)).T
            for k in range(8):
                q = base + start + k
                both = found[k * 16 : k * 16 + 8] + found[k * 16 + 8 : k * 16 + 16]
                tile = owner[q]
                rank = taken[tile]
                taken[tile] = rank + 1
                slot = tile * CAP + rank
                slot_out[q] = slot
                ident = jnp.full((4, 128), local[q], jnp.int32).astype(F32)
                out[slot] = jnp.where(mark, ident, both[0:4])
        return c

    lax.fori_loop(0, blocks // DEPOSIT_GROUP, group, 0)


def swap_groups(v):
    row = lax.broadcasted_iota(jnp.int32, v.shape, 1)
    grp = lax.broadcasted_iota(jnp.int32, v.shape, 2) // 16
    for s in range(3):
        step = 1 << s
        ra, gb = (row >> s) & 1, (grp >> s) & 1
        up = pltpu.roll(pltpu.roll(v, 8 - step, 1), 16 * step, 2)
        dn = pltpu.roll(pltpu.roll(v, step, 1), 128 - 16 * step, 2)
        v = jnp.where(ra == gb, v, jnp.where(ra < gb, up, dn))
    return v


def places(sx, sy):
    return [
        (bx * 2, slice(by * 4, by * 4 + 4), slice(h * 128, h * 128 + 128))
        for bx in range(sx // 2)
        for by in range(sy // 4)
        for h in range(2)
    ]


def to_bricks(grid, m):
    tiles = [jnp.concatenate([grid[m, x, y, z], grid[m, x + 1, y, z]], axis=0) for x, y, z in places(*grid.shape[1:3])]
    return swap_groups(jnp.stack(tiles, axis=0)).reshape(len(tiles) * 8, 128)


def old_kernel(fv, sent, bricks, around, inner, grid):
    around[...] = sent[96:144, :]
    sx, sy, sz = fv.shape[1:]
    yrow = lax.broadcasted_iota(jnp.int32, (sy, sz), 0)
    zlane = lax.broadcasted_iota(jnp.int32, (sy, sz), 1)
    zero = jnp.zeros((sy, sz), F32)
    for m in range(3):
        bricks[m] = to_bricks(fv, m)
        for x in range(sx):
            f = fv[m, x]
            beside = (fv[m, x + 1] if x < sx - 1 else zero) + (fv[m, x - 1] if x > 0 else zero)
            beside = beside + jnp.where(yrow == sy - 1, 0.0, pltpu.roll(f, sy - 1, 0))
            beside = beside + jnp.where(yrow == 0, 0.0, pltpu.roll(f, 1, 0))
            beside = beside + jnp.where(zlane == sz - 1, 0.0, pltpu.roll(f, sz - 1, 1))
            beside = beside + jnp.where(zlane == 0, 0.0, pltpu.roll(f, 1, 1))
            grid[m, x] = f + 0.1 * (beside - 6.0 * f)
    for m in range(3):
        inner[m] = to_bricks(grid, m)


def spread_kernel(side, inner, first_x, second_x, first_y, second_y, bricks):
    sx, sz = first_y.shape[1:]
    sy = 16
    odd = side[0].astype(F32)
    odd_y = jnp.full((sx, sz), side[1], jnp.int32) == 1
    row4 = lax.broadcasted_iota(jnp.int32, (4, 128), 0)
    zero = jnp.zeros((4, 128), F32)
    for m in range(3):
        lefts = 0.1 * jnp.where(odd_y, first_y[m], second_y[m])
        rights = 0.1 * jnp.where(odd_y, second_y[m], first_y[m])
        tiles, rows = [], []
        for i, (x0, y, z) in enumerate(places(sx, sy)):
            if 0 < x0 < sx - 2 and 0 < y.start < sy - 4:
                bricks[m, i * 8 : i * 8 + 8] = inner[m, i * 8 : i * 8 + 8]
                continue
            halves = []
            for x in (x0, x0 + 1):
                part = zero
                if x in (0, sx - 1):
                    at = (m * 2 + z.start // 128) * 16
                    first = first_x[at + y.start : at + y.stop, :]
                    second = second_x[at + y.start : at + y.stop, :]
                    keep = odd if x == 0 else 1.0 - odd
                    part = 0.1 * (keep * first + (1.0 - keep) * second)
                if y.start == 0:
                    part = part + jnp.where(row4 == 0, jnp.broadcast_to(lefts[x : x + 1, z], (4, 128)), 0.0)
                if y.stop == sy:
                    part = part + jnp.where(row4 == 3, jnp.broadcast_to(rights[x : x + 1, z], (4, 128)), 0.0)
                halves.append(part)
            tiles.append(jnp.concatenate(halves, axis=0))
            rows.append(i * 8)
        moved = swap_groups(jnp.stack(tiles, axis=0))
        for k, at in enumerate(rows):
            bricks[m, at : at + 8] = inner[m, at : at + 8] + moved[k]


def fluid_kernel(recv, old, spread, answer, fluid, done):
    done[...] = jnp.zeros(done.shape, F32)
    slots = recv.shape[0] // 4
    bricks = old.shape[1]
    count = recv[pl.ds(0, slots, stride=4), :]
    lane = lax.broadcasted_iota(jnp.int32, (slots, 128), 1)
    ident = count[:, 127:128]
    ident_row = count.T[127:128, :]
    wide = lax.broadcasted_iota(jnp.int32, (slots, bricks), 1).astype(F32)
    by_slot = (wide == jnp.broadcast_to(ident, (slots, bricks))).astype(F32).astype(BF16)
    tall = lax.broadcasted_iota(jnp.int32, (bricks, slots), 0).astype(F32)
    by_brick = (tall == jnp.broadcast_to(ident_row, (bricks, slots))).astype(F32).astype(BF16)
    parts = [jnp.where(lane == 127, 1.0, count).astype(BF16)]
    for m in range(3):
        parts += list(split2(recv[pl.ds(m + 1, slots, stride=4), :]))
    summed = dot(by_brick, jnp.concatenate(parts, axis=1))
    cnt = summed[:, 0:128]
    momentum = [summed[:, (1 + 2 * m) * 128 : (2 + 2 * m) * 128] + summed[:, (2 + 2 * m) * 128 : (3 + 2 * m) * 128] for m in range(3)]
    last = lax.broadcasted_iota(jnp.int32, (bricks, 128), 1) == 127
    others = jnp.sum(jnp.where(last, 0.0, cnt), axis=1, keepdims=True)
    cnt = jnp.where(last, 128.0 * cnt - others, cnt)
    solid = 0.5 * cnt
    voids = 1.0 - 0.6 * solid / (1.0 + solid)
    beta = (1.0 - voids) / (voids * voids)
    scale = 0.15 * beta
    table = []
    for m in range(3):
        new = spread[m] + scale * (momentum[m] - cnt * old[m])
        table += list(split2(new))
        moved = swap_groups(new.reshape(bricks // 8, 8, 128))
        for i, (x, y, z) in enumerate(places(*fluid.shape[1:3])):
            fluid[m, x, y, z] = moved[i, 0:4]
            fluid[m, x + 1, y, z] = moved[i, 4:8]
    table += list(split2(beta))
    found = dot(by_slot, jnp.concatenate(table, axis=1))
    for c in range(4):
        answer[pl.ds(c, slots, stride=4), :] = (
            found[:, 2 * c * 128 : (2 * c + 1) * 128] + found[:, (2 * c + 1) * 128 : (2 * c + 2) * 128]
        )


def feature_rows(x):
    hi, lo, both = [], [], []
    for m in range(3):
        u = x[m] - 0.5
        h = u.astype(BF16).astype(F32)
        l = (u - h).astype(BF16).astype(F32)
        hi.append(h)
        lo.append(l)
        both.append(h + l)
    return hi, lo, both, both[0] * both[0] + both[1] * both[1] + both[2] * both[2]


def split3(n):
    a = n.astype(BF16).astype(F32)
    b = (n - a).astype(BF16).astype(F32)
    return a, b, n - a - b


def order_pair(first, second, ordered, p, own):
    n = first.shape[1]
    b = second[1, p]
    inside = (b < n // 2).astype(jnp.int32)
    at = jnp.where(inside == 1, own, n - 1 - p + own)
    ordered[at] = first[1, p]
    ordered[n + at] = b
    return own + inside


def features(side, pos, listed, feat_b, feat_a):
    blocks = pos.shape[1]
    one = jnp.ones((8, 128), F32)
    zero = jnp.zeros((8, 128), F32)

    def put(ref, q0, feats):
        for k, v in enumerate(feats):
            ref[pl.ds(q0 * 16 + k, 8, stride=16), :] = v

    def own(g, c):
        q0 = pl.multiple_of(g * 8, 8)
        hi, lo, both, norm = feature_rows([pos[m, pl.ds(q0, 8), :] for m in range(3)])
        n = split3(norm)
        put(feat_b, q0, hi + [one, n[0], n[1], n[2], one] + lo + [one, zero, zero, zero, zero])
        n = split3(norm + EPS2)
        h2, l2 = [-2.0 * v for v in hi], [-2.0 * v for v in lo]
        put(feat_a, q0, h2 + [n[0], one, one, one, n[1]] + l2 + [n[2], zero, zero, zero, zero])
        return c

    lax.fori_loop(0, blocks // 8, own, 0, unroll=2)
    for i, refs in enumerate(listed):
        upper = side[0] if i else 1 - side[0]
        for g in range(2):
            hi, lo, _, norm = feature_rows([sum(ref[at + m * 16 + g * 8 : at + m * 16 + g * 8 + 8, :] for ref, at in refs) for m in range(3)])
            n = split3(norm)
            put(feat_b, pl.multiple_of(blocks + upper * 16 + g * 8, 8), hi + [one, n[0], n[1], n[2], one] + lo + [one, zero, zero, zero, zero])


def push_pairs(pair, begin, end, group, push, feat_b, feat_a, beside=lambda p, c: c):
    top = lax.broadcasted_iota(jnp.int32, (8, 128), 0) < 3

    def one_pair(p):
        a, b = pair(p)
        fb = feat_b[pl.ds(pl.multiple_of(b * 16, 16), 16), :]
        fa = feat_a[pl.ds(pl.multiple_of(a * 16, 16), 16), :]
        x, y = fa[0:8], fa[8:16]
        z = jnp.where(top, y, 0.0)
        ga = jnp.concatenate([x, jnp.where(top, x, y), z, z], axis=0).astype(BF16)
        lhs = fb.astype(BF16)
        r2 = dot(jnp.concatenate([lhs, lhs], axis=0), ga, ((0,), (0,)))
        w = jnp.maximum(lax.rsqrt(jnp.maximum(r2, EPS2)) - 4.0, 0.0)
        res = dot(jnp.concatenate([lhs, lhs], axis=1), jnp.concatenate(split2(w), axis=0))
        total = jnp.broadcast_to(res[3:4], (8, 128))
        return a, (-0.5) * (x + z) * total - (res[0:8] + res[8:16])

    def pairs(g, c):
        done = []
        for k in range(group):
            done.append(one_pair(g * group + k))
            c = beside(g * group + k, c)
        for a, f in done:
            rows = pl.ds(pl.multiple_of(a * 8, 8), 8)
            push[rows, :] = push[rows, :] + f
        return c

    return lax.fori_loop(begin, end, pairs, jnp.int32(0))


def push_kernel(side, first, second, slot, pos, listed_a, listed_b, around, after, push, slot_out, ordered, feat_b, feat_a):
    def hand_on(q, c):
        slot_out[q] = slot[q]
        return c

    lax.fori_loop(0, slot.shape[0], hand_on, 0, unroll=8)
    listed = (((listed_a, 96),), ((listed_b, 96), (around, 0)))
    features(side, pos, listed, feat_b, feat_a)
    push[...] = jnp.zeros(push.shape, F32)
    groups = first.shape[1] // PAIR_GROUP
    order = functools.partial(order_pair, first, second, ordered)
    own = push_pairs(lambda p: (first[0, p], second[0, p]), 0, groups, PAIR_GROUP, push, feat_b, feat_a, order)
    ordered[2 * first.shape[1]] = own // ORDERED_GROUP


def advance(pos, vel, push, flow, pos_out, vel_out):
    blocks = pos.shape[1]
    drift = 2.0 * flow[pl.ds(3, blocks, stride=8), :]
    for m in range(3):
        v = vel[m]
        force = 2.5 * push[pl.ds(m, blocks, stride=8), :] + drift * (flow[pl.ds(m, blocks, stride=8), :] - v)
        if m == 2:
            force = force - 1.0
        v = v + 0.1 * force
        vel_out[m] = v
        pos_out[m] = pos[m] + 0.1 * v


def pick(hot, v):
    v = jnp.concatenate([v, v], axis=0)
    hi = v.astype(BF16).astype(F32)
    both = dot(jnp.concatenate([hi, v - hi], axis=0).astype(BF16), hot)
    return both[0:8] + both[8:16]


def pick_kernel(side, slot, halo, back, cell, pos, vel, push, flow, pos_out, vel_out, first_x, second_x):
    def group(g, c):
        base = pl.multiple_of(g * BLOCK_GROUP, BLOCK_GROUP)
        cells = cell[pl.ds(base, BLOCK_GROUP), :]
        for k in range(BLOCK_GROUP):
            q = base + k
            flow[pl.ds(pl.multiple_of(q * 8, 8), 8), :] = pick(onehot_cells(cells[k : k + 1, :]), back[slot[q]])
        return c

    lax.fori_loop(0, cell.shape[0] // BLOCK_GROUP, group, 0)
    advance(pos, vel, push, flow, pos_out, vel_out)
    put_listed(halo, 1 - side[0], pos_out, first_x, 0)
    put_listed(halo, side[0], pos_out, second_x, 0)


def inner_kernel(ordered, pos, push, feat_b, feat_a):
    n = pos.shape[1] * 2
    features(None, pos, (), feat_b, feat_a)
    push[...] = jnp.zeros(push.shape, F32)
    push_pairs(lambda p: (ordered[p], ordered[n + p]), 0, ordered[2 * n], ORDERED_GROUP, push, feat_b, feat_a)


def last_kernel(side, ordered, pos, vel, listed_a, listed_b, flow, inner, pos_out, vel_out, push, feat_b, feat_a):
    n = pos.shape[1] * 2
    features(side, pos, (((listed_a, 0),), ((listed_b, 0),)), feat_b, feat_a)
    push[...] = inner[...]
    groups = n // ORDERED_GROUP
    push_pairs(lambda p: (ordered[p], ordered[n + p]), ordered[2 * n], groups, ORDERED_GROUP, push, feat_b, feat_a)
    advance(pos, vel, push, flow, pos_out, vel_out)


def call(kernel, in_specs, out_shape, out_specs, scratch=(), micros=1, vmem=20 * 1024 * 1024):
    return pl.pallas_call(
        kernel,
        in_specs=in_specs,
        out_shape=out_shape,
        out_specs=out_specs,
        scratch_shapes=list(scratch),
        compiler_params=pltpu.CompilerParams(vmem_limit_bytes=vmem),
        cost_estimate=pl.CostEstimate(flops=micros * 1_000_000_000, bytes_accessed=micros * 3_000_000, transcendentals=0),
    )


def shape(*dims, dtype=F32):
    return jax.ShapeDtypeStruct(dims, dtype)


def per_device(
    fluid_vel,
    part_pos,
    part_vel,
    brick_owner,
    brick_local,
    cell_in_brick,
    pair_self,
    pair_other,
    halo_list,
):
    nx, ny = lax.axis_size("gx"), lax.axis_size("gy")
    tiles = nx * ny
    blocks = part_pos.shape[0]
    slots = tiles * CAP
    sx, sy, sz = fluid_vel.shape[1:]
    pos = jnp.transpose(part_pos, (1, 0, 2))
    vel = jnp.transpose(part_vel, (1, 0, 2))

    send, slot, placed = call(
        deposit_kernel,
        [HBM] * 4,
        [shape(slots, 4, 128), shape(blocks, dtype=jnp.int32), shape(8, 128)],
        [VMEM, SMEM, VMEM],
        [
            pltpu.SMEM((tiles,), jnp.int32),
            pltpu.SMEM((blocks,), jnp.int32),
            pltpu.SMEM((blocks,), jnp.int32),
            pltpu.VMEM((blocks, 128), jnp.int32),
            pltpu.VMEM((3, blocks, 128), F32),
            pltpu.SemaphoreType.DMA((4,)),
        ],
        7,
        63_000_000,
    )(brick_owner[:, 0], brick_local, cell_in_brick, vel)
    recv = lax.all_to_all(send.reshape(slots * 4, 128), ("gx", "gy"), split_axis=0, concat_axis=0, tiled=True)

    me_x, me_y = lax.axis_index("gx"), lax.axis_index("gy")
    side = jnp.stack([me_x % 2, me_y % 2]).astype(jnp.int32)
    first_x, second_x, first_y, second_y = call(
        faces_kernel,
        [SMEM, SMEM, VMEM, VMEM, VMEM],
        [shape(144, 128), shape(144, 128), shape(3, sx, sz), shape(3, sx, sz)],
        [VMEM] * 4,
    )(side, halo_list, fluid_vel, pos, placed)
    bricks = sx // 2 * (sy // 4) * (sz // 16)
    old, around, inner = call(
        old_kernel,
        [VMEM, VMEM],
        [shape(3, bricks, 128), shape(48, 128), shape(3, bricks, 128)],
        [VMEM] * 3,
        [pltpu.VMEM((3, sx, sy, sz), F32)],
        2,
    )(fluid_vel, second_x)
    perms_x, perms_y = swaps(nx, True), swaps(ny, False)
    first_x = lax.ppermute(first_x, "gx", perms_x[0])
    second_x = lax.ppermute(second_x, "gx", perms_x[1][1:-1])
    around = lax.ppermute(around, "gx", [(0, nx - 1), (nx - 1, 0)])
    first_y = lax.ppermute(first_y, "gy", perms_y[0])
    second_y = lax.ppermute(second_y, "gy", perms_y[1])

    spread = call(
        spread_kernel,
        [SMEM] + [VMEM] * 5,
        shape(3, bricks, 128),
        VMEM,
    )(side, inner, first_x, second_x, first_y, second_y)
    answer, fluid, stepped = call(
        fluid_kernel,
        [VMEM] * 3,
        [shape(slots * 4, 128), shape(3, sx, sy, sz), shape(8, 128)],
        [VMEM] * 3,
        (),
        3,
    )(recv, old, spread)
    back = lax.all_to_all(answer, ("gx", "gy"), split_axis=0, concat_axis=0, tiled=True).reshape(slots, 4, 128)
    pair_scratch = [pltpu.VMEM(((blocks + 32) * 16, 128), F32), pltpu.VMEM((blocks * 16, 128), F32)]
    push, slot, ordered = call(
        push_kernel,
        [SMEM] * 4 + [VMEM] * 5,
        [
            shape(blocks * 8, 128),
            shape(blocks, dtype=jnp.int32),
            shape(2 * pair_self.shape[1] + 128, dtype=jnp.int32),
        ],
        [VMEM, SMEM, SMEM],
        pair_scratch,
        14,
    )(side, pair_self, pair_other, slot, pos, first_x, second_x, around, stepped)

    flow, pos, vel, listed_a, listed_b = call(
        pick_kernel,
        [SMEM] * 3 + [VMEM] * 5,
        [shape(blocks * 8, 128), shape(3, blocks, 128), shape(3, blocks, 128), shape(48, 128), shape(48, 128)],
        [VMEM] * 5,
        (),
        4,
    )(side, slot, halo_list, back, cell_in_brick, pos, vel, push)
    listed_a = lax.ppermute(listed_a, "gx", perms_x[0])
    listed_b = lax.ppermute(listed_b, "gx", perms_x[1])
    inner = call(
        inner_kernel,
        [SMEM, VMEM],
        shape(blocks * 8, 128),
        VMEM,
        pair_scratch,
        10,
    )(ordered, pos)
    pos, vel = call(
        last_kernel,
        [SMEM] * 2 + [VMEM] * 6,
        [shape(3, blocks, 128), shape(3, blocks, 128)],
        [VMEM] * 2,
        [pltpu.VMEM((blocks * 8, 128), F32)] + pair_scratch,
        5,
    )(side, ordered, pos, vel, listed_a, listed_b, flow, inner)
    return fluid, jnp.transpose(pos, (1, 0, 2)), jnp.transpose(vel, (1, 0, 2))


def solution(mesh):
    in_specs = (
        P(None, "gx", "gy", None),
        P(("gx", "gy"), None, None),
        P(("gx", "gy"), None, None),
        P(("gx", "gy"), None),
        P(("gx", "gy")),
        P(("gx", "gy"), None),
        P(None, ("gx", "gy")),
        P(None, ("gx", "gy")),
        P(("gx", "gy")),
    )
    out_specs = (
        P(None, "gx", "gy", None),
        P(("gx", "gy"), None, None),
        P(("gx", "gy"), None, None),
    )
    return jax.shard_map(
        per_device, mesh=mesh, in_specs=in_specs, out_specs=out_specs, check_vma=False
    )
```

```python
import functools

import jax
import jax.numpy as jnp
from jax import lax
from jax.experimental import pallas as pl
from jax.experimental.pallas import tpu as pltpu
from jax.sharding import PartitionSpec as P

F32 = jnp.float32
BF16 = jnp.bfloat16
PAIR_GROUP = 256
INNER_GROUP = 384
LAST_GROUP = 128
BLOCK_GROUP = 128
DEPOSIT_GROUP = 128
CAP = 4
EPS2 = 0.0025
VMEM = pl.BlockSpec(memory_space=pltpu.VMEM)
SMEM = pl.BlockSpec(memory_space=pltpu.SMEM)
HBM = pl.BlockSpec(memory_space=pltpu.HBM)


def split2(x):
    hi = x.astype(BF16)
    return hi, (x - hi.astype(F32)).astype(BF16)


def onehot_cells(row):
    cells = lax.broadcasted_iota(jnp.int32, (128, 128), 0)
    return (cells == jnp.broadcast_to(row, (128, 128))).astype(F32).astype(BF16)


def dot(a, b, dims=((1,), (0,))):
    return lax.dot_general(a, b, (dims, ((), ())), preferred_element_type=F32)


def swaps(n, closed):
    first = [(i, i ^ 1) for i in range(n)]
    second = [(i, (i + 1 if i % 2 else i - 1) % n) for i in range(n)]
    return first, (second if closed else second[1:-1])


def put_listed(halo, half, pos, out, at):
    for j in range(16):
        q = halo[half * 16 + j]
        for m in range(3):
            out[at + m * 16 + j : at + m * 16 + j + 1, :] = pos[m, pl.ds(q, 1), :]


def faces_kernel(side, halo, fv, pos, after, first_x, second_x, first_y, second_y):
    sx, sy, sz = fv.shape[1:]
    for out, upper in ((first_x, 1 - side[0]), (second_x, side[0])):
        x = upper * (sx - 1)
        for m in range(3):
            for h in range(2):
                out[(m * 2 + h) * 16 : (m * 2 + h + 1) * 16, :] = fv[m, x, :, h * 128 : (h + 1) * 128]
        put_listed(halo, upper, pos, out, 96)
    odd = jnp.full((sx, sz), side[1], jnp.int32) == 1
    for m in range(3):
        begin, end = fv[m, :, 0, :], fv[m, :, sy - 1, :]
        first_y[m] = jnp.where(odd, begin, end)
        second_y[m] = jnp.where(odd, end, begin)


def deposit_kernel(owner_in, local_in, cell_in, vel_in, out, slot_out, done, taken, owner, local, cell, vel, sems):
    blocks = cell.shape[0]
    copies = [
        pltpu.make_async_copy(src, dst, sems.at[i])
        for i, (src, dst) in enumerate(((vel_in, vel), (cell_in, cell), (owner_in, owner), (local_in, local)))
    ]
    for c in copies:
        c.start()
    lanes = lax.broadcasted_iota(jnp.int32, (4, 128), 1)
    rows4 = lax.broadcasted_iota(jnp.int32, (4, 128), 0)
    mark = (lanes == 127) & (rows4 == 0)
    done[...] = jnp.zeros(done.shape, F32)
    out[...] = jnp.broadcast_to(jnp.where(mark, -1.0, 0.0).astype(F32)[None], out.shape)

    def clear(t, c):
        taken[t] = 0
        return c

    lax.fori_loop(0, taken.shape[0], clear, 0, unroll=8)
    r8 = lax.broadcasted_iota(jnp.int32, (8, 128), 0)
    lane16 = lax.broadcasted_iota(jnp.int32, (128, 128), 1) // 16
    for c in copies:
        c.wait()

    def group(g, c):
        base = pl.multiple_of(g * DEPOSIT_GROUP, DEPOSIT_GROUP)
        cells = cell[pl.ds(base, DEPOSIT_GROUP), :]
        v = [vel[m, pl.ds(base, DEPOSIT_GROUP), :] for m in range(3)]
        for start in range(0, DEPOSIT_GROUP, 8):
            loads, hots = [], []
            for k in range(start, start + 8):
                rows = [jnp.broadcast_to(v[m][k : k + 1, :], (8, 128)) for m in range(3)]
                load = jnp.where(r8 == 1, rows[0], jnp.where(r8 == 2, rows[1], rows[2]))
                load = jnp.where(r8 == 0, 1.0, jnp.where(r8 < 4, load, 0.0))
                hi = load.astype(BF16).astype(F32)
                loads += [hi, load - hi]
                hots.append(onehot_cells(cells[k : k + 1, :]))
            turned = jnp.concatenate(loads, axis=0).T
            turned = turned.astype(BF16)
            apart = [jnp.where(lane16 == k, turned, jnp.zeros_like(turned)) for k in range(8)]
            found = dot(jnp.concatenate(hots, axis=1), jnp.concatenate(apart, axis=0)).T
            for k in range(8):
                q = base + start + k
                both = found[k * 16 : k * 16 + 8] + found[k * 16 + 8 : k * 16 + 16]
                tile = owner[q]
                rank = taken[tile]
                taken[tile] = rank + 1
                slot = tile * CAP + rank
                slot_out[q] = slot
                ident = jnp.full((4, 128), local[q], jnp.int32).astype(F32)
                out[slot] = jnp.where(mark, ident, both[0:4])
        return c

    lax.fori_loop(0, blocks // DEPOSIT_GROUP, group, 0)


def swap_groups(v):
    row = lax.broadcasted_iota(jnp.int32, v.shape, 1)
    grp = lax.broadcasted_iota(jnp.int32, v.shape, 2) // 16
    for s in range(3):
        step = 1 << s
        ra, gb = (row >> s) & 1, (grp >> s) & 1
        up = pltpu.roll(pltpu.roll(v, 8 - step, 1), 16 * step, 2)
        dn = pltpu.roll(pltpu.roll(v, step, 1), 128 - 16 * step, 2)
        v = jnp.where(ra == gb, v, jnp.where(ra < gb, up, dn))
    return v


def places(sx, sy):
    return [
        (bx * 2, slice(by * 4, by * 4 + 4), slice(h * 128, h * 128 + 128))
        for bx in range(sx // 2)
        for by in range(sy // 4)
        for h in range(2)
    ]


def to_bricks(grid, m):
    tiles = [jnp.concatenate([grid[m, x, y, z], grid[m, x + 1, y, z]], axis=0) for x, y, z in places(*grid.shape[1:3])]
    return swap_groups(jnp.stack(tiles, axis=0)).reshape(len(tiles) * 8, 128)


def old_kernel(fv, sent, bricks, around, inner, grid):
    around[...] = sent[96:144, :]
    sx, sy, sz = fv.shape[1:]
    yrow = lax.broadcasted_iota(jnp.int32, (sy, sz), 0)
    zlane = lax.broadcasted_iota(jnp.int32, (sy, sz), 1)
    zero = jnp.zeros((sy, sz), F32)
    for m in range(3):
        bricks[m] = to_bricks(fv, m)
        for x in range(sx):
            f = fv[m, x]
            beside = (fv[m, x + 1] if x < sx - 1 else zero) + (fv[m, x - 1] if x > 0 else zero)
            beside = beside + jnp.where(yrow == sy - 1, 0.0, pltpu.roll(f, sy - 1, 0))
            beside = beside + jnp.where(yrow == 0, 0.0, pltpu.roll(f, 1, 0))
            beside = beside + jnp.where(zlane == sz - 1, 0.0, pltpu.roll(f, sz - 1, 1))
            beside = beside + jnp.where(zlane == 0, 0.0, pltpu.roll(f, 1, 1))
            grid[m, x] = f + 0.1 * (beside - 6.0 * f)
    for m in range(3):
        inner[m] = to_bricks(grid, m)


def spread_kernel(side, inner, first_x, second_x, first_y, second_y, bricks):
    sx, sz = first_y.shape[1:]
    sy = 16
    odd = side[0].astype(F32)
    odd_y = jnp.full((sx, sz), side[1], jnp.int32) == 1
    row4 = lax.broadcasted_iota(jnp.int32, (4, 128), 0)
    zero = jnp.zeros((4, 128), F32)
    for m in range(3):
        lefts = 0.1 * jnp.where(odd_y, first_y[m], second_y[m])
        rights = 0.1 * jnp.where(odd_y, second_y[m], first_y[m])
        tiles, rows = [], []
        for i, (x0, y, z) in enumerate(places(sx, sy)):
            if 0 < x0 < sx - 2 and 0 < y.start < sy - 4:
                bricks[m, i * 8 : i * 8 + 8] = inner[m, i * 8 : i * 8 + 8]
                continue
            halves = []
            for x in (x0, x0 + 1):
                part = zero
                if x in (0, sx - 1):
                    at = (m * 2 + z.start // 128) * 16
                    first = first_x[at + y.start : at + y.stop, :]
                    second = second_x[at + y.start : at + y.stop, :]
                    keep = odd if x == 0 else 1.0 - odd
                    part = 0.1 * (keep * first + (1.0 - keep) * second)
                if y.start == 0:
                    part = part + jnp.where(row4 == 0, jnp.broadcast_to(lefts[x : x + 1, z], (4, 128)), 0.0)
                if y.stop == sy:
                    part = part + jnp.where(row4 == 3, jnp.broadcast_to(rights[x : x + 1, z], (4, 128)), 0.0)
                halves.append(part)
            tiles.append(jnp.concatenate(halves, axis=0))
            rows.append(i * 8)
        moved = swap_groups(jnp.stack(tiles, axis=0))
        for k, at in enumerate(rows):
            bricks[m, at : at + 8] = inner[m, at : at + 8] + moved[k]


def fluid_kernel(recv, old, spread, answer, fluid, done):
    done[...] = jnp.zeros(done.shape, F32)
    slots = recv.shape[0] // 4
    bricks = old.shape[1]
    count = recv[pl.ds(0, slots, stride=4), :]
    lane = lax.broadcasted_iota(jnp.int32, (slots, 128), 1)
    ident = count[:, 127:128]
    ident_row = count.T[127:128, :]
    wide = lax.broadcasted_iota(jnp.int32, (slots, bricks), 1).astype(F32)
    by_slot = (wide == jnp.broadcast_to(ident, (slots, bricks))).astype(F32).astype(BF16)
    tall = lax.broadcasted_iota(jnp.int32, (bricks, slots), 0).astype(F32)
    by_brick = (tall == jnp.broadcast_to(ident_row, (bricks, slots))).astype(F32).astype(BF16)
    parts = [jnp.where(lane == 127, 1.0, count).astype(BF16)]
    for m in range(3):
        parts += list(split2(recv[pl.ds(m + 1, slots, stride=4), :]))
    summed = dot(by_brick, jnp.concatenate(parts, axis=1))
    cnt = summed[:, 0:128]
    momentum = [summed[:, (1 + 2 * m) * 128 : (2 + 2 * m) * 128] + summed[:, (2 + 2 * m) * 128 : (3 + 2 * m) * 128] for m in range(3)]
    last = lax.broadcasted_iota(jnp.int32, (bricks, 128), 1) == 127
    others = jnp.sum(jnp.where(last, 0.0, cnt), axis=1, keepdims=True)
    cnt = jnp.where(last, 128.0 * cnt - others, cnt)
    solid = 0.5 * cnt
    voids = 1.0 - 0.6 * solid / (1.0 + solid)
    beta = (1.0 - voids) / (voids * voids)
    scale = 0.15 * beta
    table = []
    for m in range(3):
        new = spread[m] + scale * (momentum[m] - cnt * old[m])
        table += list(split2(new))
        moved = swap_groups(new.reshape(bricks // 8, 8, 128))
        for i, (x, y, z) in enumerate(places(*fluid.shape[1:3])):
            fluid[m, x, y, z] = moved[i, 0:4]
            fluid[m, x + 1, y, z] = moved[i, 4:8]
    table += list(split2(beta))
    found = dot(by_slot, jnp.concatenate(table, axis=1))
    for c in range(4):
        answer[pl.ds(c, slots, stride=4), :] = (
            found[:, 2 * c * 128 : (2 * c + 1) * 128] + found[:, (2 * c + 1) * 128 : (2 * c + 2) * 128]
        )


def feature_rows(x):
    hi, lo, both = [], [], []
    for m in range(3):
        u = x[m] - 0.5
        h = u.astype(BF16).astype(F32)
        l = (u - h).astype(BF16).astype(F32)
        hi.append(h)
        lo.append(l)
        both.append(h + l)
    return hi, lo, both, both[0] * both[0] + both[1] * both[1] + both[2] * both[2]


def split3(n):
    a = n.astype(BF16).astype(F32)
    b = (n - a).astype(BF16).astype(F32)
    return a, b, n - a - b


def order_pair(first, second, ordered, p, own):
    n = first.shape[1]
    b = second[1, p]
    inside = (b < n // 2).astype(jnp.int32)
    at = jnp.where(inside == 1, own, n - 1 - p + own)
    ordered[at] = first[1, p]
    ordered[n + at] = b
    return own + inside


def features(side, pos, listed, feat_b, feat_a):
    blocks = pos.shape[1]
    one = jnp.ones((8, 128), F32)
    zero = jnp.zeros((8, 128), F32)

    def put(ref, q0, feats):
        for k, v in enumerate(feats):
            ref[pl.ds(q0 * 16 + k, 8, stride=16), :] = v

    def own(g, c):
        q0 = pl.multiple_of(g * 8, 8)
        hi, lo, both, norm = feature_rows([pos[m, pl.ds(q0, 8), :] for m in range(3)])
        n = split3(norm)
        put(feat_b, q0, hi + [one, n[0], n[1], n[2], one] + lo + [one, zero, zero, zero, zero])
        n = split3(norm + EPS2)
        h2, l2 = [-2.0 * v for v in hi], [-2.0 * v for v in lo]
        put(feat_a, q0, h2 + [n[0], one, one, one, n[1]] + l2 + [n[2], zero, zero, zero, zero])
        return c

    lax.fori_loop(0, blocks // 8, own, 0, unroll=2)
    for i, refs in enumerate(listed):
        upper = side[0] if i else 1 - side[0]
        for g in range(2):
            hi, lo, _, norm = feature_rows([sum(ref[at + m * 16 + g * 8 : at + m * 16 + g * 8 + 8, :] for ref, at in refs) for m in range(3)])
            n = split3(norm)
            put(feat_b, pl.multiple_of(blocks + upper * 16 + g * 8, 8), hi + [one, n[0], n[1], n[2], one] + lo + [one, zero, zero, zero, zero])


def push_pairs(pair, begin, end, group, push, feat_b, feat_a, beside=lambda p, c: c):
    top = lax.broadcasted_iota(jnp.int32, (8, 128), 0) < 3

    def one_pair(p):
        a, b = pair(p)
        fb = feat_b[pl.ds(pl.multiple_of(b * 16, 16), 16), :]
        fa = feat_a[pl.ds(pl.multiple_of(a * 16, 16), 16), :]
        x, y = fa[0:8], fa[8:16]
        z = jnp.where(top, y, 0.0)
        ga = jnp.concatenate([x, jnp.where(top, x, y), z, z], axis=0).astype(BF16)
        lhs = fb.astype(BF16)
        r2 = dot(jnp.concatenate([lhs, lhs], axis=0), ga, ((0,), (0,)))
        w = jnp.maximum(lax.rsqrt(jnp.maximum(r2, EPS2)) - 4.0, 0.0)
        res = dot(jnp.concatenate([lhs, lhs], axis=1), jnp.concatenate(split2(w), axis=0))
        total = jnp.broadcast_to(res[3:4], (8, 128))
        return a, (-0.5) * (x + z) * total - (res[0:8] + res[8:16])

    def pairs(g, c):
        done = []
        for k in range(group):
            done.append(one_pair(g * group + k))
            c = beside(g * group + k, c)
        for a, f in done:
            rows = pl.ds(pl.multiple_of(a * 8, 8), 8)
            push[rows, :] = push[rows, :] + f
        return c

    return lax.fori_loop(begin, end, pairs, jnp.int32(0))


def push_kernel(side, first, second, slot, pos, listed_a, listed_b, around, after, push, slot_out, ordered, feat_b, feat_a):
    def hand_on(q, c):
        slot_out[q] = slot[q]
        return c

    lax.fori_loop(0, slot.shape[0], hand_on, 0, unroll=8)
    listed = (((listed_a, 96),), ((listed_b, 96), (around, 0)))
    features(side, pos, listed, feat_b, feat_a)
    push[...] = jnp.zeros(push.shape, F32)
    groups = first.shape[1] // PAIR_GROUP
    order = functools.partial(order_pair, first, second, ordered)
    own = push_pairs(lambda p: (first[0, p], second[0, p]), 0, groups, PAIR_GROUP, push, feat_b, feat_a, order)
    ordered[2 * first.shape[1]] = own // INNER_GROUP


def advance(pos, vel, push, air, pos_out, vel_out):
    blocks = pos.shape[1]
    for m in range(3):
        v = vel[m]
        force = 2.5 * push[pl.ds(m, blocks, stride=8), :] + air[3] * (air[m] - v)
        if m == 2:
            force = force - 1.0
        v = v + 0.1 * force
        vel_out[m] = v
        pos_out[m] = pos[m] + 0.1 * v


def pick(hot, v):
    v = jnp.concatenate([v, v], axis=0)
    hi = v.astype(BF16).astype(F32)
    both = dot(jnp.concatenate([hi, v - hi], axis=0).astype(BF16), hot)
    return both[0:8] + both[8:16]


def pick_kernel(side, slot, halo, back, cell, pos, vel, push, air, pos_out, vel_out, first_x, second_x, flow):
    def group(g, c):
        base = pl.multiple_of(g * BLOCK_GROUP, BLOCK_GROUP)
        cells = cell[pl.ds(base, BLOCK_GROUP), :]
        for k in range(BLOCK_GROUP):
            q = base + k
            flow[pl.ds(pl.multiple_of(q * 8, 8), 8), :] = pick(onehot_cells(cells[k : k + 1, :]), back[slot[q]])
        return c

    lax.fori_loop(0, cell.shape[0] // BLOCK_GROUP, group, 0)
    for m in range(3):
        air[m] = flow[pl.ds(m, cell.shape[0], stride=8), :]
    air[3] = 2.0 * flow[pl.ds(3, cell.shape[0], stride=8), :]
    advance(pos, vel, push, air, pos_out, vel_out)
    put_listed(halo, 1 - side[0], pos_out, first_x, 0)
    put_listed(halo, side[0], pos_out, second_x, 0)


def inner_kernel(ordered, pos, push, feat_b, feat_a):
    n = pos.shape[1] * 2
    features(None, pos, (), feat_b, feat_a)
    push[...] = jnp.zeros(push.shape, F32)
    push_pairs(lambda p: (ordered[p], ordered[n + p]), 0, ordered[2 * n], INNER_GROUP, push, feat_b, feat_a)


def last_kernel(side, ordered, pos, vel, listed_a, listed_b, air, inner, pos_out, vel_out, push, feat_b, feat_a):
    n = pos.shape[1] * 2
    features(side, pos, (((listed_a, 0),), ((listed_b, 0),)), feat_b, feat_a)
    push[...] = inner[...]
    begin = ordered[2 * n] * (INNER_GROUP // LAST_GROUP)
    push_pairs(lambda p: (ordered[p], ordered[n + p]), begin, n // LAST_GROUP, LAST_GROUP, push, feat_b, feat_a)
    advance(pos, vel, push, air, pos_out, vel_out)


def call(kernel, in_specs, out_shape, out_specs, scratch=(), micros=1, vmem=20 * 1024 * 1024):
    return pl.pallas_call(
        kernel,
        in_specs=in_specs,
        out_shape=out_shape,
        out_specs=out_specs,
        scratch_shapes=list(scratch),
        compiler_params=pltpu.CompilerParams(vmem_limit_bytes=vmem),
        cost_estimate=pl.CostEstimate(flops=micros * 1_000_000_000, bytes_accessed=micros * 3_000_000, transcendentals=0),
    )


def shape(*dims, dtype=F32):
    return jax.ShapeDtypeStruct(dims, dtype)


def per_device(
    fluid_vel,
    part_pos,
    part_vel,
    brick_owner,
    brick_local,
    cell_in_brick,
    pair_self,
    pair_other,
    halo_list,
):
    nx, ny = lax.axis_size("gx"), lax.axis_size("gy")
    tiles = nx * ny
    blocks = part_pos.shape[0]
    slots = tiles * CAP
    sx, sy, sz = fluid_vel.shape[1:]
    pos = jnp.transpose(part_pos, (1, 0, 2))
    vel = jnp.transpose(part_vel, (1, 0, 2))

    send, slot, placed = call(
        deposit_kernel,
        [HBM] * 4,
        [shape(slots, 4, 128), shape(blocks, dtype=jnp.int32), shape(8, 128)],
        [VMEM, SMEM, VMEM],
        [
            pltpu.SMEM((tiles,), jnp.int32),
            pltpu.SMEM((blocks,), jnp.int32),
            pltpu.SMEM((blocks,), jnp.int32),
            pltpu.VMEM((blocks, 128), jnp.int32),
            pltpu.VMEM((3, blocks, 128), F32),
            pltpu.SemaphoreType.DMA((4,)),
        ],
        7,
        63_000_000,
    )(brick_owner[:, 0], brick_local, cell_in_brick, vel)
    recv = lax.all_to_all(send.reshape(slots * 4, 128), ("gx", "gy"), split_axis=0, concat_axis=0, tiled=True)

    me_x, me_y = lax.axis_index("gx"), lax.axis_index("gy")
    side = jnp.stack([me_x % 2, me_y % 2]).astype(jnp.int32)
    first_x, second_x, first_y, second_y = call(
        faces_kernel,
        [SMEM, SMEM, VMEM, VMEM, VMEM],
        [shape(144, 128), shape(144, 128), shape(3, sx, sz), shape(3, sx, sz)],
        [VMEM] * 4,
    )(side, halo_list, fluid_vel, pos, placed)
    bricks = sx // 2 * (sy // 4) * (sz // 16)
    old, around, inner = call(
        old_kernel,
        [VMEM, VMEM],
        [shape(3, bricks, 128), shape(48, 128), shape(3, bricks, 128)],
        [VMEM] * 3,
        [pltpu.VMEM((3, sx, sy, sz), F32)],
        2,
    )(fluid_vel, second_x)
    perms_x, perms_y = swaps(nx, True), swaps(ny, False)
    first_x = lax.ppermute(first_x, "gx", perms_x[0])
    second_x = lax.ppermute(second_x, "gx", perms_x[1][1:-1])
    around = lax.ppermute(around, "gx", [(0, nx - 1), (nx - 1, 0)])
    first_y = lax.ppermute(first_y, "gy", perms_y[0])
    second_y = lax.ppermute(second_y, "gy", perms_y[1])

    spread = call(
        spread_kernel,
        [SMEM] + [VMEM] * 5,
        shape(3, bricks, 128),
        VMEM,
    )(side, inner, first_x, second_x, first_y, second_y)
    answer, fluid, stepped = call(
        fluid_kernel,
        [VMEM] * 3,
        [shape(slots * 4, 128), shape(3, sx, sy, sz), shape(8, 128)],
        [VMEM] * 3,
        (),
        3,
    )(recv, old, spread)
    back = lax.all_to_all(answer, ("gx", "gy"), split_axis=0, concat_axis=0, tiled=True).reshape(slots, 4, 128)
    pair_scratch = [pltpu.VMEM(((blocks + 32) * 16, 128), F32), pltpu.VMEM((blocks * 16, 128), F32)]
    push, slot, ordered = call(
        push_kernel,
        [SMEM] * 4 + [VMEM] * 5,
        [
            shape(blocks * 8, 128),
            shape(blocks, dtype=jnp.int32),
            shape(2 * pair_self.shape[1] + 128, dtype=jnp.int32),
        ],
        [VMEM, SMEM, SMEM],
        pair_scratch,
        14,
    )(side, pair_self, pair_other, slot, pos, first_x, second_x, around, stepped)

    air, pos, vel, listed_a, listed_b = call(
        pick_kernel,
        [SMEM] * 3 + [VMEM] * 5,
        [shape(4, blocks, 128), shape(3, blocks, 128), shape(3, blocks, 128), shape(48, 128), shape(48, 128)],
        [VMEM] * 5,
        [pltpu.VMEM((blocks * 8, 128), F32)],
        4,
    )(side, slot, halo_list, back, cell_in_brick, pos, vel, push)
    listed_a = lax.ppermute(listed_a, "gx", perms_x[0])
    listed_b = lax.ppermute(listed_b, "gx", perms_x[1])
    inner = call(
        inner_kernel,
        [SMEM, VMEM],
        shape(blocks * 8, 128),
        VMEM,
        pair_scratch,
        10,
    )(ordered, pos)
    pos, vel = call(
        last_kernel,
        [SMEM] * 2 + [VMEM] * 6,
        [shape(3, blocks, 128), shape(3, blocks, 128)],
        [VMEM] * 2,
        [pltpu.VMEM((blocks * 8, 128), F32)] + pair_scratch,
        5,
    )(side, ordered, pos, vel, listed_a, listed_b, air, inner)
    return fluid, jnp.transpose(pos, (1, 0, 2)), jnp.transpose(vel, (1, 0, 2))


def solution(mesh):
    in_specs = (
        P(None, "gx", "gy", None),
        P(("gx", "gy"), None, None),
        P(("gx", "gy"), None, None),
        P(("gx", "gy"), None),
        P(("gx", "gy")),
        P(("gx", "gy"), None),
        P(None, ("gx", "gy")),
        P(None, ("gx", "gy")),
        P(("gx", "gy")),
    )
    out_specs = (
        P(None, "gx", "gy", None),
        P(("gx", "gy"), None, None),
        P(("gx", "gy"), None, None),
    )
    return jax.shard_map(
        per_device, mesh=mesh, in_specs=in_specs, out_specs=out_specs, check_vma=False
    )
```

```python
import functools

import jax
import jax.numpy as jnp
from jax import lax
from jax.experimental import pallas as pl
from jax.experimental.pallas import tpu as pltpu
from jax.sharding import PartitionSpec as P

F32 = jnp.float32
BF16 = jnp.bfloat16
PAIR_GROUP = 256
INNER_GROUP = 384
LAST_GROUP = 128
BLOCK_GROUP = 256
DEPOSIT_GROUP = 128
CAP = 4
EPS2 = 0.0025
VMEM = pl.BlockSpec(memory_space=pltpu.VMEM)
SMEM = pl.BlockSpec(memory_space=pltpu.SMEM)
HBM = pl.BlockSpec(memory_space=pltpu.HBM)


def split2(x):
    hi = x.astype(BF16)
    return hi, (x - hi.astype(F32)).astype(BF16)


def onehot_cells(row):
    cells = lax.broadcasted_iota(jnp.int32, (128, 128), 0)
    return (cells == jnp.broadcast_to(row, (128, 128))).astype(F32).astype(BF16)


def dot(a, b, dims=((1,), (0,))):
    return lax.dot_general(a, b, (dims, ((), ())), preferred_element_type=F32)


def swaps(n, closed):
    first = [(i, i ^ 1) for i in range(n)]
    second = [(i, (i + 1 if i % 2 else i - 1) % n) for i in range(n)]
    return first, (second if closed else second[1:-1])


def put_listed(halo, half, pos, out, at):
    for j in range(16):
        q = halo[half * 16 + j]
        for m in range(3):
            out[at + m * 16 + j : at + m * 16 + j + 1, :] = pos[m, pl.ds(q, 1), :]


def faces_kernel(side, halo, fv, pos, after, first_x, second_x, first_y, second_y):
    sx, sy, sz = fv.shape[1:]
    for out, upper in ((first_x, 1 - side[0]), (second_x, side[0])):
        x = upper * (sx - 1)
        for m in range(3):
            for h in range(2):
                out[(m * 2 + h) * 16 : (m * 2 + h + 1) * 16, :] = fv[m, x, :, h * 128 : (h + 1) * 128]
        put_listed(halo, upper, pos, out, 96)
    odd = jnp.full((sx, sz), side[1], jnp.int32) == 1
    for m in range(3):
        begin, end = fv[m, :, 0, :], fv[m, :, sy - 1, :]
        first_y[m] = jnp.where(odd, begin, end)
        second_y[m] = jnp.where(odd, end, begin)


def deposit_kernel(owner_in, local_in, cell_in, vel_in, out, slot_out, done, taken, owner, local, cell, vel, sems):
    blocks = cell.shape[0]
    groups = blocks // DEPOSIT_GROUP
    lists = [pltpu.make_async_copy(owner_in, owner, sems.at[0]), pltpu.make_async_copy(local_in, local, sems.at[1])]
    parts = []
    for g in range(groups):
        some = pl.ds(g * DEPOSIT_GROUP, DEPOSIT_GROUP)
        parts.append(
            [
                pltpu.make_async_copy(cell_in.at[some, :], cell.at[some, :], sems.at[2 + 2 * g]),
                pltpu.make_async_copy(vel_in.at[:, some, :], vel.at[:, some, :], sems.at[3 + 2 * g]),
            ]
        )
    for c in lists + sum(parts, []):
        c.start()
    lanes = lax.broadcasted_iota(jnp.int32, (4, 128), 1)
    rows4 = lax.broadcasted_iota(jnp.int32, (4, 128), 0)
    mark = (lanes == 127) & (rows4 == 0)
    done[...] = jnp.zeros(done.shape, F32)
    out[...] = jnp.broadcast_to(jnp.where(mark, -1.0, 0.0).astype(F32)[None], out.shape)

    def clear(t, c):
        taken[t] = 0
        return c

    lax.fori_loop(0, taken.shape[0], clear, 0, unroll=8)
    r8 = lax.broadcasted_iota(jnp.int32, (8, 128), 0)
    lane16 = lax.broadcasted_iota(jnp.int32, (128, 128), 1) // 16
    for c in lists:
        c.wait()
    for g in range(groups):
        for c in parts[g]:
            c.wait()
        base = g * DEPOSIT_GROUP
        cells = cell[pl.ds(base, DEPOSIT_GROUP), :]
        v = [vel[m, pl.ds(base, DEPOSIT_GROUP), :] for m in range(3)]
        for start in range(0, DEPOSIT_GROUP, 8):
            loads, hots = [], []
            for k in range(start, start + 8):
                rows = [jnp.broadcast_to(v[m][k : k + 1, :], (8, 128)) for m in range(3)]
                load = jnp.where(r8 == 1, rows[0], jnp.where(r8 == 2, rows[1], rows[2]))
                load = jnp.where(r8 == 0, 1.0, jnp.where(r8 < 4, load, 0.0))
                hi = load.astype(BF16).astype(F32)
                loads += [hi, load - hi]
                hots.append(onehot_cells(cells[k : k + 1, :]))
            turned = jnp.concatenate(loads, axis=0).T
            turned = turned.astype(BF16)
            apart = [jnp.where(lane16 == k, turned, jnp.zeros_like(turned)) for k in range(8)]
            found = dot(jnp.concatenate(hots, axis=1), jnp.concatenate(apart, axis=0)).T
            for k in range(8):
                q = base + start + k
                both = found[k * 16 : k * 16 + 8] + found[k * 16 + 8 : k * 16 + 16]
                tile = owner[q]
                rank = taken[tile]
                taken[tile] = rank + 1
                slot = tile * CAP + rank
                slot_out[q] = slot
                ident = jnp.full((4, 128), local[q], jnp.int32).astype(F32)
                out[slot] = jnp.where(mark, ident, both[0:4])


def swap_groups(v):
    row = lax.broadcasted_iota(jnp.int32, v.shape, 1)
    grp = lax.broadcasted_iota(jnp.int32, v.shape, 2) // 16
    for s in range(3):
        step = 1 << s
        ra, gb = (row >> s) & 1, (grp >> s) & 1
        up = pltpu.roll(pltpu.roll(v, 8 - step, 1), 16 * step, 2)
        dn = pltpu.roll(pltpu.roll(v, step, 1), 128 - 16 * step, 2)
        v = jnp.where(ra == gb, v, jnp.where(ra < gb, up, dn))
    return v


def places(sx, sy):
    return [
        (bx * 2, slice(by * 4, by * 4 + 4), slice(h * 128, h * 128 + 128))
        for bx in range(sx // 2)
        for by in range(sy // 4)
        for h in range(2)
    ]


def to_bricks(grid, m):
    tiles = [jnp.concatenate([grid[m, x, y, z], grid[m, x + 1, y, z]], axis=0) for x, y, z in places(*grid.shape[1:3])]
    return swap_groups(jnp.stack(tiles, axis=0)).reshape(len(tiles) * 8, 128)


def old_kernel(fv, sent, bricks, around, inner, grid):
    around[...] = sent[96:144, :]
    sx, sy, sz = fv.shape[1:]
    yrow = lax.broadcasted_iota(jnp.int32, (sy, sz), 0)
    zlane = lax.broadcasted_iota(jnp.int32, (sy, sz), 1)
    zero = jnp.zeros((sy, sz), F32)
    for m in range(3):
        bricks[m] = to_bricks(fv, m)
        for x in range(sx):
            f = fv[m, x]
            beside = (fv[m, x + 1] if x < sx - 1 else zero) + (fv[m, x - 1] if x > 0 else zero)
            beside = beside + jnp.where(yrow == sy - 1, 0.0, pltpu.roll(f, sy - 1, 0))
            beside = beside + jnp.where(yrow == 0, 0.0, pltpu.roll(f, 1, 0))
            beside = beside + jnp.where(zlane == sz - 1, 0.0, pltpu.roll(f, sz - 1, 1))
            beside = beside + jnp.where(zlane == 0, 0.0, pltpu.roll(f, 1, 1))
            grid[m, x] = f + 0.1 * (beside - 6.0 * f)
    for m in range(3):
        inner[m] = to_bricks(grid, m)


def spread_kernel(side, inner, first_x, second_x, first_y, second_y, bricks):
    sx, sz = first_y.shape[1:]
    sy = 16
    odd = side[0].astype(F32)
    odd_y = jnp.full((sx, sz), side[1], jnp.int32) == 1
    row4 = lax.broadcasted_iota(jnp.int32, (4, 128), 0)
    zero = jnp.zeros((4, 128), F32)
    for m in range(3):
        lefts = 0.1 * jnp.where(odd_y, first_y[m], second_y[m])
        rights = 0.1 * jnp.where(odd_y, second_y[m], first_y[m])
        tiles, rows = [], []
        for i, (x0, y, z) in enumerate(places(sx, sy)):
            if 0 < x0 < sx - 2 and 0 < y.start < sy - 4:
                bricks[m, i * 8 : i * 8 + 8] = inner[m, i * 8 : i * 8 + 8]
                continue
            halves = []
            for x in (x0, x0 + 1):
                part = zero
                if x in (0, sx - 1):
                    at = (m * 2 + z.start // 128) * 16
                    first = first_x[at + y.start : at + y.stop, :]
                    second = second_x[at + y.start : at + y.stop, :]
                    keep = odd if x == 0 else 1.0 - odd
                    part = 0.1 * (keep * first + (1.0 - keep) * second)
                if y.start == 0:
                    part = part + jnp.where(row4 == 0, jnp.broadcast_to(lefts[x : x + 1, z], (4, 128)), 0.0)
                if y.stop == sy:
                    part = part + jnp.where(row4 == 3, jnp.broadcast_to(rights[x : x + 1, z], (4, 128)), 0.0)
                halves.append(part)
            tiles.append(jnp.concatenate(halves, axis=0))
            rows.append(i * 8)
        moved = swap_groups(jnp.stack(tiles, axis=0))
        for k, at in enumerate(rows):
            bricks[m, at : at + 8] = inner[m, at : at + 8] + moved[k]


def fluid_kernel(recv, old, spread, answer, fluid, done):
    done[...] = jnp.zeros(done.shape, F32)
    slots = recv.shape[0] // 4
    bricks = old.shape[1]
    count = recv[pl.ds(0, slots, stride=4), :]
    lane = lax.broadcasted_iota(jnp.int32, (slots, 128), 1)
    ident = count[:, 127:128]
    ident_row = count.T[127:128, :]
    wide = lax.broadcasted_iota(jnp.int32, (slots, bricks), 1).astype(F32)
    by_slot = (wide == jnp.broadcast_to(ident, (slots, bricks))).astype(F32).astype(BF16)
    tall = lax.broadcasted_iota(jnp.int32, (bricks, slots), 0).astype(F32)
    by_brick = (tall == jnp.broadcast_to(ident_row, (bricks, slots))).astype(F32).astype(BF16)
    parts = [jnp.where(lane == 127, 1.0, count).astype(BF16)]
    for m in range(3):
        parts += list(split2(recv[pl.ds(m + 1, slots, stride=4), :]))
    summed = dot(by_brick, jnp.concatenate(parts, axis=1))
    cnt = summed[:, 0:128]
    momentum = [summed[:, (1 + 2 * m) * 128 : (2 + 2 * m) * 128] + summed[:, (2 + 2 * m) * 128 : (3 + 2 * m) * 128] for m in range(3)]
    last = lax.broadcasted_iota(jnp.int32, (bricks, 128), 1) == 127
    others = jnp.sum(jnp.where(last, 0.0, cnt), axis=1, keepdims=True)
    cnt = jnp.where(last, 128.0 * cnt - others, cnt)
    solid = 0.5 * cnt
    voids = 1.0 - 0.6 * solid / (1.0 + solid)
    beta = (1.0 - voids) / (voids * voids)
    scale = 0.15 * beta
    table = []
    for m in range(3):
        new = spread[m] + scale * (momentum[m] - cnt * old[m])
        table += list(split2(new))
        moved = swap_groups(new.reshape(bricks // 8, 8, 128))
        for i, (x, y, z) in enumerate(places(*fluid.shape[1:3])):
            fluid[m, x, y, z] = moved[i, 0:4]
            fluid[m, x + 1, y, z] = moved[i, 4:8]
    table += list(split2(beta))
    found = dot(by_slot, jnp.concatenate(table, axis=1))
    for c in range(4):
        answer[pl.ds(c, slots, stride=4), :] = (
            found[:, 2 * c * 128 : (2 * c + 1) * 128] + found[:, (2 * c + 1) * 128 : (2 * c + 2) * 128]
        )


def feature_rows(x):
    hi, lo, both = [], [], []
    for m in range(3):
        u = x[m] - 0.5
        h = u.astype(BF16).astype(F32)
        l = (u - h).astype(BF16).astype(F32)
        hi.append(h)
        lo.append(l)
        both.append(h + l)
    return hi, lo, both, both[0] * both[0] + both[1] * both[1] + both[2] * both[2]


def split3(n):
    a = n.astype(BF16).astype(F32)
    b = (n - a).astype(BF16).astype(F32)
    return a, b, n - a - b


def order_pair(first, second, ordered, p, own):
    n = first.shape[1]
    b = second[1, p]
    inside = (b < n // 2).astype(jnp.int32)
    at = jnp.where(inside == 1, own, n - 1 - p + own)
    ordered[at] = first[1, p]
    ordered[n + at] = b
    return own + inside


def features(side, pos, listed, feat_b, feat_a):
    blocks = pos.shape[1]
    one = jnp.ones((8, 128), F32)
    zero = jnp.zeros((8, 128), F32)

    def put(ref, q0, feats):
        for k, v in enumerate(feats):
            ref[pl.ds(q0 * 16 + k, 8, stride=16), :] = v

    def own(g, c):
        q0 = pl.multiple_of(g * 8, 8)
        hi, lo, both, norm = feature_rows([pos[m, pl.ds(q0, 8), :] for m in range(3)])
        n = split3(norm)
        put(feat_b, q0, hi + [one, n[0], n[1], n[2], one] + lo + [one, zero, zero, zero, zero])
        n = split3(norm + EPS2)
        h2, l2 = [-2.0 * v for v in hi], [-2.0 * v for v in lo]
        put(feat_a, q0, h2 + [n[0], one, one, one, n[1]] + l2 + [n[2], zero, zero, zero, zero])
        return c

    lax.fori_loop(0, blocks // 8, own, 0, unroll=2)
    for i, refs in enumerate(listed):
        upper = side[0] if i else 1 - side[0]
        for g in range(2):
            hi, lo, _, norm = feature_rows([sum(ref[at + m * 16 + g * 8 : at + m * 16 + g * 8 + 8, :] for ref, at in refs) for m in range(3)])
            n = split3(norm)
            put(feat_b, pl.multiple_of(blocks + upper * 16 + g * 8, 8), hi + [one, n[0], n[1], n[2], one] + lo + [one, zero, zero, zero, zero])


def push_pairs(pair, begin, end, group, push, feat_b, feat_a, beside=lambda p, c: c):
    top = lax.broadcasted_iota(jnp.int32, (8, 128), 0) < 3

    def one_pair(p):
        a, b = pair(p)
        fb = feat_b[pl.ds(pl.multiple_of(b * 16, 16), 16), :]
        fa = feat_a[pl.ds(pl.multiple_of(a * 16, 16), 16), :]
        x, y = fa[0:8], fa[8:16]
        z = jnp.where(top, y, 0.0)
        ga = jnp.concatenate([x, jnp.where(top, x, y), z, z], axis=0).astype(BF16)
        lhs = fb.astype(BF16)
        r2 = dot(jnp.concatenate([lhs, lhs], axis=0), ga, ((0,), (0,)))
        w = jnp.maximum(lax.rsqrt(jnp.maximum(r2, EPS2)) - 4.0, 0.0)
        res = dot(jnp.concatenate([lhs, lhs], axis=1), jnp.concatenate(split2(w), axis=0))
        total = jnp.broadcast_to(res[3:4], (8, 128))
        return a, (-0.5) * (x + z) * total - (res[0:8] + res[8:16])

    def pairs(g, c):
        done = []
        for k in range(group):
            done.append(one_pair(g * group + k))
            c = beside(g * group + k, c)
        for a, f in done:
            rows = pl.ds(pl.multiple_of(a * 8, 8), 8)
            push[rows, :] = push[rows, :] + f
        return c

    return lax.fori_loop(begin, end, pairs, jnp.int32(0))


def push_kernel(side, first, second, slot, pos, listed_a, listed_b, around, after, push, slot_out, ordered, feat_b, feat_a):
    def hand_on(q, c):
        slot_out[q] = slot[q]
        return c

    lax.fori_loop(0, slot.shape[0], hand_on, 0, unroll=8)
    listed = (((listed_a, 96),), ((listed_b, 96), (around, 0)))
    features(side, pos, listed, feat_b, feat_a)
    push[...] = jnp.zeros(push.shape, F32)
    groups = first.shape[1] // PAIR_GROUP
    order = functools.partial(order_pair, first, second, ordered)
    own = push_pairs(lambda p: (first[0, p], second[0, p]), 0, groups, PAIR_GROUP, push, feat_b, feat_a, order)
    ordered[2 * first.shape[1]] = own // INNER_GROUP


def advance(pos, vel, push, air, pos_out, vel_out):
    blocks = pos.shape[1]
    for m in range(3):
        v = vel[m]
        force = 2.5 * push[pl.ds(m, blocks, stride=8), :] + air[3] * (air[m] - v)
        if m == 2:
            force = force - 1.0
        v = v + 0.1 * force
        vel_out[m] = v
        pos_out[m] = pos[m] + 0.1 * v


def pick(hot, v):
    v = jnp.concatenate([v, v], axis=0)
    hi = v.astype(BF16).astype(F32)
    both = dot(jnp.concatenate([hi, v - hi], axis=0).astype(BF16), hot)
    return both[0:8] + both[8:16]


def pick_kernel(side, slot, halo, back, cell, pos, vel, push, air, pos_out, vel_out, first_x, second_x, flow):
    def group(g, c):
        base = pl.multiple_of(g * BLOCK_GROUP, BLOCK_GROUP)
        cells = cell[pl.ds(base, BLOCK_GROUP), :]
        for k in range(BLOCK_GROUP):
            q = base + k
            flow[pl.ds(pl.multiple_of(q * 8, 8), 8), :] = pick(onehot_cells(cells[k : k + 1, :]), back[slot[q]])
        return c

    lax.fori_loop(0, cell.shape[0] // BLOCK_GROUP, group, 0)
    for m in range(3):
        air[m] = flow[pl.ds(m, cell.shape[0], stride=8), :]
    air[3] = 2.0 * flow[pl.ds(3, cell.shape[0], stride=8), :]
    advance(pos, vel, push, air, pos_out, vel_out)
    put_listed(halo, 1 - side[0], pos_out, first_x, 0)
    put_listed(halo, side[0], pos_out, second_x, 0)


def inner_kernel(ordered, pos, push, feat_b, feat_a):
    n = pos.shape[1] * 2
    features(None, pos, (), feat_b, feat_a)
    push[...] = jnp.zeros(push.shape, F32)
    push_pairs(lambda p: (ordered[p], ordered[n + p]), 0, ordered[2 * n], INNER_GROUP, push, feat_b, feat_a)


def last_kernel(side, ordered, pos, vel, listed_a, listed_b, air, inner, pos_out, vel_out, push, feat_b, feat_a):
    n = pos.shape[1] * 2
    features(side, pos, (((listed_a, 0),), ((listed_b, 0),)), feat_b, feat_a)
    push[...] = inner[...]
    begin = ordered[2 * n] * (INNER_GROUP // LAST_GROUP)
    push_pairs(lambda p: (ordered[p], ordered[n + p]), begin, n // LAST_GROUP, LAST_GROUP, push, feat_b, feat_a)
    advance(pos, vel, push, air, pos_out, vel_out)


def call(kernel, in_specs, out_shape, out_specs, scratch=(), micros=1, vmem=20 * 1024 * 1024):
    return pl.pallas_call(
        kernel,
        in_specs=in_specs,
        out_shape=out_shape,
        out_specs=out_specs,
        scratch_shapes=list(scratch),
        compiler_params=pltpu.CompilerParams(vmem_limit_bytes=vmem),
        cost_estimate=pl.CostEstimate(flops=micros * 1_000_000_000, bytes_accessed=micros * 3_000_000, transcendentals=0),
    )


def shape(*dims, dtype=F32):
    return jax.ShapeDtypeStruct(dims, dtype)


def per_device(
    fluid_vel,
    part_pos,
    part_vel,
    brick_owner,
    brick_local,
    cell_in_brick,
    pair_self,
    pair_other,
    halo_list,
):
    nx, ny = lax.axis_size("gx"), lax.axis_size("gy")
    tiles = nx * ny
    blocks = part_pos.shape[0]
    slots = tiles * CAP
    sx, sy, sz = fluid_vel.shape[1:]
    pos = jnp.transpose(part_pos, (1, 0, 2))
    vel = jnp.transpose(part_vel, (1, 0, 2))

    send, slot, placed = call(
        deposit_kernel,
        [HBM] * 4,
        [shape(slots, 4, 128), shape(blocks, dtype=jnp.int32), shape(8, 128)],
        [VMEM, SMEM, VMEM],
        [
            pltpu.SMEM((tiles,), jnp.int32),
            pltpu.SMEM((blocks,), jnp.int32),
            pltpu.SMEM((blocks,), jnp.int32),
            pltpu.VMEM((blocks, 128), jnp.int32),
            pltpu.VMEM((3, blocks, 128), F32),
            pltpu.SemaphoreType.DMA((2 + 2 * blocks // DEPOSIT_GROUP,)),
        ],
        7,
        63_000_000,
    )(brick_owner[:, 0], brick_local, cell_in_brick, vel)
    recv = lax.all_to_all(send.reshape(slots * 4, 128), ("gx", "gy"), split_axis=0, concat_axis=0, tiled=True)

    me_x, me_y = lax.axis_index("gx"), lax.axis_index("gy")
    side = jnp.stack([me_x % 2, me_y % 2]).astype(jnp.int32)
    first_x, second_x, first_y, second_y = call(
        faces_kernel,
        [SMEM, SMEM, VMEM, VMEM, VMEM],
        [shape(144, 128), shape(144, 128), shape(3, sx, sz), shape(3, sx, sz)],
        [VMEM] * 4,
    )(side, halo_list, fluid_vel, pos, placed)
    bricks = sx // 2 * (sy // 4) * (sz // 16)
    old, around, inner = call(
        old_kernel,
        [VMEM, VMEM],
        [shape(3, bricks, 128), shape(48, 128), shape(3, bricks, 128)],
        [VMEM] * 3,
        [pltpu.VMEM((3, sx, sy, sz), F32)],
        2,
    )(fluid_vel, second_x)
    perms_x, perms_y = swaps(nx, True), swaps(ny, False)
    first_x = lax.ppermute(first_x, "gx", perms_x[0])
    second_x = lax.ppermute(second_x, "gx", perms_x[1][1:-1])
    around = lax.ppermute(around, "gx", [(0, nx - 1), (nx - 1, 0)])
    first_y = lax.ppermute(first_y, "gy", perms_y[0])
    second_y = lax.ppermute(second_y, "gy", perms_y[1])

    spread = call(
        spread_kernel,
        [SMEM] + [VMEM] * 5,
        shape(3, bricks, 128),
        VMEM,
    )(side, inner, first_x, second_x, first_y, second_y)
    answer, fluid, stepped = call(
        fluid_kernel,
        [VMEM] * 3,
        [shape(slots * 4, 128), shape(3, sx, sy, sz), shape(8, 128)],
        [VMEM] * 3,
        (),
        3,
    )(recv, old, spread)
    back = lax.all_to_all(answer, ("gx", "gy"), split_axis=0, concat_axis=0, tiled=True).reshape(slots, 4, 128)
    pair_scratch = [pltpu.VMEM(((blocks + 32) * 16, 128), F32), pltpu.VMEM((blocks * 16, 128), F32)]
    push, slot, ordered = call(
        push_kernel,
        [SMEM] * 4 + [VMEM] * 5,
        [
            shape(blocks * 8, 128),
            shape(blocks, dtype=jnp.int32),
            shape(2 * pair_self.shape[1] + 128, dtype=jnp.int32),
        ],
        [VMEM, SMEM, SMEM],
        pair_scratch,
        14,
    )(side, pair_self, pair_other, slot, pos, first_x, second_x, around, stepped)

    air, pos, vel, listed_a, listed_b = call(
        pick_kernel,
        [SMEM] * 3 + [VMEM] * 5,
        [shape(4, blocks, 128), shape(3, blocks, 128), shape(3, blocks, 128), shape(48, 128), shape(48, 128)],
        [VMEM] * 5,
        [pltpu.VMEM((blocks * 8, 128), F32)],
        4,
    )(side, slot, halo_list, back, cell_in_brick, pos, vel, push)
    listed_a = lax.ppermute(listed_a, "gx", perms_x[0])
    listed_b = lax.ppermute(listed_b, "gx", perms_x[1])
    inner = call(
        inner_kernel,
        [SMEM, VMEM],
        shape(blocks * 8, 128),
        VMEM,
        pair_scratch,
        10,
    )(ordered, pos)
    pos, vel = call(
        last_kernel,
        [SMEM] * 2 + [VMEM] * 6,
        [shape(3, blocks, 128), shape(3, blocks, 128)],
        [VMEM] * 2,
        [pltpu.VMEM((blocks * 8, 128), F32)] + pair_scratch,
        5,
    )(side, ordered, pos, vel, listed_a, listed_b, air, inner)
    return fluid, jnp.transpose(pos, (1, 0, 2)), jnp.transpose(vel, (1, 0, 2))


def solution(mesh):
    in_specs = (
        P(None, "gx", "gy", None),
        P(("gx", "gy"), None, None),
        P(("gx", "gy"), None, None),
        P(("gx", "gy"), None),
        P(("gx", "gy")),
        P(("gx", "gy"), None),
        P(None, ("gx", "gy")),
        P(None, ("gx", "gy")),
        P(("gx", "gy")),
    )
    out_specs = (
        P(None, "gx", "gy", None),
        P(("gx", "gy"), None, None),
        P(("gx", "gy"), None, None),
    )
    return jax.shard_map(
        per_device, mesh=mesh, in_specs=in_specs, out_specs=out_specs, check_vma=False
    )
```

```python
import functools

import jax
import jax.numpy as jnp
from jax import lax
from jax.experimental import pallas as pl
from jax.experimental.pallas import tpu as pltpu
from jax.sharding import PartitionSpec as P

F32 = jnp.float32
BF16 = jnp.bfloat16
PAIR_GROUP = 256
INNER_GROUP = 384
LAST_GROUP = 128
BLOCK_GROUP = 256
DEPOSIT_GROUP = 128
CAP = 4
EPS2 = 0.0025
VMEM = pl.BlockSpec(memory_space=pltpu.VMEM)
SMEM = pl.BlockSpec(memory_space=pltpu.SMEM)
HBM = pl.BlockSpec(memory_space=pltpu.HBM)


def split2(x):
    hi = x.astype(BF16)
    return hi, (x - hi.astype(F32)).astype(BF16)


def onehot_cells(row):
    cells = lax.broadcasted_iota(jnp.int32, (128, 128), 0)
    return (cells == jnp.broadcast_to(row, (128, 128))).astype(F32).astype(BF16)


def dot(a, b, dims=((1,), (0,))):
    return lax.dot_general(a, b, (dims, ((), ())), preferred_element_type=F32)


def swaps(n, closed):
    first = [(i, i ^ 1) for i in range(n)]
    second = [(i, (i + 1 if i % 2 else i - 1) % n) for i in range(n)]
    return first, (second if closed else second[1:-1])


def put_listed(halo, half, pos, out, at):
    for j in range(16):
        q = halo[half * 16 + j]
        for m in range(3):
            out[at + m * 16 + j : at + m * 16 + j + 1, :] = pos[m, pl.ds(q, 1), :]


def faces_kernel(side, halo, fv, pos, after, first_x, second_x, first_y, second_y):
    sx, sy, sz = fv.shape[1:]
    for out, upper in ((first_x, 1 - side[0]), (second_x, side[0])):
        x = upper * (sx - 1)
        for m in range(3):
            for h in range(2):
                out[(m * 2 + h) * 16 : (m * 2 + h + 1) * 16, :] = fv[m, x, :, h * 128 : (h + 1) * 128]
        put_listed(halo, upper, pos, out, 96)
    odd = jnp.full((sx, sz), side[1], jnp.int32) == 1
    for m in range(3):
        begin, end = fv[m, :, 0, :], fv[m, :, sy - 1, :]
        first_y[m] = jnp.where(odd, begin, end)
        second_y[m] = jnp.where(odd, end, begin)


def deposit_kernel(owner_in, local_in, cell_in, vel_in, out, slot_out, done, taken, owner, local, cell, vel, sems):
    blocks = cell.shape[0]
    copies = [
        pltpu.make_async_copy(src, dst, sems.at[i])
        for i, (src, dst) in enumerate(((vel_in, vel), (cell_in, cell), (owner_in, owner), (local_in, local)))
    ]
    for c in copies:
        c.start()
    lanes = lax.broadcasted_iota(jnp.int32, (4, 128), 1)
    rows4 = lax.broadcasted_iota(jnp.int32, (4, 128), 0)
    mark = (lanes == 127) & (rows4 == 0)
    done[...] = jnp.zeros(done.shape, F32)
    out[...] = jnp.broadcast_to(jnp.where(mark, -1.0, 0.0).astype(F32)[None], out.shape)

    def clear(t, c):
        taken[t] = 0
        return c

    lax.fori_loop(0, taken.shape[0], clear, 0, unroll=8)
    r8 = lax.broadcasted_iota(jnp.int32, (8, 128), 0)
    lane16 = lax.broadcasted_iota(jnp.int32, (128, 128), 1) // 16
    for c in copies:
        c.wait()

    def group(g, c):
        base = pl.multiple_of(g * DEPOSIT_GROUP, DEPOSIT_GROUP)
        cells = cell[pl.ds(base, DEPOSIT_GROUP), :]
        v = [vel[m, pl.ds(base, DEPOSIT_GROUP), :] for m in range(3)]
        for start in range(0, DEPOSIT_GROUP, 8):
            loads, hots = [], []
            for k in range(start, start + 8):
                rows = [jnp.broadcast_to(v[m][k : k + 1, :], (8, 128)) for m in range(3)]
                load = jnp.where(r8 == 1, rows[0], jnp.where(r8 == 2, rows[1], rows[2]))
                load = jnp.where(r8 == 0, 1.0, jnp.where(r8 < 4, load, 0.0))
                hi = load.astype(BF16).astype(F32)
                loads += [hi, load - hi]
                hots.append(onehot_cells(cells[k : k + 1, :]))
            turned = jnp.concatenate(loads, axis=0).T
            turned = turned.astype(BF16)
            apart = [jnp.where(lane16 == k, turned, jnp.zeros_like(turned)) for k in range(8)]
            found = dot(jnp.concatenate(hots, axis=1), jnp.concatenate(apart, axis=0)).T
            for k in range(8):
                q = base + start + k
                both = found[k * 16 : k * 16 + 8] + found[k * 16 + 8 : k * 16 + 16]
                tile = owner[q]
                rank = taken[tile]
                taken[tile] = rank + 1
                slot = tile * CAP + rank
                slot_out[q] = slot
                ident = jnp.full((4, 128), local[q], jnp.int32).astype(F32)
                out[slot] = jnp.where(mark, ident, both[0:4])
        return c

    lax.fori_loop(0, blocks // DEPOSIT_GROUP, group, 0)


def swap_groups(v):
    row = lax.broadcasted_iota(jnp.int32, v.shape, 1)
    grp = lax.broadcasted_iota(jnp.int32, v.shape, 2) // 16
    for s in range(3):
        step = 1 << s
        ra, gb = (row >> s) & 1, (grp >> s) & 1
        up = pltpu.roll(pltpu.roll(v, 8 - step, 1), 16 * step, 2)
        dn = pltpu.roll(pltpu.roll(v, step, 1), 128 - 16 * step, 2)
        v = jnp.where(ra == gb, v, jnp.where(ra < gb, up, dn))
    return v


def places(sx, sy):
    return [
        (bx * 2, slice(by * 4, by * 4 + 4), slice(h * 128, h * 128 + 128))
        for bx in range(sx // 2)
        for by in range(sy // 4)
        for h in range(2)
    ]


def to_bricks(grid, m):
    tiles = [jnp.concatenate([grid[m, x, y, z], grid[m, x + 1, y, z]], axis=0) for x, y, z in places(*grid.shape[1:3])]
    return swap_groups(jnp.stack(tiles, axis=0)).reshape(len(tiles) * 8, 128)


def old_kernel(fv, sent, bricks, around, inner, grid):
    around[...] = sent[96:144, :]
    sx, sy, sz = fv.shape[1:]
    yrow = lax.broadcasted_iota(jnp.int32, (sy, sz), 0)
    zlane = lax.broadcasted_iota(jnp.int32, (sy, sz), 1)
    zero = jnp.zeros((sy, sz), F32)
    for m in range(3):
        bricks[m] = to_bricks(fv, m)
        for x in range(sx):
            f = fv[m, x]
            beside = (fv[m, x + 1] if x < sx - 1 else zero) + (fv[m, x - 1] if x > 0 else zero)
            beside = beside + jnp.where(yrow == sy - 1, 0.0, pltpu.roll(f, sy - 1, 0))
            beside = beside + jnp.where(yrow == 0, 0.0, pltpu.roll(f, 1, 0))
            beside = beside + jnp.where(zlane == sz - 1, 0.0, pltpu.roll(f, sz - 1, 1))
            beside = beside + jnp.where(zlane == 0, 0.0, pltpu.roll(f, 1, 1))
            grid[m, x] = f + 0.1 * (beside - 6.0 * f)
    for m in range(3):
        inner[m] = to_bricks(grid, m)


def spread_kernel(side, inner, first_x, second_x, first_y, second_y, bricks):
    sx, sz = first_y.shape[1:]
    sy = 16
    odd = side[0].astype(F32)
    odd_y = jnp.full((sx, sz), side[1], jnp.int32) == 1
    row4 = lax.broadcasted_iota(jnp.int32, (4, 128), 0)
    zero = jnp.zeros((4, 128), F32)
    for m in range(3):
        lefts = 0.1 * jnp.where(odd_y, first_y[m], second_y[m])
        rights = 0.1 * jnp.where(odd_y, second_y[m], first_y[m])
        tiles, rows = [], []
        for i, (x0, y, z) in enumerate(places(sx, sy)):
            if 0 < x0 < sx - 2 and 0 < y.start < sy - 4:
                bricks[m, i * 8 : i * 8 + 8] = inner[m, i * 8 : i * 8 + 8]
                continue
            halves = []
            for x in (x0, x0 + 1):
                part = zero
                if x in (0, sx - 1):
                    at = (m * 2 + z.start // 128) * 16
                    first = first_x[at + y.start : at + y.stop, :]
                    second = second_x[at + y.start : at + y.stop, :]
                    keep = odd if x == 0 else 1.0 - odd
                    part = 0.1 * (keep * first + (1.0 - keep) * second)
                if y.start == 0:
                    part = part + jnp.where(row4 == 0, jnp.broadcast_to(lefts[x : x + 1, z], (4, 128)), 0.0)
                if y.stop == sy:
                    part = part + jnp.where(row4 == 3, jnp.broadcast_to(rights[x : x + 1, z], (4, 128)), 0.0)
                halves.append(part)
            tiles.append(jnp.concatenate(halves, axis=0))
            rows.append(i * 8)
        moved = swap_groups(jnp.stack(tiles, axis=0))
        for k, at in enumerate(rows):
            bricks[m, at : at + 8] = inner[m, at : at + 8] + moved[k]


def fluid_kernel(recv, old, spread, answer, fluid, done):
    done[...] = jnp.zeros(done.shape, F32)
    slots = recv.shape[0] // 4
    bricks = old.shape[1]
    count = recv[pl.ds(0, slots, stride=4), :]
    lane = lax.broadcasted_iota(jnp.int32, (slots, 128), 1)
    ident = count[:, 127:128]
    ident_row = count.T[127:128, :]
    wide = lax.broadcasted_iota(jnp.int32, (slots, bricks), 1).astype(F32)
    by_slot = (wide == jnp.broadcast_to(ident, (slots, bricks))).astype(F32).astype(BF16)
    tall = lax.broadcasted_iota(jnp.int32, (bricks, slots), 0).astype(F32)
    by_brick = (tall == jnp.broadcast_to(ident_row, (bricks, slots))).astype(F32).astype(BF16)
    parts = [jnp.where(lane == 127, 1.0, count).astype(BF16)]
    for m in range(3):
        parts += list(split2(recv[pl.ds(m + 1, slots, stride=4), :]))
    summed = dot(by_brick, jnp.concatenate(parts, axis=1))
    cnt = summed[:, 0:128]
    momentum = [summed[:, (1 + 2 * m) * 128 : (2 + 2 * m) * 128] + summed[:, (2 + 2 * m) * 128 : (3 + 2 * m) * 128] for m in range(3)]
    last = lax.broadcasted_iota(jnp.int32, (bricks, 128), 1) == 127
    others = jnp.sum(jnp.where(last, 0.0, cnt), axis=1, keepdims=True)
    cnt = jnp.where(last, 128.0 * cnt - others, cnt)
    solid = 0.5 * cnt
    voids = 1.0 - 0.6 * solid / (1.0 + solid)
    beta = (1.0 - voids) / (voids * voids)
    scale = 0.15 * beta
    table = []
    for m in range(3):
        new = spread[m] + scale * (momentum[m] - cnt * old[m])
        table += list(split2(new))
        moved = swap_groups(new.reshape(bricks // 8, 8, 128))
        for i, (x, y, z) in enumerate(places(*fluid.shape[1:3])):
            fluid[m, x, y, z] = moved[i, 0:4]
            fluid[m, x + 1, y, z] = moved[i, 4:8]
    table += list(split2(beta))
    found = dot(by_slot, jnp.concatenate(table, axis=1))
    for c in range(4):
        answer[pl.ds(c, slots, stride=4), :] = (
            found[:, 2 * c * 128 : (2 * c + 1) * 128] + found[:, (2 * c + 1) * 128 : (2 * c + 2) * 128]
        )


def feature_rows(x):
    hi, lo, both = [], [], []
    for m in range(3):
        u = x[m] - 0.5
        h = u.astype(BF16).astype(F32)
        l = (u - h).astype(BF16).astype(F32)
        hi.append(h)
        lo.append(l)
        both.append(h + l)
    return hi, lo, both, both[0] * both[0] + both[1] * both[1] + both[2] * both[2]


def split3(n):
    a = n.astype(BF16).astype(F32)
    b = (n - a).astype(BF16).astype(F32)
    return a, b, n - a - b


def order_pair(first, second, ordered, p, own):
    n = first.shape[1]
    b = second[1, p]
    inside = (b < n // 2).astype(jnp.int32)
    at = jnp.where(inside == 1, own, n - 1 - p + own)
    ordered[at] = first[1, p]
    ordered[n + at] = b
    return own + inside


def features(side, pos, listed, feat_b, feat_a):
    blocks = pos.shape[1]
    one = jnp.ones((8, 128), F32)
    zero = jnp.zeros((8, 128), F32)

    def put(ref, q0, feats):
        for k, v in enumerate(feats):
            ref[pl.ds(q0 * 16 + k, 8, stride=16), :] = v

    def own(g, c):
        q0 = pl.multiple_of(g * 8, 8)
        hi, lo, both, norm = feature_rows([pos[m, pl.ds(q0, 8), :] for m in range(3)])
        n = split3(norm)
        put(feat_b, q0, hi + [one, n[0], n[1], n[2], one] + lo + [one, zero, zero, zero, zero])
        n = split3(norm + EPS2)
        h2, l2 = [-2.0 * v for v in hi], [-2.0 * v for v in lo]
        put(feat_a, q0, h2 + [n[0], one, one, one, n[1]] + l2 + [n[2], zero, zero, zero, zero])
        return c

    lax.fori_loop(0, blocks // 8, own, 0, unroll=2)
    for i, refs in enumerate(listed):
        upper = side[0] if i else 1 - side[0]
        for g in range(2):
            hi, lo, _, norm = feature_rows([sum(ref[at + m * 16 + g * 8 : at + m * 16 + g * 8 + 8, :] for ref, at in refs) for m in range(3)])
            n = split3(norm)
            put(feat_b, pl.multiple_of(blocks + upper * 16 + g * 8, 8), hi + [one, n[0], n[1], n[2], one] + lo + [one, zero, zero, zero, zero])


def push_pairs(pair, begin, end, group, push, feat_b, feat_a, beside=lambda p, c: c):
    top = lax.broadcasted_iota(jnp.int32, (8, 128), 0) < 3

    def one_pair(p):
        a, b = pair(p)
        fb = feat_b[pl.ds(pl.multiple_of(b * 16, 16), 16), :]
        fa = feat_a[pl.ds(pl.multiple_of(a * 16, 16), 16), :]
        x, y = fa[0:8], fa[8:16]
        z = jnp.where(top, y, 0.0)
        ga = jnp.concatenate([x, jnp.where(top, x, y), z, z], axis=0).astype(BF16)
        lhs = fb.astype(BF16)
        r2 = dot(jnp.concatenate([lhs, lhs], axis=0), ga, ((0,), (0,)))
        w = jnp.maximum(lax.rsqrt(jnp.maximum(r2, EPS2)) - 4.0, 0.0)
        res = dot(jnp.concatenate([lhs, lhs], axis=1), jnp.concatenate(split2(w), axis=0))
        total = jnp.broadcast_to(res[3:4], (8, 128))
        return a, (-0.5) * (x + z) * total - (res[0:8] + res[8:16])

    def pairs(g, c):
        done = []
        for k in range(group):
            done.append(one_pair(g * group + k))
            c = beside(g * group + k, c)
        for a, f in done:
            rows = pl.ds(pl.multiple_of(a * 8, 8), 8)
            push[rows, :] = push[rows, :] + f
        return c

    return lax.fori_loop(begin, end, pairs, jnp.int32(0))


def push_kernel(side, first, second, slot, pos, listed_a, listed_b, around, after, push, slot_out, ordered, feat_b, feat_a):
    def hand_on(q, c):
        slot_out[q] = slot[q]
        return c

    lax.fori_loop(0, slot.shape[0], hand_on, 0, unroll=8)
    listed = (((listed_a, 96),), ((listed_b, 96), (around, 0)))
    features(side, pos, listed, feat_b, feat_a)
    push[...] = jnp.zeros(push.shape, F32)
    groups = first.shape[1] // PAIR_GROUP
    order = functools.partial(order_pair, first, second, ordered)
    own = push_pairs(lambda p: (first[0, p], second[0, p]), 0, groups, PAIR_GROUP, push, feat_b, feat_a, order)
    ordered[2 * first.shape[1]] = own // INNER_GROUP


def advance(pos, vel, push, air, pos_out, vel_out):
    blocks = pos.shape[1]
    for m in range(3):
        v = vel[m]
        force = 2.5 * push[pl.ds(m, blocks, stride=8), :] + air[3] * (air[m] - v)
        if m == 2:
            force = force - 1.0
        v = v + 0.1 * force
        vel_out[m] = v
        pos_out[m] = pos[m] + 0.1 * v


def pick(hot, v):
    v = jnp.concatenate([v, v], axis=0)
    hi = v.astype(BF16).astype(F32)
    both = dot(jnp.concatenate([hi, v - hi], axis=0).astype(BF16), hot)
    return both[0:8] + both[8:16]


def pick_kernel(side, slot, halo, back, cell, pos, vel, push, air, pos_out, vel_out, first_x, second_x, flow):
    def group(g, c):
        base = pl.multiple_of(g * BLOCK_GROUP, BLOCK_GROUP)
        cells = cell[pl.ds(base, BLOCK_GROUP), :]
        for k in range(BLOCK_GROUP):
            q = base + k
            flow[pl.ds(pl.multiple_of(q * 8, 8), 8), :] = pick(onehot_cells(cells[k : k + 1, :]), back[slot[q]])
        return c

    lax.fori_loop(0, cell.shape[0] // BLOCK_GROUP, group, 0)
    for m in range(3):
        air[m] = flow[pl.ds(m, cell.shape[0], stride=8), :]
    air[3] = 2.0 * flow[pl.ds(3, cell.shape[0], stride=8), :]
    advance(pos, vel, push, air, pos_out, vel_out)
    put_listed(halo, 1 - side[0], pos_out, first_x, 0)
    put_listed(halo, side[0], pos_out, second_x, 0)


def inner_kernel(ordered, pos, push, feat_b, feat_a):
    n = pos.shape[1] * 2
    features(None, pos, (), feat_b, feat_a)
    push[...] = jnp.zeros(push.shape, F32)
    push_pairs(lambda p: (ordered[p], ordered[n + p]), 0, ordered[2 * n], INNER_GROUP, push, feat_b, feat_a)


def last_kernel(side, ordered, pos, vel, listed_a, listed_b, air, inner, pos_out, vel_out, push, feat_b, feat_a):
    n = pos.shape[1] * 2
    features(side, pos, (((listed_a, 0),), ((listed_b, 0),)), feat_b, feat_a)
    push[...] = inner[...]
    begin = ordered[2 * n] * (INNER_GROUP // LAST_GROUP)
    push_pairs(lambda p: (ordered[p], ordered[n + p]), begin, n // LAST_GROUP, LAST_GROUP, push, feat_b, feat_a)
    advance(pos, vel, push, air, pos_out, vel_out)


def call(kernel, in_specs, out_shape, out_specs, scratch=(), micros=1, vmem=20 * 1024 * 1024):
    return pl.pallas_call(
        kernel,
        in_specs=in_specs,
        out_shape=out_shape,
        out_specs=out_specs,
        scratch_shapes=list(scratch),
        compiler_params=pltpu.CompilerParams(vmem_limit_bytes=vmem),
        cost_estimate=pl.CostEstimate(flops=micros * 1_000_000_000, bytes_accessed=micros * 3_000_000, transcendentals=0),
    )


def shape(*dims, dtype=F32):
    return jax.ShapeDtypeStruct(dims, dtype)


def per_device(
    fluid_vel,
    part_pos,
    part_vel,
    brick_owner,
    brick_local,
    cell_in_brick,
    pair_self,
    pair_other,
    halo_list,
):
    nx, ny = lax.axis_size("gx"), lax.axis_size("gy")
    tiles = nx * ny
    blocks = part_pos.shape[0]
    slots = tiles * CAP
    sx, sy, sz = fluid_vel.shape[1:]
    pos = jnp.transpose(part_pos, (1, 0, 2))
    vel = jnp.transpose(part_vel, (1, 0, 2))

    send, slot, placed = call(
        deposit_kernel,
        [HBM] * 4,
        [shape(slots, 4, 128), shape(blocks, dtype=jnp.int32), shape(8, 128)],
        [VMEM, SMEM, VMEM],
        [
            pltpu.SMEM((tiles,), jnp.int32),
            pltpu.SMEM((blocks,), jnp.int32),
            pltpu.SMEM((blocks,), jnp.int32),
            pltpu.VMEM((blocks, 128), jnp.int32),
            pltpu.VMEM((3, blocks, 128), F32),
            pltpu.SemaphoreType.DMA((4,)),
        ],
        7,
        63_000_000,
    )(brick_owner[:, 0], brick_local, cell_in_brick, vel)
    recv = lax.all_to_all(send.reshape(slots * 4, 128), ("gx", "gy"), split_axis=0, concat_axis=0, tiled=True)

    me_x, me_y = lax.axis_index("gx"), lax.axis_index("gy")
    side = jnp.stack([me_x % 2, me_y % 2]).astype(jnp.int32)
    first_x, second_x, first_y, second_y = call(
        faces_kernel,
        [SMEM, SMEM, VMEM, VMEM, VMEM],
        [shape(144, 128), shape(144, 128), shape(3, sx, sz), shape(3, sx, sz)],
        [VMEM] * 4,
    )(side, halo_list, fluid_vel, pos, placed)
    bricks = sx // 2 * (sy // 4) * (sz // 16)
    old, around, inner = call(
        old_kernel,
        [VMEM, VMEM],
        [shape(3, bricks, 128), shape(48, 128), shape(3, bricks, 128)],
        [VMEM] * 3,
        [pltpu.VMEM((3, sx, sy, sz), F32)],
        2,
    )(fluid_vel, second_x)
    perms_x, perms_y = swaps(nx, True), swaps(ny, False)
    first_x = lax.ppermute(first_x, "gx", perms_x[0])
    second_x = lax.ppermute(second_x, "gx", perms_x[1][1:-1])
    around = lax.ppermute(around, "gx", [(0, nx - 1), (nx - 1, 0)])
    first_y = lax.ppermute(first_y, "gy", perms_y[0])
    second_y = lax.ppermute(second_y, "gy", perms_y[1])

    spread = call(
        spread_kernel,
        [SMEM] + [VMEM] * 5,
        shape(3, bricks, 128),
        VMEM,
    )(side, inner, first_x, second_x, first_y, second_y)
    answer, fluid, stepped = call(
        fluid_kernel,
        [VMEM] * 3,
        [shape(slots * 4, 128), shape(3, sx, sy, sz), shape(8, 128)],
        [VMEM] * 3,
        (),
        3,
    )(recv, old, spread)
    back = lax.all_to_all(answer, ("gx", "gy"), split_axis=0, concat_axis=0, tiled=True).reshape(slots, 4, 128)
    pair_scratch = [pltpu.VMEM(((blocks + 32) * 16, 128), F32), pltpu.VMEM((blocks * 16, 128), F32)]
    push, slot, ordered = call(
        push_kernel,
        [SMEM] * 4 + [VMEM] * 5,
        [
            shape(blocks * 8, 128),
            shape(blocks, dtype=jnp.int32),
            shape(2 * pair_self.shape[1] + 128, dtype=jnp.int32),
        ],
        [VMEM, SMEM, SMEM],
        pair_scratch,
        14,
    )(side, pair_self, pair_other, slot, pos, first_x, second_x, around, stepped)

    air, pos, vel, listed_a, listed_b = call(
        pick_kernel,
        [SMEM] * 3 + [VMEM] * 5,
        [shape(4, blocks, 128), shape(3, blocks, 128), shape(3, blocks, 128), shape(48, 128), shape(48, 128)],
        [VMEM] * 5,
        [pltpu.VMEM((blocks * 8, 128), F32)],
        4,
    )(side, slot, halo_list, back, cell_in_brick, pos, vel, push)
    listed_a = lax.ppermute(listed_a, "gx", perms_x[0])
    listed_b = lax.ppermute(listed_b, "gx", perms_x[1])
    inner = call(
        inner_kernel,
        [SMEM, VMEM],
        shape(blocks * 8, 128),
        VMEM,
        pair_scratch,
        10,
    )(ordered, pos)
    pos, vel = call(
        last_kernel,
        [SMEM] * 2 + [VMEM] * 6,
        [shape(3, blocks, 128), shape(3, blocks, 128)],
        [VMEM] * 2,
        [pltpu.VMEM((blocks * 8, 128), F32)] + pair_scratch,
        5,
    )(side, ordered, pos, vel, listed_a, listed_b, air, inner)
    return fluid, jnp.transpose(pos, (1, 0, 2)), jnp.transpose(vel, (1, 0, 2))


def solution(mesh):
    in_specs = (
        P(None, "gx", "gy", None),
        P(("gx", "gy"), None, None),
        P(("gx", "gy"), None, None),
        P(("gx", "gy"), None),
        P(("gx", "gy")),
        P(("gx", "gy"), None),
        P(None, ("gx", "gy")),
        P(None, ("gx", "gy")),
        P(("gx", "gy")),
    )
    out_specs = (
        P(None, "gx", "gy", None),
        P(("gx", "gy"), None, None),
        P(("gx", "gy"), None, None),
    )
    return jax.shard_map(
        per_device, mesh=mesh, in_specs=in_specs, out_specs=out_specs, check_vma=False
    )
```
